32 devices in a mesh: dp: 2 (over core), expert: 4 (over z), tensor: 4 (over y, x).
Axes of the slice: x: 2, y: 2, z: 4, core: 2. Of those that a mesh axis runs over, the one named last changes fastest.
Arguments:
- hidden_in: bfloat16 [8, 1024, 768], P(('dp', 'expert'), 'tensor'), may hold values from -6 to 6
- cotangent: bfloat16 [8, 1024, 768], P(('dp', 'expert'), 'tensor'), may hold values from -6 to 6
- attn_gain: bfloat16 [768], replicated, may hold values from 0.5 to 1.5
- query_key_value_weight: bfloat16 [768, 3, 768], P(None, None, 'tensor'), may hold values from -0.21875 to 0.21875
- attention_output_weight: bfloat16 [768, 768], P('tensor'), may hold values from -4 to 4
- rel_bias: bfloat16 [12, 32], P('tensor'), may hold values from -4 to 4
- bucket_table: int32 [2047], replicated, may hold values from 0 to 31
- prefix_len: int32 [8], P(('dp', 'expert')), may hold values from 102 to 512
- moe_gain: bfloat16 [768], replicated, may hold values from 0.5 to 1.5
- w_router: bfloat16 [768, 4], replicated, may hold values from -0.4375 to 0.4375
- routes: int32 [8, 4, 1, 256, 1], P(('dp', 'expert'), 'tensor'), may hold values from 0 to 3; in each aligned block of 256 rows (0 to 255, 256 to 511, ..., all dimensions but the last counted through in order) at most 128 rows name the same one
- w_expert_in: bfloat16 [4, 768, 3072], P('expert', None, 'tensor'), may hold values from -0.21875 to 0.21875
- w_expert_out: bfloat16 [4, 3072, 768], P('expert', 'tensor'), may hold values from -0.75 to 0.75
Outputs:
- layer_out: bfloat16 [8, 1024, 768], P(('dp', 'expert'), 'tensor')
- x_grad: float32 [8, 1024, 768], P(('dp', 'expert'), 'tensor')
- attn_gain_grad: float32 [768], P('tensor')
- qkv_grad: float32 [768, 3, 768], P(None, None, 'tensor')
- attn_out_grad: float32 [768, 768], P('tensor')
- rel_bias_grad: float32 [12, 32], P('tensor')
- moe_gain_grad: float32 [768], P('tensor')
- router_grad: float32 [768, 4], P('tensor')
- expert_in_grad: float32 [4, 768, 3072], P('expert', None, 'tensor')
- expert_out_grad: float32 [4, 3072, 768], P('expert', 'tensor')
The draws below stay inside these ranges and needn't reach their ends.
Inputs may be any that keep to these rules, and one draw needn't show every extreme that they name: `routes`: in each aligned block of 256 rows of the array (the tokens of one device), no expert is named more than 128 times, a bound that some block reaches.
All inputs are finite; a program needn't handle non-finite values.
Results may differ from the reference program's by a relative error of at most 0.013.
Values may be sent and summed in bfloat16 or wider, within the bound.
No kernel may reach another device: no remote copies, remote signals or barrier semaphores. Data moves between devices by JAX's collectives and lax.ppermute only.
A program may use at most 128 MiB of HBM per device.

```python
import math
import jax
import jax.numpy as jnp
import numpy as np
from jax import lax

D = 768
HEADS = 12
HEAD_DIM = 64
FF = 3072
BUCKETS = 32
LENGTH = 1024
SEQ_DEV = 1
EXPERTS = 4
INNER = 768
QUARTER = 256
ROWS = 256
CAP = 128
GROUPS = 8
SEQS = 8
N_TENSOR = 4


def set_ends(values, key, low, top_value):
    longest = values.shape.index(max(values.shape))
    spots = []
    for shift in (0, 1):
        where = [jax.random.randint(jax.random.fold_in(key, axis), (), 0, length) for axis, length in enumerate(values.shape)]
        where[longest] = (where[longest] + shift) % values.shape[longest]
        spots.append(tuple(where))
    return values.at[spots[0]].set(low).at[spots[1]].set(top_value)


def block_levels(key, shape, split, least, high):
    factor_of = 1.0
    for dim, blocks in split:
        draws = jax.random.uniform(jax.random.fold_in(jax.random.fold_in(key, 6), dim), (blocks,), jnp.float32, least / len(split), high / len(split))
        factor_of = factor_of * jnp.repeat(jnp.exp(draws), shape[dim] // blocks).reshape((-1,) + (1,) * (len(shape) - 1 - dim))
    return factor_of


def assign_block(rng, own, number, rows, amount, top, reach, slope):
    ranking = jax.random.permutation(rng, amount)
    crowded, common = portions_of(amount, rows * top, reach, slope, True), portions_of(amount, rows * top, reach, slope, False)
    places = jnp.arange(amount)

    def named(sizes, rotation):
        used = int((sizes > 0).sum())
        fixed = max(1, used // 4)
        passed = fixed + (places - fixed + rotation * (used - fixed)) % max(1, amount - fixed)
        return jnp.zeros((amount,), jnp.int32).at[ranking[jnp.where(places < fixed, places, passed)]].set(jnp.asarray(sizes, jnp.int32))

    sizes = jnp.where(number % 4 == 0, named(crowded, number // 4), named(common, number - number // 4 - 1))
    mixed = jax.random.permutation(jax.random.fold_in(own, 3), amount)
    giver, sink = mixed[0:amount // 2 * 2:2], mixed[1:amount // 2 * 2:2]
    slack = jnp.minimum(sizes[giver] - 1, reach - sizes[sink]) // 2
    slack = jnp.where((giver == ranking[0]) | (sink == ranking[0]) | (sizes[sink] == 0), 0, jnp.maximum(slack, 0))
    passed = jax.random.randint(jax.random.fold_in(own, 4), (amount // 2,), 0, 1 << 20) % (slack + 1)
    sizes = sizes.at[giver].add(-passed).at[sink].add(passed)
    labels = jnp.searchsorted(jnp.cumsum(sizes), jnp.arange(rows * top), side="right").astype(jnp.int32)
    table = labels.reshape(top, rows).T
    table = table[jax.random.permutation(jax.random.fold_in(own, 1), rows)]
    rotation = jax.random.randint(jax.random.fold_in(own, 2), (rows, 1), 0, top)
    return jnp.take_along_axis(table, (jnp.arange(top)[None, :] + rotation) % top, axis=1)


def portions_of(number_of, total, limit, slope, full):
    weights = [(1 << 20) // math.isqrt(standing ** slope) + 1 for standing in range(1, number_of + 1)]
    largest = limit if full else min(limit, max(-(-total // number_of), total * weights[0] // sum(weights)))
    least = 1 if total - largest >= number_of - 1 else 0
    holding, surplus = [largest] + [least] * (number_of - 1), total - largest - least * (number_of - 1)
    while surplus > 0:
        free = [i for i in range(1, number_of) if holding[i] < largest] or [i for i in range(1, number_of) if holding[i] < limit]
        pool, budget = sum([weights[i] for i in free]), surplus
        for i in free:
            extra = min(limit - holding[i], max(1, budget * weights[i] // pool), surplus)
            holding[i] = holding[i] + extra
            surplus = surplus - extra
    return np.array(holding)


def normal_values(own_key, dims, deviation, most, shards=(), kind=jnp.bfloat16):
    entries = deviation * jax.random.normal(own_key, dims, jnp.float32)
    if shards:
        entries = entries * block_levels(own_key, dims, shards, -0.22, 0.18)
    return jnp.clip(entries, -most, most).astype(kind)


def setup_inputs(seed: int = 0) -> dict:
    key_of = jax.random.split(jax.random.key(seed), 14)
    hidden_in = normal_values(key_of[0], (SEQS, LENGTH, D), 1.0, 6.0, ((0, 8), (1, 4)))
    cotangent = normal_values(key_of[1], (SEQS, LENGTH, D), 1.0, 6.0, ((0, 8), (1, 4)))
    attn_gain = jnp.clip(1.0 + 0.1 * jax.random.normal(key_of[2], (D,), jnp.float32), 0.5, 1.5).astype(jnp.bfloat16)
    query_key_value_weight = normal_values(key_of[3], (D, 3, INNER), D ** -0.5, 0.21875, ((2, 4),))
    attention_output_weight = normal_values(key_of[4], (INNER, D), (7.0 / INNER ** 0.5), 4.0, ((0, 4),))
    rel_bias = normal_values(key_of[5], (HEADS, BUCKETS), 1.0, 4.0, ((0, 4),))
    bucket_table = set_ends(jax.random.randint(key_of[6], (2 * LENGTH - 1,), 0, BUCKETS), jax.random.fold_in(key_of[6], 1), 0, BUCKETS - 1).astype(jnp.int32)
    prefix_len = set_ends(jax.random.randint(key_of[7], (SEQS,), LENGTH // 10, LENGTH // 2 + 1), jax.random.fold_in(key_of[7], 1), LENGTH // 10, (LENGTH // 2 + 1) - 1).astype(jnp.int32)
    moe_gain = jnp.clip(1.0 + 0.1 * jax.random.normal(key_of[8], (D,), jnp.float32), 0.5, 1.5).astype(jnp.bfloat16)
    w_router = normal_values(key_of[9], (D, EXPERTS), (0.8 / D ** 0.5), 0.4375)
    routes_keys = jax.random.split(jax.random.fold_in(key_of[10], 1), GROUPS * N_TENSOR * SEQ_DEV * QUARTER // ROWS)
    routes_turns = jax.random.permutation(jax.random.fold_in(key_of[10], 3), GROUPS * N_TENSOR * SEQ_DEV * QUARTER // ROWS)
    routes = jax.vmap(lambda own, number: assign_block(jax.random.fold_in(key_of[10], 2), own, number, ROWS, EXPERTS, 1, CAP, 1))(routes_keys, routes_turns).reshape((GROUPS, N_TENSOR, SEQ_DEV, QUARTER, 1))
    w_expert_in = normal_values(key_of[11], (EXPERTS, D, FF), D ** -0.5, 0.21875, ((0, 4), (2, 4)))
    w_expert_out = normal_values(key_of[12], (EXPERTS, FF, D), (0.7 * EXPERTS / FF ** 0.5), 0.75, ((0, 4), (1, 4)))
    return {"hidden_in": hidden_in, "cotangent": cotangent, "attn_gain": attn_gain, "query_key_value_weight": query_key_value_weight, "attention_output_weight": attention_output_weight, "rel_bias": rel_bias, "bucket_table": bucket_table, "prefix_len": prefix_len, "moe_gain": moe_gain, "w_router": w_router, "routes": routes, "w_expert_in": w_expert_in, "w_expert_out": w_expert_out}


EPSILON = 1e-06
NEG = -1e+30
TOP_PRECISION = lax.Precision.HIGHEST

@jax.custom_vjp
def low(v):
    return lax.optimization_barrier(v.astype(jnp.bfloat16)).astype(jnp.float32)

@jax.custom_vjp
def low_back(v):
    return v

def low_keep(v):
    return (low(v), None)

def low_pass(kept, grad):
    return (grad,)

def back_keep(v):
    return (v, None)

def back_low(kept, grad):
    return (low(grad),)
low.defvjp(low_keep, low_pass)
low_back.defvjp(back_keep, back_low)

def rms_norm(values, gain_vec):
    inverse = lax.rsqrt(lax.optimization_barrier(jnp.mean(values * values, axis=-1, keepdims=True)) + EPSILON)
    return values * inverse * gain_vec

def attend_one(packed, bias_full):
    queries, keys, values, prefix = packed
    scores = jnp.einsum('ihd,jhd->hij', queries, keys, precision=TOP_PRECISION) * HEAD_DIM ** (-0.5) + bias_full
    scores = low_back(scores)
    positions = jnp.arange(LENGTH, dtype=jnp.int32)
    allowed = (positions[None, :] <= positions[:, None]) | (positions[None, :] < prefix)
    scores = jnp.where(allowed[None], scores, NEG)
    weights = low(jax.nn.softmax(scores, axis=-1))
    return jnp.einsum('hij,jhd->ihd', weights, values, precision=TOP_PRECISION)

def block_layer(params, inputs, route_rows, prefixes, bucket_index):
    attn_gain, query_key_value_weight, attention_output_weight, rel_bias, moe_gain, w_router, w_expert_in, w_expert_out = params
    seq_count = inputs.shape[0]
    token_count = seq_count * LENGTH
    first_normed = low(rms_norm(inputs, attn_gain))
    projected_rows = low_back(low(jnp.einsum('vqa,afo->vqfo', first_normed, query_key_value_weight, precision=TOP_PRECISION)))
    split_shape = (seq_count, LENGTH, HEADS, HEAD_DIM)
    queries = projected_rows[:, :, 0].reshape(split_shape)
    keys = projected_rows[:, :, 1].reshape(split_shape)
    values = projected_rows[:, :, 2].reshape(split_shape)
    bias_full = rel_bias[:, bucket_index]
    attend = jax.checkpoint(lambda packed: attend_one(packed, bias_full))
    context_rows = lax.map(attend, (queries, keys, values, prefixes))
    context_rows = low_back(low(context_rows.reshape(seq_count, LENGTH, INNER)))
    attention_result = low_back(jnp.einsum('ofq,qb->ofb', context_rows, attention_output_weight, precision=TOP_PRECISION))
    first_sum = (inputs + attention_result).reshape(token_count, D)
    normed_two = low(rms_norm(first_sum, moe_gain))
    logits = low_back(jnp.dot(normed_two, w_router, precision=TOP_PRECISION))
    router_probs = jax.nn.softmax(logits, axis=-1)
    flat_routes = route_rows.reshape(token_count)
    route_hot = (flat_routes[:, None] == jnp.arange(EXPERTS, dtype=jnp.int32)[None, :]).astype(jnp.float32)
    gate_value = lax.optimization_barrier(jnp.sum(router_probs * route_hot, axis=-1))

    def expert_step(running, packed):
        weight_in, weight_out, expert_id = packed
        pre_act = low_back(jnp.dot(normed_two, weight_in, precision=TOP_PRECISION))
        active = low(jax.nn.gelu(pre_act, approximate=False))
        result = jnp.dot(active, weight_out, precision=TOP_PRECISION)
        member = (flat_routes == expert_id).astype(jnp.float32)[:, None]
        return (running + member * result, None)
    start_sum = jnp.zeros((token_count, D), jnp.float32)
    expert_out, ignored = lax.scan(jax.checkpoint(expert_step), start_sum, (w_expert_in, w_expert_out, jnp.arange(EXPERTS, dtype=jnp.int32)))
    expert_out = low_back(expert_out)
    mixed = first_sum + gate_value[:, None] * expert_out
    return mixed.reshape(seq_count, LENGTH, D)

def reference(hidden_in, cotangent, attn_gain, query_key_value_weight, attention_output_weight, rel_bias, bucket_table, prefix_len, moe_gain, w_router, routes, w_expert_in, w_expert_out):
    positions = jnp.arange(LENGTH, dtype=jnp.int32)
    bucket_index = bucket_table[(positions[None, :] - positions[:, None] + LENGTH - 1).astype(jnp.int32)]
    route_rows = routes[..., 0].transpose(0, 2, 1, 3).reshape(SEQS, LENGTH)
    params = tuple((weight.astype(jnp.float32) for weight in (attn_gain, query_key_value_weight, attention_output_weight, rel_bias, moe_gain, w_router, w_expert_in, w_expert_out)))
    group_size = math.gcd(SEQS, max(1, 4096 // LENGTH))
    group_count = SEQS // group_size

    def regroup(array):
        return array.reshape((group_count, group_size) + array.shape[1:])

    def one_group(totals, packed):
        inputs, cot_group, route_group, prefix_group = packed

        def forward(weights, values):
            return block_layer(weights, values, route_group, prefix_group, bucket_index)
        mixed, pullback = jax.vjp(forward, params, inputs)
        weight_grads, input_grad = pullback(cot_group)
        totals = jax.tree.map(jnp.add, totals, weight_grads)
        return (totals, (mixed.astype(jnp.bfloat16), input_grad))
    zero_totals = jax.tree.map(jnp.zeros_like, params)
    totals, outputs = lax.scan(one_group, zero_totals, (regroup(hidden_in.astype(jnp.float32)), regroup(cotangent.astype(jnp.float32)), regroup(route_rows), regroup(prefix_len)))
    mixed, input_grad = outputs
    return (mixed.reshape(SEQS, LENGTH, D), input_grad.reshape(SEQS, LENGTH, D), totals[0], totals[1], totals[2], totals[3], totals[4], totals[5], totals[6], totals[7])
```

```python
import functools

import jax
import jax.numpy as jnp
from jax import lax
from jax.experimental import pallas as pl
from jax.experimental.pallas import tpu as pltpu
from jax.sharding import PartitionSpec as P

EPSILON = 1e-06
NEG = -1e30
TOP_PRECISION = lax.Precision.HIGHEST
BF = jnp.bfloat16
F32 = jnp.float32
LANES = 128
VMEM = pl.BlockSpec(memory_space=pltpu.VMEM)
SMEM = pl.BlockSpec(memory_space=pltpu.SMEM)
SQRT_HALF = 0.7071067811865476
INV_SQRT_TWO_PI = 0.3989422804014327


def params(mib):
    return pltpu.CompilerParams(vmem_limit_bytes=mib * 1024 * 1024)


def dot_nn(a, b):
    return lax.dot_general(a, b, (((1,), (0,)), ((), ())), preferred_element_type=F32)


def dot_nt(a, b):
    return lax.dot_general(a, b, (((1,), (1,)), ((), ())), preferred_element_type=F32)


def dot_tn(a, b):
    return lax.dot_general(a, b, (((0,), (0,)), ((), ())), preferred_element_type=F32)


def rms_scale(values):
    return lax.rsqrt(jnp.mean(values * values, axis=-1, keepdims=True) + EPSILON)


def norm_back(values, inverse, gain_vec, upstream):
    scaled = upstream * gain_vec
    return inverse * scaled - values * (inverse * inverse * inverse) * jnp.mean(
        scaled * values, axis=-1, keepdims=True
    )


def swap(values, axis, step):
    count = lax.axis_size(axis)
    return lax.ppermute(values, axis, [(i, i ^ step) for i in range(count)])


def skew_into(skew_ref, offset_ref, heads, width):
    for head in range(heads):
        row = jnp.broadcast_to(offset_ref[head : head + 1, :], (LANES, width))
        skew_ref[head] = pltpu.roll(row, width - (LANES - 1), 1, stride=1, stride_axis=0)


def attend_kernel(parts, heads, where_ref, *refs):
    x_refs = refs[:parts]
    gain_ref, weight_ref, offset_ref = refs[parts : parts + 3]
    normed_ref, proj_ref, lse_ref = refs[parts + 3 : parts + 6]
    ctx_refs = refs[parts + 6 : 2 * parts + 6]
    skew_ref, ctx_ref = refs[2 * parts + 6 :]
    quarter = x_refs[0].shape[0]
    length = quarter * parts
    inner = weight_ref.shape[1] // 3
    head_dim = inner // heads
    place, prefix = where_ref[0], where_ref[1]
    lane = lax.broadcasted_iota(jnp.int32, (1, 3 * inner), 1)
    column_scale = jnp.where(lane < inner, F32(head_dim ** (-0.5)), F32(1.0))
    for part in range(parts):
        x = x_refs[part][...].astype(F32)
        normed = (x * rms_scale(x) * gain_ref[...]).astype(BF)
        rows = pl.ds(pl.multiple_of((place ^ part) * quarter, quarter), quarter)
        normed_ref[rows, :] = normed
        proj_ref[rows, :] = (dot_nn(normed, weight_ref[...]) * column_scale).astype(BF)
    skew_into(skew_ref, offset_ref, heads, 2 * length)
    tiles = length // LANES
    per_block = quarter // LANES
    for block in range(parts):
        first = block * quarter
        reach = max(length // 2, first + quarter)
        key_pos = first + lax.broadcasted_iota(jnp.int32, (quarter, reach - first), 1)
        query_pos = first + lax.broadcasted_iota(jnp.int32, (quarter, reach - first), 0)
        allowed = (key_pos <= query_pos) | (key_pos < prefix)
        pieces, logs = [], []
        for head in range(heads):
            low = head * head_dim
            query = proj_ref[first : first + quarter, low : low + head_dim]
            keys = proj_ref[0:reach, inner + low : inner + low + head_dim]
            values = proj_ref[0:reach, 2 * inner + low : 2 * inner + low + head_dim]
            bias = jnp.concatenate(
                [
                    skew_ref[
                        head,
                        :,
                        LANES * (tiles - 1 - block * per_block - sub) : LANES
                        * (tiles - 1 - block * per_block - sub)
                        + reach,
                    ]
                    for sub in range(per_block)
                ],
                axis=0,
            )
            scores = dot_nt(query, keys) + bias
            tail = jnp.where(allowed, scores[:, first:], F32(NEG))
            scores = jnp.concatenate([scores[:, :first], tail], axis=1) if first else tail
            peak = jnp.max(scores, axis=1, keepdims=True)
            exponent = jnp.exp(scores - peak)
            total = jnp.sum(exponent, axis=1, keepdims=True)
            pieces.append(dot_nn(exponent.astype(BF), values) / total)
            logs.append(jnp.broadcast_to(peak + jnp.log(total), (quarter, LANES)))
        ctx_ref[place ^ block] = jnp.concatenate(pieces, axis=1).astype(BF)
        lane_row = lax.broadcasted_iota(jnp.int32, (quarter, LANES), 1)
        stacked = logs[0]
        for head in range(1, heads):
            stacked = jnp.where(lane_row == head, logs[head], stacked)
        lse_ref[block] = jnp.transpose(stacked)[0:8, :]
    for part in range(parts):
        ctx_refs[part][...] = ctx_ref[part]


def attend(where, blocks, gain, weight, offsets, heads):
    parts = len(blocks)
    quarter, width = blocks[0].shape
    length = parts * quarter
    inner3 = weight.shape[1]
    outs = pl.pallas_call(
        functools.partial(attend_kernel, parts, heads),
        out_shape=[
            jax.ShapeDtypeStruct((length, width), BF),
            jax.ShapeDtypeStruct((length, inner3), BF),
            jax.ShapeDtypeStruct((parts, 8, quarter), F32),
        ]
        + [jax.ShapeDtypeStruct((quarter, inner3 // 3), BF)] * parts,
        in_specs=[SMEM] + [VMEM] * (parts + 3),
        out_specs=[VMEM] * (parts + 3),
        scratch_shapes=[
            pltpu.VMEM((heads, LANES, 2 * length), F32),
            pltpu.VMEM((parts, quarter, inner3 // 3), BF),
        ],
        compiler_params=params(40),
    )(where, *blocks, gain, weight, offsets)
    return outs[0], outs[1], outs[2], outs[3:]


def attend_back_kernel(parts, heads, experts, split, where_ref, *refs):
    cot_refs = refs[:parts]
    ctx_refs = refs[parts : 2 * parts]
    proj_ref, normed_ref, lse_ref, weight_ref, offset_ref = refs[2 * parts : 2 * parts + 5]
    outs = refs[2 * parts + 5 :]
    own_ref = outs[0]
    send_refs = outs[1:parts]
    gain_ref, fold_out_ref, keep_ref, give_ref = outs[parts : parts + 4]
    skew_ref, fold_ref, cot_ref, ctx_ref, dproj_ref, key_acc, value_acc = outs[parts + 4 :]
    quarter = cot_refs[0].shape[0]
    length = quarter * parts
    inner = weight_ref.shape[1] // 3
    head_dim = inner // heads
    place, prefix, core, layer = where_ref[0], where_ref[1], where_ref[2], where_ref[3]
    for part in range(parts):
        rows = pl.ds(pl.multiple_of((place ^ part) * quarter, quarter), quarter)
        cot_ref[rows, :] = cot_refs[part][...]
        ctx_ref[rows, :] = ctx_refs[part][...]
    skew_into(skew_ref, offset_ref, heads, 2 * length)
    fold_ref[...] = jnp.zeros_like(fold_ref)
    key_acc[...] = jnp.zeros_like(key_acc)
    value_acc[...] = jnp.zeros_like(value_acc)
    keys_across = jnp.transpose(proj_ref[:, inner : 2 * inner])
    head_row = lax.broadcasted_iota(jnp.int32, (8, inner), 0)
    head_lane = lax.broadcasted_iota(jnp.int32, (8, inner), 1)
    picks = (head_lane // head_dim == head_row).astype(BF)
    for block in range(parts):
        first = block * quarter
        reach = max(length // 2, first + quarter)
        key_pos = first + lax.broadcasted_iota(jnp.int32, (reach - first, quarter), 0)
        query_pos = first + lax.broadcasted_iota(jnp.int32, (reach - first, quarter), 1)
        allowed = (key_pos <= query_pos) | (key_pos < prefix)
        product = cot_ref[first : first + quarter, :].astype(F32) * ctx_ref[
            first : first + quarter, :
        ].astype(F32)
        high = product.astype(BF)
        rest = (product - high.astype(F32)).astype(BF)
        inner_sum = dot_nt(picks, high) + dot_nt(picks, rest)
        query_pieces = []
        for head in range(heads):
            low = head * head_dim
            query = proj_ref[first : first + quarter, low : low + head_dim]
            keys = proj_ref[0:reach, inner + low : inner + low + head_dim]
            values = proj_ref[0:reach, 2 * inner + low : 2 * inner + low + head_dim]
            grad = cot_ref[first : first + quarter, low : low + head_dim]
            bias = jnp.concatenate(
                [
                    skew_ref[
                        head,
                        :,
                        first - LANES * sub + length - LANES : first
                        - LANES * sub
                        + length
                        - LANES
                        + quarter,
                    ]
                    for sub in range(reach // LANES)
                ],
                axis=0,
            )
            scores = dot_nt(keys, query) + bias
            tail = jnp.where(allowed, scores[first:], F32(NEG))
            scores = jnp.concatenate([scores[:first], tail], axis=0) if first else tail
            probs = jnp.exp(scores - lse_ref[block, head : head + 1, :])
            prob_grad = dot_nt(values, grad)
            score_grad = (probs * (prob_grad - inner_sum[head : head + 1, :])).astype(BF)
            wide = score_grad.astype(F32)
            for sub in range(reach // LANES):
                column = first - LANES * sub + length - LANES
                fold_ref[head, :, column : column + quarter] += wide[
                    LANES * sub : LANES * (sub + 1)
                ]
            value_acc[head, 0:reach, :] += dot_nn(probs.astype(BF), grad)
            key_acc[head, 0:reach, :] += dot_nn(score_grad, query)
            query_pieces.append(dot_nn(keys_across[low : low + head_dim, 0:reach], score_grad))
        query_grad = jnp.transpose(jnp.concatenate(query_pieces, axis=0)) * F32(head_dim ** (-0.5))
        dproj_ref[first : first + quarter, 0:inner] = query_grad.astype(BF)
    dproj_ref[:, inner : 3 * inner] = jnp.concatenate(
        [key_acc[head] for head in range(heads)] + [value_acc[head] for head in range(heads)],
        axis=1,
    ).astype(BF)
    gain_sum = jnp.zeros((1, normed_ref.shape[1]), F32)
    for part in reversed(range(parts)):
        rows = pl.ds(pl.multiple_of((place ^ part) * quarter, quarter), quarter)
        upstream = dot_nt(dproj_ref[rows, :], weight_ref[...])
        gain_sum = gain_sum + jnp.sum(
            upstream * normed_ref[rows, :].astype(F32), axis=0, keepdims=True
        )
        if part:
            send_refs[part - 1][...] = upstream.astype(BF)
        else:
            own_ref[...] = upstream
    gain_ref[...] = jnp.broadcast_to(gain_sum, gain_ref.shape)
    width = normed_ref.shape[1]
    piece = width // (2 * split)
    for half in range(2):
        grad_rows = dot_tn(
            normed_ref[:, half * (width // 2) : (half + 1) * (width // 2)], dproj_ref[...]
        )
        mine = core == half
        for part in range(split):
            chunk = grad_rows[part * piece : (part + 1) * piece]
            slot = (layer ^ part) if split > 1 else part

            @pl.when(mine)
            def _(chunk=chunk, slot=slot):
                keep_ref[slot] = chunk

            @pl.when(jnp.logical_not(mine))
            def _(chunk=chunk, slot=slot):
                give_ref[slot] = chunk.astype(BF)

    row_index = lax.broadcasted_iota(jnp.int32, (LANES, 2 * length), 0)
    for head in range(heads):
        tile = fold_ref[head]
        for bit in range(7):
            moved = pltpu.roll(tile, 2 * length - (1 << bit), 1)
            tile = jnp.where(((row_index >> bit) & 1) == 1, moved, tile)
        tile = pltpu.roll(tile, LANES - 1, 1)
        fold_out_ref[head : head + 1, :] = jnp.sum(tile, axis=0, keepdims=True)
    fold_out_ref[heads:, :] = jnp.zeros((8 - heads, 2 * length), F32)


def attend_back(where, cots, ctxs, proj, normed, lse, weight, offsets, heads, experts, split):
    parts = len(cots)
    quarter, inner = cots[0].shape
    width = normed.shape[1]
    length = parts * quarter
    piece = width // (2 * split)
    outs = pl.pallas_call(
        functools.partial(attend_back_kernel, parts, heads, experts, split),
        out_shape=[jax.ShapeDtypeStruct((quarter, width), F32)]
        + [jax.ShapeDtypeStruct((quarter, width), BF)] * (parts - 1)
        + [
            jax.ShapeDtypeStruct((8, width), F32),
            jax.ShapeDtypeStruct((8, 2 * length), F32),
            jax.ShapeDtypeStruct((split, piece, 3 * inner), F32),
            jax.ShapeDtypeStruct((split, piece, 3 * inner), BF),
        ],
        in_specs=[SMEM] + [VMEM] * (2 * parts + 5),
        out_specs=[VMEM] * (parts + 4),
        scratch_shapes=[
            pltpu.VMEM((heads, LANES, 2 * length), F32),
            pltpu.VMEM((heads, LANES, 2 * length), F32),
            pltpu.VMEM((length, inner), BF),
            pltpu.VMEM((length, inner), BF),
            pltpu.VMEM((length, 3 * inner), BF),
            pltpu.VMEM((heads, length, inner // heads), F32),
            pltpu.VMEM((heads, length, inner // heads), F32),
        ],
        compiler_params=params(48),
    )(where, *cots, *ctxs, proj, normed, lse, weight, offsets)
    return outs[0], outs[1:parts], outs[parts], outs[parts + 1], outs[parts + 2], outs[parts + 3]


def expert_kernel(sources, units, experts, where_ref, *refs):
    refs = list(refs)
    row_refs, cot_refs = refs[:sources], refs[sources : 2 * sources]
    base = 2 * sources
    in_refs, out_w_refs = refs[base : base + units], refs[base + units : base + 2 * units]
    router_ref = refs[base + 2 * units]
    outs = refs[base + 2 * units + 1 :]
    out_refs, grad_refs = outs[:sources], outs[sources : 2 * sources]
    rows_ref, gated_ref, act_ref, hidden_ref, logit_ref = outs[2 * sources : 2 * sources + 5]
    total_ref, back_ref = outs[2 * sources + 5 :]
    name = where_ref[3]
    slots, width = rows_ref.shape
    capacity = slots // sources
    span = in_refs[0].shape[1]
    for source in range(sources):
        rows_ref[source * capacity : (source + 1) * capacity, :] = row_refs[source][...]
    step_rows = 256

    def step(index, carry):
        rows_at = pl.ds(pl.multiple_of(index * step_rows, step_rows), step_rows)
        rows = rows_ref[rows_at, :]
        lane = lax.broadcasted_iota(jnp.int32, (step_rows, LANES), 1)
        logits = jnp.where(lane < experts, dot_nn(rows, router_ref[...]), F32(NEG))
        logits = jnp.exp(logits - jnp.max(logits, axis=1, keepdims=True))
        router = logits / jnp.sum(logits, axis=1, keepdims=True)
        hot = (lane == name).astype(F32)
        gate = jnp.sum(router * hot, axis=1, keepdims=True)
        cot = gated_ref[rows_at, :].astype(F32)
        gated = (cot * gate).astype(BF)
        total = jnp.zeros((step_rows, width), F32)
        back = jnp.zeros((step_rows, width), F32)
        for unit in range(units):
            columns = slice(unit * span, (unit + 1) * span)
            pre_act = dot_nn(rows, in_refs[unit][...])
            below = 0.5 + 0.5 * lax.erf(pre_act * F32(SQRT_HALF))
            active = (pre_act * below).astype(BF)
            slope = below + pre_act * jnp.exp(pre_act * pre_act * F32(-0.5)) * F32(INV_SQRT_TWO_PI)
            hidden = (dot_nt(gated, out_w_refs[unit][...]) * slope).astype(BF)
            act_ref[rows_at, columns] = active
            hidden_ref[rows_at, columns] = hidden
            total = total + dot_nn(active, out_w_refs[unit][...])
            back = back + dot_nt(hidden, in_refs[unit][...])
        gate_grad = jnp.sum(cot * total, axis=1, keepdims=True)
        logit_grad = ((gate_grad * gate) * (hot - router)).astype(BF)
        back = back + dot_nt(logit_grad, router_ref[...])
        gated_ref[rows_at, :] = gated
        logit_ref[rows_at, :] = logit_grad
        total_ref[rows_at, :] = total.astype(BF)
        back_ref[rows_at, :] = back.astype(BF)
        return carry

    for source in range(sources):
        gated_ref[source * capacity : (source + 1) * capacity, :] = cot_refs[source][...]
    lax.fori_loop(0, slots // step_rows, step, 0)
    for source in range(sources):
        out_refs[source][...] = total_ref[source * capacity : (source + 1) * capacity, :]
        grad_refs[source][...] = back_ref[source * capacity : (source + 1) * capacity, :]


def run_expert(where, rows, cots, in_units, out_units, router, experts):
    sources, units = len(rows), len(in_units)
    capacity, width = rows[0].shape
    slots = sources * capacity
    hidden = units * in_units[0].shape[1]
    outs = pl.pallas_call(
        functools.partial(expert_kernel, sources, units, experts),
        out_shape=[jax.ShapeDtypeStruct((capacity, width), BF)] * (2 * sources)
        + [
            jax.ShapeDtypeStruct((slots, width), BF),
            jax.ShapeDtypeStruct((slots, width), BF),
            jax.ShapeDtypeStruct((slots, hidden), BF),
            jax.ShapeDtypeStruct((slots, hidden), BF),
            jax.ShapeDtypeStruct((slots, LANES), BF),
        ],
        in_specs=[SMEM] + [VMEM] * (2 * sources + 2 * units + 1),
        out_specs=[VMEM] * (2 * sources + 5),
        scratch_shapes=[pltpu.VMEM((slots, width), BF), pltpu.VMEM((slots, width), BF)],
        compiler_params=params(56),
    )(where, *rows, *cots, *in_units, *out_units, router)
    return outs[:sources], outs[sources : 2 * sources], outs[2 * sources :]


def body(
    hidden_in,
    cotangent,
    attn_gain,
    query_key_value_weight,
    attention_output_weight,
    rel_bias,
    bucket_table,
    prefix_len,
    moe_gain,
    w_router,
    routes,
    w_expert_in,
    w_expert_out,
):
    seq_count, quarter, model_width = hidden_in.shape
    parts = lax.axis_size("tensor")
    layers = lax.axis_size("expert")
    length = quarter * parts
    row_count = seq_count * quarter
    experts = w_router.shape[1]
    capacity = max(2, 2 * row_count // experts)
    slot_count = experts * capacity
    heads, buckets = rel_bias.shape
    inner = query_key_value_weight.shape[2]
    span = w_expert_in.shape[2] // 2
    near = layers <= 8
    place, layer, core = lax.axis_index("tensor"), lax.axis_index("expert"), lax.axis_index("dp")
    where = jnp.stack([place, prefix_len[0], core, layer]).astype(jnp.int32)

    own_hidden = hidden_in[0]
    hidden_blocks = [own_hidden] + [swap(own_hidden, "tensor", k) for k in range(1, parts)]

    chosen = routes.reshape(row_count)
    relative = (chosen ^ layer) if near else chosen
    route_hot = (relative[:, None] == jnp.arange(experts, dtype=jnp.int32)[None, :]).astype(BF)
    rank = jnp.arange(row_count, dtype=jnp.int32)
    below = (rank[None, :] < rank[:, None]).astype(BF)
    before = jnp.dot(below, route_hot, preferred_element_type=F32)
    slot_index = jnp.sum(before * route_hot.astype(F32), axis=1).astype(jnp.int32)
    target = relative * capacity + slot_index
    place_hot = (jnp.arange(slot_count, dtype=jnp.int32)[:, None] == target[None, :]).astype(BF)

    def pack(values):
        return dot_nn(place_hot, values).astype(BF).reshape(experts, capacity, model_width)

    def exchange(blocks):
        if near:
            return [blocks[0]] + [swap(blocks[k], "expert", k) for k in range(1, layers)]
        whole = jnp.concatenate(blocks, axis=0).reshape(experts, capacity, model_width)
        moved = lax.all_to_all(whole, "expert", split_axis=0, concat_axis=0, tiled=True)
        return [moved.reshape(slot_count, model_width)]

    def blocks_of(packed):
        return [packed[k] for k in range(experts)]

    cot_blocks = exchange(blocks_of(pack(cotangent[0])))

    out_weights = [attention_output_weight] + [
        swap(attention_output_weight, "tensor", k) for k in range(1, parts)
    ]

    in_own = lax.dynamic_slice(w_expert_in[0], (0, core * span), (model_width, span))
    in_other = lax.dynamic_slice(w_expert_in[0], (0, (1 - core) * span), (model_width, span))
    out_own = lax.dynamic_slice(w_expert_out[0], (core * span, 0), (span, model_width))
    out_other = lax.dynamic_slice(w_expert_out[0], ((1 - core) * span, 0), (span, model_width))
    in_a = [in_own] + [swap(in_own, "tensor", k) for k in range(1, parts)]
    out_a = [out_own] + [swap(out_own, "tensor", k) for k in range(1, parts)]
    in_b = [in_other] + [swap(in_a[k], "dp", 1) for k in range(1, parts)]
    out_b = [out_other] + [swap(out_a[k], "dp", 1) for k in range(1, parts)]

    weight = query_key_value_weight.reshape(model_width, 3 * inner)
    table_hot = (
        bucket_table[None, :] == jnp.arange(buckets, dtype=jnp.int32)[:, None]
    ).astype(F32)
    table_hot = jnp.pad(table_hot, ((0, 0), (0, 1)))
    rel_padded = jnp.pad(rel_bias.astype(F32), ((0, 8 - heads), (0, 0)))
    offset_bias = jnp.dot(rel_padded, table_hot, precision=TOP_PRECISION)
    back_table = jnp.flip(bucket_table)
    back_hot = (back_table[None, :] == jnp.arange(buckets, dtype=jnp.int32)[:, None]).astype(F32)
    back_hot = jnp.pad(back_hot, ((0, 0), (0, 1)))
    offset_back = jnp.dot(rel_padded, back_hot, precision=TOP_PRECISION)
    attn_scale = attn_gain.astype(F32)
    normed_one, projected, lse, contexts = attend(
        where, hidden_blocks, attn_scale[None], weight, offset_bias, heads
    )
    own_contexts = [contexts[0]] + [swap(contexts[k], "tensor", k) for k in range(1, parts)]

    own_float = own_hidden.astype(F32)
    first_sum = own_float + sum(dot_nn(c, w) for c, w in zip(own_contexts, out_weights))
    moe_scale = moe_gain.astype(F32)
    inverse_two = rms_scale(first_sum)
    normed_two = (first_sum * inverse_two * moe_scale).astype(BF)
    rows = exchange(blocks_of(pack(normed_two)))

    router = jnp.pad(w_router, ((0, 0), (0, LANES - experts)))
    out_blocks, grad_blocks, kept = run_expert(
        where, rows, cot_blocks, in_a + in_b, out_a + out_b, router, experts
    )
    all_rows, all_gated, active, hidden_grad, logit_grad = kept
    grads_home = exchange(list(grad_blocks))
    outs_home = exchange(list(out_blocks))

    def unpack(blocks):
        return dot_tn(place_hot, jnp.concatenate(blocks, axis=0))

    normed_two_grad = unpack(grads_home)
    cot_rows = cotangent[0].astype(F32)
    moe_gain_part = jnp.sum(normed_two_grad * first_sum * inverse_two, axis=0)
    residual_grad = cot_rows + norm_back(first_sum, inverse_two, moe_scale, normed_two_grad)
    residual_low = residual_grad.astype(BF)
    context_cots = [dot_nt(residual_low, w).astype(BF) for w in out_weights]
    context_cots = [context_cots[0]] + [swap(context_cots[k], "tensor", k) for k in range(1, parts)]

    half = parts * span
    in_give = dot_tn(all_rows, hidden_grad[:, half:]).astype(BF)
    out_give = dot_tn(active[:, half:], all_gated).astype(BF)
    in_got = swap(in_give, "dp", 1)
    out_got = swap(out_give, "dp", 1)
    in_sum, out_sum = [], []
    for k in range(parts):
        cols = slice(k * span, (k + 1) * span)
        in_sum.append(dot_tn(all_rows, hidden_grad[:, cols]) + in_got[:, cols].astype(F32))
        out_sum.append(dot_tn(active[:, cols], all_gated) + out_got[cols].astype(F32))
    in_total, out_total = in_sum[0], out_sum[0]
    for k in range(1, parts):
        in_total = in_total + swap(in_sum[k].astype(BF), "tensor", k).astype(F32)
        out_total = out_total + swap(out_sum[k].astype(BF), "tensor", k).astype(F32)
    in_peer, out_peer = swap(in_total, "dp", 1), swap(out_total, "dp", 1)
    low_core = core == 0
    expert_in_grad = jnp.concatenate(
        [jnp.where(low_core, in_total, in_peer), jnp.where(low_core, in_peer, in_total)], axis=1
    )
    expert_out_grad = jnp.concatenate(
        [jnp.where(low_core, out_total, out_peer), jnp.where(low_core, out_peer, out_total)], axis=0
    )

    expert_out = unpack(outs_home)
    logits = jnp.dot(normed_two, w_router, preferred_element_type=F32)
    router_probs = jax.nn.softmax(logits, axis=-1)
    own_hot = (chosen[:, None] == jnp.arange(experts, dtype=jnp.int32)[None, :]).astype(F32)
    gate_value = jnp.sum(router_probs * own_hot, axis=-1)
    layer_out = (first_sum + gate_value[:, None] * expert_out).astype(BF)

    side = model_width // 2
    low_cols = lax.dynamic_slice(residual_low, (0, core * side), (row_count, side))
    high_cols = lax.dynamic_slice(residual_low, (0, (1 - core) * side), (row_count, side))
    stacked_ctx = jnp.concatenate(own_contexts, axis=1)
    wo_got = swap(dot_tn(stacked_ctx, high_cols).astype(BF), "dp", 1)
    wo_keep = dot_tn(stacked_ctx, low_cols) + wo_got.astype(F32)
    wo_total = wo_keep[:inner]
    for k in range(1, parts):
        wo_total = wo_total + swap(
            wo_keep[k * inner : (k + 1) * inner].astype(BF), "tensor", k
        ).astype(F32)

    def sum_layers(values):
        if not near:
            return lax.psum(values, "expert")
        step = 1
        while step < layers:
            values = values.astype(BF)
            values = values.astype(F32) + swap(values, "expert", step).astype(F32)
            step *= 2
        return values

    wo_total = sum_layers(wo_total)
    wo_peer = swap(wo_total, "dp", 1)
    attn_out_grad = jnp.concatenate(
        [jnp.where(low_core, wo_total, wo_peer), jnp.where(low_core, wo_peer, wo_total)], axis=1
    )

    split = layers if layers == 4 else 1
    own_up, send_ups, gain_part, fold, keep, give = attend_back(
        where, context_cots, contexts, projected, normed_one, lse, weight, offset_back,
        heads, experts, split,
    )
    ups = own_up
    for k in range(1, parts):
        ups = ups + swap(send_ups[k - 1], "tensor", k).astype(F32)
    inverse_own = rms_scale(own_float)
    input_grad = residual_grad + norm_back(own_float, inverse_own, attn_scale, ups)

    summed = keep + swap(give, "dp", 1).astype(F32)
    if split > 1:
        low = summed.astype(BF)
        mine = summed[0]
        for k in range(1, layers):
            mine = mine + swap(low[k], "expert", k).astype(F32)
        mine = mine.astype(BF)
        pieces = jnp.stack([mine] + [swap(mine, "expert", k) for k in range(1, layers)])
    else:
        pieces = lax.psum(summed, "expert")
    peer_pieces = swap(pieces, "dp", 1)
    qkv_grad = assemble(where, pieces, peer_pieces).reshape(model_width, 3, inner)

    bias_part = lax.dot_general(fold[:heads], back_hot, (((1,), (1,)), ((), ())), precision=TOP_PRECISION)
    router_part = dot_tn(logit_grad, all_rows)[:experts]

    def sum_all(values, axes):
        for axis in axes:
            if axis == "expert" and not near:
                values = lax.psum(values, "expert")
                continue
            step = 1
            while step < lax.axis_size(axis):
                values = values + swap(values, axis, step)
                step *= 2
        return values

    early = jnp.concatenate([moe_gain_part[None], router_part], axis=0)
    early = sum_all(early, ("dp", "expert", "tensor"))
    bias_row = jnp.pad(bias_part.reshape(1, heads * buckets), ((0, 0), (0, model_width - heads * buckets)))
    late = jnp.concatenate([gain_part[:1] / attn_scale[None], bias_row], axis=0)
    late = sum_all(late, ("dp", "expert"))
    bias_grad = late[1, : heads * buckets].reshape(heads, buckets)
    gain_row = sum_all(late[:1], ("tensor",))
    share = model_width // parts
    early = lax.dynamic_slice(early, (0, place * share), (1 + experts, share))
    gain_own = lax.dynamic_slice(gain_row, (0, place * share), (1, share))
    return (
        layer_out.reshape(seq_count, quarter, model_width),
        input_grad.reshape(seq_count, quarter, model_width),
        gain_own[0],
        qkv_grad,
        attn_out_grad,
        bias_grad,
        early[0],
        early[1:].T,
        expert_in_grad[None],
        expert_out_grad[None],
    )


def assemble_kernel(where_ref, mine_ref, peer_ref, out_ref):
    split, piece, _ = mine_ref.shape
    core, layer = where_ref[2], where_ref[3]
    for part in range(split):
        slot = (layer ^ part) if split > 1 else part
        for ref, side in ((mine_ref, core), (peer_ref, 1 - core)):
            row = pl.multiple_of((side * split + slot) * piece, 8)
            out_ref[pl.ds(row, piece), :] = ref[part].astype(F32)


def assemble(where, mine, peer):
    split, piece, columns = mine.shape
    return pl.pallas_call(
        assemble_kernel,
        out_shape=jax.ShapeDtypeStruct((2 * split * piece, columns), F32),
        in_specs=[SMEM, VMEM, VMEM],
        out_specs=VMEM,
        compiler_params=params(16),
    )(where, mine, peer)


def solution(mesh):
    placed = (
        P(("dp", "expert"), "tensor", None),
        P(("dp", "expert"), "tensor", None),
        P(),
        P(None, None, "tensor"),
        P("tensor", None),
        P("tensor", None),
        P(),
        P(("dp", "expert")),
        P(),
        P(),
        P(("dp", "expert"), "tensor", None, None, None),
        P("expert", None, "tensor"),
        P("expert", "tensor", None),
    )
    return jax.shard_map(
        body,
        mesh=mesh,
        in_specs=placed,
        out_specs=(
            P(("dp", "expert"), "tensor", None),
            P(("dp", "expert"), "tensor", None),
            P("tensor"),
            P(None, None, "tensor"),
            P("tensor", None),
            P("tensor", None),
            P("tensor"),
            P("tensor", None),
            P("expert", None, "tensor"),
            P("expert", "tensor", None),
        ),
        check_vma=False,
    )
```

```python
import functools

import jax
import jax.numpy as jnp
from jax import lax
from jax.experimental import pallas as pl
from jax.experimental.pallas import tpu as pltpu
from jax.sharding import PartitionSpec as P

EPSILON = 1e-06
NEG = -1e30
TOP_PRECISION = lax.Precision.HIGHEST
BF = jnp.bfloat16
F32 = jnp.float32
LANES = 128
VMEM = pl.BlockSpec()
SMEM = pl.BlockSpec(memory_space=pltpu.SMEM)
SQRT_HALF = 0.7071067811865476
INV_SQRT_TWO_PI = 0.3989422804014327


def params(mib):
    return pltpu.CompilerParams(vmem_limit_bytes=mib * 1024 * 1024)


def cost(flops, moved):
    return pl.CostEstimate(flops=int(flops), bytes_accessed=int(moved), transcendentals=0)


def dot_nn(a, b):
    return lax.dot_general(a, b, (((1,), (0,)), ((), ())), preferred_element_type=F32)


def dot_nt(a, b):
    return lax.dot_general(a, b, (((1,), (1,)), ((), ())), preferred_element_type=F32)


def dot_tn(a, b):
    return lax.dot_general(a, b, (((0,), (0,)), ((), ())), preferred_element_type=F32)


def rms_scale(values):
    return lax.rsqrt(jnp.mean(values * values, axis=-1, keepdims=True) + EPSILON)


def norm_back(values, inverse, gain_vec, upstream):
    scaled = upstream * gain_vec
    return inverse * scaled - values * (inverse * inverse * inverse) * jnp.mean(
        scaled * values, axis=-1, keepdims=True
    )


def swap(values, axis, step):
    count = lax.axis_size(axis)
    return lax.ppermute(values, axis, [(i, i ^ step) for i in range(count)])


def skew_into(skew_ref, offset_ref, heads, width):
    for head in range(heads):
        row = jnp.broadcast_to(offset_ref[head : head + 1, :], (LANES, width))
        skew_ref[head] = pltpu.roll(row, width - (LANES - 1), 1, stride=1, stride_axis=0)


def attend_kernel(parts, heads, where_ref, *refs):
    x_refs = refs[:parts]
    gain_ref, weight_ref, offset_ref = refs[parts : parts + 3]
    normed_ref, proj_ref, lse_ref, ctx_ref = refs[parts + 3 : parts + 7]
    send_refs, skew_ref = refs[parts + 7 : 2 * parts + 7], refs[2 * parts + 7]
    quarter = x_refs[0].shape[0]
    length = quarter * parts
    inner = weight_ref.shape[0] // 3
    head_dim = inner // heads
    place, prefix = where_ref[0], where_ref[1]
    lane = lax.broadcasted_iota(jnp.int32, (1, 3 * inner), 1)
    column_scale = jnp.where(lane < inner, F32(head_dim ** (-0.5)), F32(1.0))
    for part in range(parts):
        x = x_refs[part][...].astype(F32)
        normed = (x * rms_scale(x) * gain_ref[...]).astype(BF)
        rows = pl.ds(pl.multiple_of((place ^ part) * quarter, quarter), quarter)
        normed_ref[rows, :] = normed
        proj_ref[rows, :] = (dot_nt(normed, weight_ref[...]) * column_scale).astype(BF)
    skew_into(skew_ref, offset_ref, heads, 2 * length)
    tiles = length // LANES
    per_block = quarter // LANES
    for block in range(parts):
        first = block * quarter
        reach = max(length // 2, first + quarter)
        key_pos = first + lax.broadcasted_iota(jnp.int32, (quarter, reach - first), 1)
        query_pos = first + lax.broadcasted_iota(jnp.int32, (quarter, reach - first), 0)
        allowed = (key_pos <= query_pos) | (key_pos < prefix)
        pieces, logs = [], []
        for head in range(heads):
            low = head * head_dim
            query = proj_ref[first : first + quarter, low : low + head_dim]
            keys = proj_ref[0:reach, inner + low : inner + low + head_dim]
            values = proj_ref[0:reach, 2 * inner + low : 2 * inner + low + head_dim]
            bias = jnp.concatenate(
                [
                    skew_ref[
                        head,
                        :,
                        LANES * (tiles - 1 - block * per_block - sub) : LANES
                        * (tiles - 1 - block * per_block - sub)
                        + reach,
                    ]
                    for sub in range(per_block)
                ],
                axis=0,
            )
            scores = dot_nt(query, keys) + bias
            tail = jnp.where(allowed, scores[:, first:], F32(NEG))
            scores = jnp.concatenate([scores[:, :first], tail], axis=1) if first else tail
            peak = jnp.max(scores, axis=1, keepdims=True)
            exponent = jnp.exp(scores - peak)
            total = jnp.sum(exponent, axis=1, keepdims=True)
            pieces.append(dot_nn(exponent.astype(BF), values) / total)
            logs.append(jnp.broadcast_to(peak + jnp.log(total), (quarter, LANES)))
        ctx_ref[block] = jnp.concatenate(pieces, axis=1).astype(BF)
        lane_row = lax.broadcasted_iota(jnp.int32, (quarter, LANES), 1)
        stacked = logs[0]
        for head in range(1, heads):
            stacked = jnp.where(lane_row == head, logs[head], stacked)
        lse_ref[block] = jnp.transpose(stacked)[0:8, :]
    for part in range(parts):
        send_refs[part][...] = ctx_ref[place ^ part]


def attend(where, blocks, gain, weight, offsets, heads):
    parts = len(blocks)
    quarter, width = blocks[0].shape
    length = parts * quarter
    inner3 = weight.shape[0]
    outs = pl.pallas_call(
        functools.partial(attend_kernel, parts, heads),
        out_shape=[
            jax.ShapeDtypeStruct((length, width), BF),
            jax.ShapeDtypeStruct((length, inner3), BF),
            jax.ShapeDtypeStruct((parts, 8, quarter), F32),
            jax.ShapeDtypeStruct((parts, quarter, inner3 // 3), BF),
        ]
        + [jax.ShapeDtypeStruct((quarter, inner3 // 3), BF)] * parts,
        in_specs=[SMEM] + [VMEM] * (parts + 3),
        out_specs=[VMEM] * (4 + parts),
        scratch_shapes=[pltpu.VMEM((heads, LANES, 2 * length), F32)],
        compiler_params=params(60),
        cost_estimate=cost(5e+10, 1e4),
    )(where, *blocks, gain, weight, offsets)
    return outs[0], outs[1], outs[2], outs[3], outs[4:]


def prepare_kernel(experts, capacity, chosen_ref, cot_ref, table_ref, bias_ref, router_in_ref, *outs):
    pack_ref, unpack_ref, packed_ref, hot_ref, offset_ref, back_ref, router_ref = outs
    slots, rows = pack_ref.shape
    chosen = chosen_ref[...]
    hot = (lax.broadcasted_iota(jnp.int32, (LANES, rows), 0) == chosen).astype(F32)
    earlier = lax.broadcasted_iota(jnp.int32, (rows, rows), 0)
    later = lax.broadcasted_iota(jnp.int32, (rows, rows), 1)
    before = dot_nn(hot.astype(BF), (earlier < later).astype(BF))
    slot = jnp.sum(before * hot, axis=0, keepdims=True)
    target = chosen * capacity + slot.astype(jnp.int32)
    pack = (lax.broadcasted_iota(jnp.int32, (slots, rows), 0) == target).astype(F32)
    pack_ref[...] = pack.astype(BF)
    unpack_ref[...] = jnp.transpose(pack).astype(BF)
    hot_ref[...] = jnp.transpose(hot)
    packed_ref[...] = dot_nn(pack.astype(BF), cot_ref[...]).astype(BF)
    heads, buckets = bias_ref.shape
    length = table_ref.shape[1]
    for row, out in ((0, offset_ref), (1, back_ref)):
        table = lax.broadcasted_iota(jnp.int32, (buckets, length), 0) == table_ref[row : row + 1, :]
        out[0:heads, :] = dot_nn(bias_ref[...], table.astype(BF))
        out[heads:, :] = jnp.zeros((8 - heads, length), F32)
    router_ref[...] = jnp.zeros_like(router_ref)
    router_ref[0:experts, :] = router_in_ref[...]


def prepare(chosen, cot, tables, bias, router, capacity):
    experts, width = router.shape
    rows = chosen.shape[1]
    slots = experts * capacity
    return pl.pallas_call(
        functools.partial(prepare_kernel, experts, capacity),
        out_shape=[
            jax.ShapeDtypeStruct((slots, rows), BF),
            jax.ShapeDtypeStruct((rows, slots), BF),
            jax.ShapeDtypeStruct((slots, width), BF),
            jax.ShapeDtypeStruct((rows, LANES), F32),
            jax.ShapeDtypeStruct((8, tables.shape[1]), F32),
            jax.ShapeDtypeStruct((8, tables.shape[1]), F32),
            jax.ShapeDtypeStruct((LANES, width), BF),
        ],
        in_specs=[VMEM] * 5,
        out_specs=[VMEM] * 7,
        compiler_params=params(60),
        cost_estimate=cost(5e+10, 1e4),
    )(chosen, cot, tables, bias, router)


def mix_kernel(parts, experts, *refs):
    hidden_ref = refs[0]
    ctx_refs, weight_refs = refs[1 : 1 + parts], refs[1 + parts : 1 + 2 * parts]
    gain_ref, router_ref, chosen_ref, pack_ref, sum_ref, gate_ref, packed_ref = refs[
        1 + 2 * parts :
    ]
    first_sum = hidden_ref[...].astype(F32)
    for part in range(parts):
        first_sum = first_sum + dot_nn(ctx_refs[part][...], weight_refs[part][...])
    sum_ref[...] = first_sum
    normed = (first_sum * rms_scale(first_sum) * gain_ref[...]).astype(BF)
    packed_ref[...] = dot_nn(pack_ref[...], normed).astype(BF)
    lane = lax.broadcasted_iota(jnp.int32, gate_ref.shape, 1)
    logits = jnp.where(lane < experts, dot_nt(normed, router_ref[...]), F32(NEG))
    logits = jnp.exp(logits - jnp.max(logits, axis=1, keepdims=True))
    gate = jnp.sum(chosen_ref[...] * logits, axis=1, keepdims=True) / jnp.sum(logits, axis=1, keepdims=True)
    gate_ref[...] = jnp.broadcast_to(gate, gate_ref.shape)


def mix(hidden, ctxs, weights, gain, router, chosen, hot, experts):
    parts = len(weights)
    rows, width = hidden.shape
    return pl.pallas_call(
        functools.partial(mix_kernel, parts, experts),
        out_shape=[
            jax.ShapeDtypeStruct((rows, width), F32),
            jax.ShapeDtypeStruct((rows, LANES), F32),
            jax.ShapeDtypeStruct((hot.shape[0], width), BF),
        ],
        in_specs=[VMEM] * (2 * parts + 5),
        out_specs=[VMEM] * 3,
        compiler_params=params(60),
        cost_estimate=cost(5e+10, 1e4),
    )(hidden, *ctxs, *weights, gain, router, chosen, hot)


def in_map_units(order):
    return [(unit, (at, row)) for at, group in enumerate(order) for row, unit in enumerate(group)]


def expert_kernel(in_map, out_map, experts, where_ref, *refs):
    row_ref, cot_ref, router_ref = refs[:3]
    in_refs, in_at = refs[3 : 3 + len(in_map)], dict(in_map_units(in_map))
    out_refs, out_at = refs[3 + len(in_map) : 3 + len(in_map) + len(out_map)], dict(in_map_units(out_map))
    back_ref, out_ref, gated_ref, near_ref, far_ref, logit_ref = refs[
        3 + len(in_map) + len(out_map) :
    ]
    name = where_ref[3]
    slots, width = row_ref.shape
    units = len(in_at)
    span = in_refs[0].shape[1]
    step_rows = 256

    def step(index, carry):
        rows_at = pl.ds(pl.multiple_of(index * step_rows, step_rows), step_rows)
        rows = row_ref[rows_at, :]
        lane = lax.broadcasted_iota(jnp.int32, (step_rows, LANES), 1)
        logits = jnp.where(lane < experts, dot_nt(rows, router_ref[...]), F32(NEG))
        logits = jnp.exp(logits - jnp.max(logits, axis=1, keepdims=True))
        router = logits / jnp.sum(logits, axis=1, keepdims=True)
        hot = (lane == name).astype(F32)
        gate = jnp.sum(router * hot, axis=1, keepdims=True)
        cot = cot_ref[rows_at, :].astype(F32)
        gated = (cot * gate).astype(BF)
        total = jnp.zeros((step_rows, width), F32)
        back = jnp.zeros((step_rows, width), F32)
        for unit in range(units):
            at, row = in_at[unit]
            inward = in_refs[at].at[row * width : (row + 1) * width, :]
            at, row = out_at[unit]
            outward = out_refs[at].at[row * span : (row + 1) * span, :]
            pre_act = dot_nn(rows, inward[...])
            below = 0.5 + 0.5 * lax.erf(pre_act * F32(SQRT_HALF))
            active = (pre_act * below).astype(BF)
            slope = below + pre_act * jnp.exp(pre_act * pre_act * F32(-0.5)) * F32(INV_SQRT_TWO_PI)
            hidden = (dot_nt(gated, outward[...]) * slope).astype(BF)
            side_ref = near_ref if unit < units // 2 else far_ref
            first = (unit % (units // 2)) * span
            side_ref[rows_at, first : first + span] = active
            first = first + units // 2 * span
            side_ref[rows_at, first : first + span] = hidden
            total = total + dot_nn(active, outward[...])
            back = back + dot_nt(hidden, inward[...])
        gate_grad = jnp.sum(cot * total, axis=1, keepdims=True)
        logit_grad = ((gate_grad * gate) * (hot - router)).astype(BF)
        back = back + dot_nn(logit_grad, router_ref[...])
        gated_ref[rows_at, :] = gated
        far_ref[rows_at, units * span :] = gated
        logit_ref[rows_at, :] = logit_grad
        out_ref[rows_at, :] = total.astype(BF)
        back_ref[rows_at, :] = back.astype(BF)
        return carry

    lax.fori_loop(0, slots // step_rows, step, 0)


def run_expert(where, rows, cots, in_parts, out_parts, in_map, out_map, router, experts):
    slots, width = rows.shape
    hidden = sum(len(group) for group in in_map) * in_parts[0].shape[1]
    return pl.pallas_call(
        functools.partial(expert_kernel, in_map, out_map, experts),
        out_shape=[
            jax.ShapeDtypeStruct((slots, width), BF),
            jax.ShapeDtypeStruct((slots, width), BF),
            jax.ShapeDtypeStruct((slots, width), BF),
            jax.ShapeDtypeStruct((slots, hidden), BF),
            jax.ShapeDtypeStruct((slots, hidden + width), BF),
            jax.ShapeDtypeStruct((slots, LANES), BF),
        ],
        in_specs=[SMEM] + [VMEM] * (len(in_parts) + len(out_parts) + 3),
        out_specs=[VMEM] * 6,
        compiler_params=params(60),
        cost_estimate=cost(5e+10, 1e4),
    )(where, rows, cots, router, *in_parts, *out_parts)


def weight_kernel(parts, where_ref, *refs):
    row_ref, peer_ref, gated_ref, near_ref, got_ref, keep_ref = refs
    place = where_ref[0]
    span = keep_ref.shape[2] // 2
    hidden = parts * span
    rows, rows_peer = jnp.transpose(row_ref[...]), jnp.transpose(peer_ref[...])
    gated, gated_peer = jnp.transpose(gated_ref[...]), jnp.transpose(got_ref[:, 2 * hidden :])
    for part in range(parts):
        at = slice(part * span, (part + 1) * span)
        outward = dot_nn(gated, near_ref[:, at]) + dot_nn(gated_peer, got_ref[:, at])
        keep_ref[place ^ part, :, span:] = outward.astype(BF)
        at = slice(hidden + part * span, hidden + (part + 1) * span)
        inward = dot_nn(rows, near_ref[:, at]) + dot_nn(rows_peer, got_ref[:, at])
        keep_ref[place ^ part, :, 0:span] = inward.astype(BF)


def weight_grads(where, rows, rows_peer, gated, near, got, parts):
    slots, width = rows.shape
    span = near.shape[1] // (2 * parts)
    return pl.pallas_call(
        functools.partial(weight_kernel, parts),
        out_shape=jax.ShapeDtypeStruct((parts, width, 2 * span), BF),
        in_specs=[SMEM] + [VMEM] * 5,
        out_specs=VMEM,
        compiler_params=params(32),
        cost_estimate=cost(1e+10, 1e4),
    )(where, rows, rows_peer, gated, near, got)


def finish_kernel(where_ref, mine_ref, peer_ref, in_ref, out_ref):
    core = where_ref[2]
    span = mine_ref.shape[1] // 2
    for ref, side in ((mine_ref, core), (peer_ref, 1 - core)):
        at = pl.ds(pl.multiple_of(side * span, LANES), span)
        in_ref[:, at] = ref[:, 0:span].astype(F32)
        out_ref[at, :] = jnp.transpose(ref[:, span:].astype(F32))


def finish(where, mine, peer):
    width, both = mine.shape
    return pl.pallas_call(
        finish_kernel,
        out_shape=[
            jax.ShapeDtypeStruct((width, both), F32),
            jax.ShapeDtypeStruct((both, width), F32),
        ],
        in_specs=[SMEM, VMEM, VMEM],
        out_specs=[VMEM, VMEM],
        compiler_params=params(24),
        cost_estimate=cost(5e+10, 1e4),
    )(where, mine, peer)


def residual_kernel(parts, where_ref, *refs):
    home_ref, hot_ref, sum_ref, cot_ref, gain_ref = refs[:5]
    weight_refs, old_refs = refs[5 : 5 + parts], refs[5 + parts : 5 + 2 * parts]
    grad_ref, gain_out_ref, keep_ref, give_ref, *ctx_refs = refs[5 + 2 * parts :]
    core = where_ref[2]
    side = grad_ref.shape[1] // 2
    upstream = dot_nn(hot_ref[...], home_ref[...])
    first_sum = sum_ref[...]
    inverse = rms_scale(first_sum)
    gain_out_ref[...] = jnp.broadcast_to(
        jnp.sum(upstream * first_sum * inverse, axis=0, keepdims=True), gain_out_ref.shape
    )
    grad = cot_ref[...].astype(F32) + norm_back(first_sum, inverse, gain_ref[...], upstream)
    grad_ref[...] = grad
    low = grad.astype(BF)
    for part in range(parts):
        ctx_refs[part][...] = dot_nt(low, weight_refs[part][...]).astype(BF)
    for part in range(parts):
        product = dot_tn(old_refs[part][...], low)

        @pl.when(core == 0)
        def _(product=product, part=part):
            keep_ref[part] = product[:, :side]
            give_ref[part] = product[:, side:].astype(BF)

        @pl.when(core != 0)
        def _(product=product, part=part):
            keep_ref[part] = product[:, side:]
            give_ref[part] = product[:, :side].astype(BF)


def residual(where, home, hot, first_sum, cot, gain, weights, ctxs):
    parts = len(weights)
    rows, width = first_sum.shape
    inner = weights[0].shape[0]
    return pl.pallas_call(
        functools.partial(residual_kernel, parts),
        out_shape=[
            jax.ShapeDtypeStruct((rows, width), F32),
            jax.ShapeDtypeStruct((8, width), F32),
            jax.ShapeDtypeStruct((parts, inner, width // 2), F32),
            jax.ShapeDtypeStruct((parts, inner, width // 2), BF),
        ]
        + [jax.ShapeDtypeStruct((rows, inner), BF)] * parts,
        in_specs=[SMEM] + [VMEM] * (2 * parts + 5),
        out_specs=[VMEM] * (4 + parts),
        compiler_params=params(60),
        cost_estimate=cost(2e+11, 1e4),
    )(where, home, hot, first_sum, cot, gain, *weights, *ctxs)


def attend_back_kernel(parts, heads, where_ref, *refs):
    cot_refs, refs = refs[:parts], refs[parts:]
    ctx_ref, proj_ref, normed_ref, lse_ref, weight_ref, offset_ref = refs[:6]
    scale_ref, small_ref, table_ref = refs[6:9]
    send_ref, bias_ref, keep_ref, give_ref = refs[9:13]
    skew_ref, fold_ref, cot_ref, dproj_ref, key_acc, value_acc = refs[13:]
    quarter = ctx_ref.shape[1]
    for part in range(parts):
        cot_ref[where_ref[0] ^ part] = cot_refs[part][...]
    length = quarter * parts
    inner = weight_ref.shape[0] // 3
    head_dim = inner // heads
    prefix, core = where_ref[1], where_ref[2]
    skew_into(skew_ref, offset_ref, heads, 2 * length)
    fold_ref[...] = jnp.zeros_like(fold_ref)
    key_acc[...] = jnp.zeros_like(key_acc)
    value_acc[...] = jnp.zeros_like(value_acc)
    keys_across = jnp.transpose(proj_ref[:, inner : 2 * inner])
    head_row = lax.broadcasted_iota(jnp.int32, (8, inner), 0)
    head_lane = lax.broadcasted_iota(jnp.int32, (8, inner), 1)
    picks = (head_lane // head_dim == head_row).astype(BF)
    for block in range(parts):
        first = block * quarter
        reach = max(length // 2, first + quarter)
        key_pos = first + lax.broadcasted_iota(jnp.int32, (reach - first, quarter), 0)
        query_pos = first + lax.broadcasted_iota(jnp.int32, (reach - first, quarter), 1)
        allowed = (key_pos <= query_pos) | (key_pos < prefix)
        product = cot_ref[block].astype(F32) * ctx_ref[block].astype(F32)
        high = product.astype(BF)
        rest = (product - high.astype(F32)).astype(BF)
        inner_sum = dot_nt(picks, high) + dot_nt(picks, rest)
        query_pieces = []
        for head in range(heads):
            low = head * head_dim
            query = proj_ref[first : first + quarter, low : low + head_dim]
            keys = proj_ref[0:reach, inner + low : inner + low + head_dim]
            values = proj_ref[0:reach, 2 * inner + low : 2 * inner + low + head_dim]
            grad = cot_ref[block, :, low : low + head_dim]
            bias = jnp.concatenate(
                [
                    skew_ref[
                        head,
                        :,
                        first - LANES * sub + length - LANES : first
                        - LANES * sub
                        + length
                        - LANES
                        + quarter,
                    ]
                    for sub in range(reach // LANES)
                ],
                axis=0,
            )
            scores = dot_nt(keys, query) + bias
            tail = jnp.where(allowed, scores[first:], F32(NEG))
            scores = jnp.concatenate([scores[:first], tail], axis=0) if first else tail
            probs = jnp.exp(scores - lse_ref[block, head : head + 1, :])
            prob_grad = dot_nt(values, grad)
            score_grad = (probs * (prob_grad - inner_sum[head : head + 1, :])).astype(BF)
            wide = score_grad.astype(F32)
            for sub in range(reach // LANES):
                column = first - LANES * sub + length - LANES
                fold_ref[head, :, column : column + quarter] += wide[
                    LANES * sub : LANES * (sub + 1)
                ]
            value_acc[head, 0:reach, :] += dot_nn(probs.astype(BF), grad)
            key_acc[head, 0:reach, :] += dot_nn(score_grad, query)
            query_pieces.append(dot_nn(keys_across[low : low + head_dim, 0:reach], score_grad))
        query_grad = jnp.transpose(jnp.concatenate(query_pieces, axis=0)) * F32(head_dim ** (-0.5))
        dproj_ref[first : first + quarter, 0:inner] = query_grad.astype(BF)
    dproj_ref[:, inner : 3 * inner] = jnp.concatenate(
        [key_acc[head] for head in range(heads)] + [value_acc[head] for head in range(heads)],
        axis=1,
    ).astype(BF)
    width = normed_ref.shape[1]
    side = width // 2
    split, piece, _ = keep_ref.shape
    layer = where_ref[3]
    for half in range(2):
        grad_rows = dot_tn(dproj_ref[...], normed_ref[:, half * side : (half + 1) * side])
        for part in range(split):
            chunk = grad_rows[part * piece : (part + 1) * piece]
            slot = (layer ^ part) if split > 1 else part

            @pl.when(core == half)
            def _(chunk=chunk, slot=slot):
                keep_ref[slot] = chunk

            @pl.when(core != half)
            def _(chunk=chunk, slot=slot):
                give_ref[slot] = chunk.astype(BF)

    gain_sum = jnp.zeros((1, width), F32)
    for block in range(parts):
        rows = slice(block * quarter, (block + 1) * quarter)
        upstream = dot_nn(dproj_ref[rows, :], weight_ref[...])
        gain_sum = gain_sum + jnp.sum(
            upstream * normed_ref[rows, :].astype(F32), axis=0, keepdims=True
        )
        send_ref[block, 0:quarter, :] = upstream.astype(BF)
    extra = small_ref.shape[0]
    row = lax.broadcasted_iota(jnp.int32, small_ref.shape, 0)
    small = jnp.where(row == 0, gain_sum / scale_ref[...], small_ref[...]).astype(BF)
    share = width // parts
    for block in range(parts):
        send_ref[block, quarter:, 0:share] = small[:, block * share : (block + 1) * share]
        send_ref[block, quarter:, share:] = jnp.zeros((extra, width - share), BF)
    row_index = lax.broadcasted_iota(jnp.int32, (LANES, 2 * length), 0)
    buckets = (row_index == table_ref[1:2, :]).astype(BF)
    for head in range(heads):
        tile = fold_ref[head]
        for bit in range(7):
            moved = pltpu.roll(tile, 2 * length - (1 << bit), 1)
            tile = jnp.where(((row_index >> bit) & 1) == 1, moved, tile)
        tile = pltpu.roll(tile, LANES - 1, 1)
        rest = jnp.broadcast_to(jnp.sum(tile, axis=0, keepdims=True), (8, 2 * length))
        total = jnp.zeros((8, LANES), F32)
        for _ in range(3):
            high = rest.astype(BF)
            rest = rest - high.astype(F32)
            total = total + dot_nt(high, buckets)
        bias_ref[head : head + 1, :] = total[0:1]
    bias_ref[heads:, :] = jnp.zeros((bias_ref.shape[0] - heads, LANES), F32)


def attend_back(
    where, cots, ctxs, proj, normed, lse, weight, offsets, scale, small, tables, heads, split
):
    parts, quarter, inner = ctxs.shape
    width = normed.shape[1]
    length = parts * quarter
    return pl.pallas_call(
        functools.partial(attend_back_kernel, parts, heads),
        out_shape=[
            jax.ShapeDtypeStruct((parts, quarter + small.shape[0], width), BF),
            jax.ShapeDtypeStruct((small.shape[0], LANES), F32),
            jax.ShapeDtypeStruct((split, 3 * inner // split, width // 2), F32),
            jax.ShapeDtypeStruct((split, 3 * inner // split, width // 2), BF),
        ],
        in_specs=[SMEM] + [VMEM] * (9 + parts),
        out_specs=[VMEM] * 4,
        scratch_shapes=[
            pltpu.VMEM((heads, LANES, 2 * length), F32),
            pltpu.VMEM((heads, LANES, 2 * length), F32),
            pltpu.VMEM((parts, quarter, inner), BF),
            pltpu.VMEM((length, 3 * inner), BF),
            pltpu.VMEM((heads, length, inner // heads), F32),
            pltpu.VMEM((heads, length, inner // heads), F32),
        ],
        compiler_params=params(60),
        cost_estimate=cost(5e+10, 1e4),
    )(where, *cots, ctxs, proj, normed, lse, weight, offsets, scale, small, tables)


def merge_kernel(parts, where_ref, keep_ref, got_ref, *refs):
    wo_refs, send_refs, wo_ref = refs[:parts], refs[parts:-1], refs[-1]
    split, piece, side = keep_ref.shape
    share = wo_ref.shape[0] // split
    layer = where_ref[3]
    total = wo_refs[0][...]
    for part in range(1, parts):
        total = total + wo_refs[part][...].astype(F32)
    wo_ref[...] = total
    for part in range(split):
        send_refs[part][0:piece, :] = (keep_ref[part] + got_ref[part].astype(F32)).astype(BF)
        row = (layer ^ part) * share if split > 1 else 0
        send_refs[part][piece:, :] = wo_ref[pl.ds(pl.multiple_of(row, 8), share), :].astype(BF)


def merge(where, keep, got, wos):
    split, piece, side = keep.shape
    rows = wos[0].shape[0]
    shape = jax.ShapeDtypeStruct((piece + rows // split, side), BF)
    return pl.pallas_call(
        functools.partial(merge_kernel, len(wos)),
        out_shape=[shape] * split,
        in_specs=[SMEM] + [VMEM] * (2 + len(wos)),
        out_specs=[VMEM] * split,
        scratch_shapes=[pltpu.VMEM((rows, side), F32)],
        compiler_params=params(16),
        cost_estimate=cost(1e+06, 1e4),
    )(where, keep, got, *wos)


def assemble_kernel(where_ref, *refs):
    *piece_refs, qkv_ref, wo_ref, first_ref, second_ref, router_ref, bias_ref, parts_ref = refs
    split = len(piece_refs) // 2
    side = qkv_ref.shape[1] // 2
    piece, share = qkv_ref.shape[0] // split, wo_ref.shape[0] // split
    core, layer = where_ref[2], where_ref[3]
    for part in range(split):
        slot = (layer ^ part) if split > 1 else 0
        for half in range(2):
            ref = piece_refs[half * split + part]
            at = pl.ds(pl.multiple_of((core ^ half) * side, LANES), side)
            values = ref[...].astype(F32)
            qkv_ref[pl.ds(pl.multiple_of(slot * piece, 8), piece), at] = values[0:piece]
            wo_ref[pl.ds(pl.multiple_of(slot * share, 8), share), at] = values[
                piece : piece + share
            ]
            parts_ref[(core ^ half) * split + slot] = values[piece + share :]
    total = parts_ref[0]
    for part in range(1, 2 * split):
        total = total + parts_ref[part]
    share = first_ref.shape[1]
    first_ref[...] = total[0:1, 0:share]
    second_ref[...] = total[1:2, 0:share]
    router_ref[...] = total[2 : 2 + router_ref.shape[0], 0:share]
    bias_ref[...] = total[0 : bias_ref.shape[0], share : share + bias_ref.shape[1]]


def assemble(where, pieces, rows, extra, width, experts, heads, buckets):
    split = len(pieces) // 2
    both, side = pieces[0].shape
    return pl.pallas_call(
        assemble_kernel,
        out_shape=[
            jax.ShapeDtypeStruct((rows, 2 * side), F32),
            jax.ShapeDtypeStruct((split * (both - extra) - rows, 2 * side), F32),
            jax.ShapeDtypeStruct((1, width), F32),
            jax.ShapeDtypeStruct((1, width), F32),
            jax.ShapeDtypeStruct((experts, width), F32),
            jax.ShapeDtypeStruct((heads, buckets), F32),
        ],
        in_specs=[SMEM] + [VMEM] * (2 * split),
        out_specs=[VMEM] * 6,
        scratch_shapes=[pltpu.VMEM((2 * split, extra, side), F32)],
        compiler_params=params(16),
        cost_estimate=cost(1e+06, 1e4),
    )(where, *pieces)


def trade(values, axis):
    return lax.all_to_all(values, axis, split_axis=0, concat_axis=0, tiled=True)


def after(values, others):
    return lax.optimization_barrier((values, others))[0]


def body(
    hidden_in,
    cotangent,
    attn_gain,
    query_key_value_weight,
    attention_output_weight,
    rel_bias,
    bucket_table,
    prefix_len,
    moe_gain,
    w_router,
    routes,
    w_expert_in,
    w_expert_out,
):
    seq_count, quarter, model_width = hidden_in.shape
    parts = lax.axis_size("tensor")
    layers = lax.axis_size("expert")
    row_count = seq_count * quarter
    experts = w_router.shape[1]
    capacity = max(2, 2 * row_count // experts)
    slot_count = experts * capacity
    heads, buckets = rel_bias.shape
    inner = query_key_value_weight.shape[2]
    span = w_expert_in.shape[2] // 2
    place, layer, core = lax.axis_index("tensor"), lax.axis_index("expert"), lax.axis_index("dp")
    where = jnp.stack([place, prefix_len[0], core, layer]).astype(jnp.int32)
    low_core = core == 0

    own_hidden = hidden_in[0]
    own_cot = cotangent[0]

    chosen = routes.reshape(1, row_count)
    tables = jnp.stack([bucket_table, jnp.flip(bucket_table)])
    tables = jnp.pad(tables, ((0, 0), (0, 1)), constant_values=-1)
    gains = jnp.stack([attn_gain, moe_gain]).astype(F32)
    pack_hot, unpack_hot, cot_packed, chosen_hot, offset_bias, offset_back, router = prepare(
        chosen, own_cot, tables, rel_bias, w_router.T, capacity
    )

    def over_experts(packed):
        packed = packed.reshape(experts, capacity, model_width)
        return trade(packed, "expert").reshape(slot_count, model_width)

    cot_slots = over_experts(cot_packed)

    hidden_blocks = [own_hidden] + [swap(own_hidden, "tensor", k) for k in range(1, parts)]
    weight = query_key_value_weight.transpose(1, 2, 0).reshape(3 * inner, model_width)
    late_weight = after(attention_output_weight, hidden_blocks)
    out_weights = [attention_output_weight] + [
        swap(late_weight if k == parts - 1 else attention_output_weight, "tensor", k)
        for k in range(1, parts)
    ]
    early_weights = out_weights[:-1]
    first_blocks, prepared = lax.optimization_barrier(
        (hidden_blocks, (early_weights, pack_hot, unpack_hot, chosen_hot, router, offset_bias,
                         offset_back, where, gains))
    )
    early_weights, pack_hot, unpack_hot, chosen_hot, router, offset_bias, offset_back, where, gains = (
        prepared
    )
    attn_scale, moe_scale = gains[0:1], gains[1:2]
    normed_one, projected, lse, contexts, sends = attend(
        where, first_blocks, attn_scale, weight, offset_bias, heads
    )

    in_own = lax.dynamic_slice(w_expert_in[0], (0, core * span), (model_width, span))
    out_own = lax.dynamic_slice(w_expert_out[0], (core * span, 0), (span, model_width))
    in_other = lax.dynamic_slice(w_expert_in[0], (0, (1 - core) * span), (model_width, span))
    out_other = lax.dynamic_slice(w_expert_out[0], ((1 - core) * span, 0), (span, model_width))
    in_own, out_own = after((in_own, out_own), hidden_blocks)
    in_step, out_step = swap(in_own, "tensor", 1), swap(out_own, "tensor", 2)
    out_weights = early_weights + out_weights[-1:]
    sends = after(sends, (in_step, out_step, out_weights[-1]))
    own_contexts = [sends[0]] + [swap(sends[k], "tensor", k) for k in range(1, parts)]


    in_step, out_step = after((in_step, out_step), own_contexts)
    in_both = jnp.concatenate([in_own, in_step], axis=0)
    out_both = jnp.concatenate([out_own, out_step], axis=0)
    own_contexts, (in_both, out_both) = lax.optimization_barrier((own_contexts, (in_both, out_both)))
    in_near = [in_own, in_step, swap(in_both, "tensor", 2)]
    out_near = [out_own, out_step, swap(out_both, "tensor", 1)]
    in_order, out_order = ((0,), (1,), (2, 3)), ((0,), (2,), (1, 3))
    in_map = in_order + tuple(tuple(parts + unit for unit in group) for group in in_order)
    out_map = out_order + tuple(tuple(parts + unit for unit in group) for group in out_order)

    first_sum, gate, packed = mix(
        own_hidden, after(own_contexts, cot_slots), out_weights, moe_scale, router,
        chosen_hot, pack_hot, experts,
    )
    row_slots = over_experts(packed)

    def cross(pieces):
        _, near, far = pieces
        return [swap(near, "dp", 1), swap(after(far, row_slots), "dp", 1)]

    in_parts = in_near + [in_other] + cross(in_near)
    out_parts = out_near + [out_other] + cross(out_near)
    rows_peer = swap(row_slots, "dp", 1)
    back_slots, out_slots, gated, near, far, logit_grad = run_expert(
        where, row_slots, cot_slots, in_parts, out_parts, in_map, out_map, router, experts
    )
    back_home = over_experts(back_slots)

    partial = weight_grads(where, row_slots, rows_peer, gated, near, swap(far, "dp", 1), parts)
    mine = lax.psum_scatter(partial, "tensor", scatter_dimension=0, tiled=True)[0]
    expert_in_grad, expert_out_grad = finish(where, mine, swap(mine, "dp", 1))

    residual_grad, moe_gain_part, wo_keep, wo_give, *cots = residual(
        where, after(back_home, partial), unpack_hot, first_sum, own_cot, moe_scale, out_weights,
        own_contexts,
    )
    context_cots = [cots[0]] + [swap(cots[k], "tensor", k) for k in range(1, parts)]
    out_slots = after(out_slots, context_cots[1])
    out_home = over_experts(out_slots)

    side = model_width // 2
    wo_keep = wo_keep + swap(wo_give, "dp", 1).astype(F32)
    wo_low = wo_keep.astype(BF)
    context_cots = after(context_cots, wo_low)

    wo_parts = [wo_keep[0]] + [swap(wo_low[k], "tensor", k) for k in range(1, parts)]

    split = layers if layers == 4 else 1
    router_part = dot_tn(logit_grad, row_slots)[:experts]
    extra = -(-(experts + 2) // 16) * 16
    small = jnp.concatenate([moe_gain_part[:1], router_part], axis=0)
    small = jnp.pad(small, ((1, extra - 2 - experts), (0, 0)))
    send_ups, bias_part, keep, give = attend_back(
        where, context_cots, contexts, projected, normed_one, lse, weight, offset_back,
        attn_scale, small, tables, heads, split,
    )
    send_ups, give = after((send_ups, give), (wo_parts, out_home))
    ups = jnp.sum(trade(send_ups, "tensor").astype(F32), axis=0)
    own_float = own_hidden.astype(F32)
    inverse_own = rms_scale(own_float)
    input_grad = residual_grad + norm_back(own_float, inverse_own, attn_scale, ups[:quarter])

    share = model_width // parts
    bias_part = jnp.pad(bias_part, ((0, 0), (0, side - share - LANES)))
    small = jnp.concatenate([ups[quarter:, :share], bias_part], axis=1)
    sends = merge(where, keep, swap(give, "dp", 1), wo_parts)
    piece = sends[0].astype(F32)
    if split > 1:
        for k in range(1, layers):
            piece = piece + swap(sends[k], "expert", k).astype(F32)
        piece = jnp.concatenate([piece, small], axis=0).astype(BF)
        pieces = [piece] + [swap(piece, "expert", k) for k in range(1, layers)]
    else:
        pieces = [lax.psum(jnp.concatenate([piece, small], axis=0), "expert")]
    pieces = pieces + [swap(x, "dp", 1) for x in pieces]
    expert_out = dot_nn(unpack_hot, after(out_home, piece))
    layer_out = (first_sum + gate[:, :1] * expert_out).astype(BF)

    done = (layer_out, expert_in_grad, expert_out_grad, input_grad)
    pieces, done = lax.optimization_barrier((pieces, done))
    layer_out, expert_in_grad, expert_out_grad, input_grad = done
    qkv_across, attn_out_grad, gain_one, gain_two, router_grad, bias_grad = assemble(
        where, pieces, 3 * inner, extra, share, experts, heads, buckets
    )
    qkv_grad = qkv_across.reshape(3, inner, model_width).transpose(2, 0, 1)
    return (
        layer_out.reshape(seq_count, quarter, model_width),
        input_grad.reshape(seq_count, quarter, model_width),
        gain_one[0],
        qkv_grad,
        attn_out_grad,
        bias_grad,
        gain_two[0],
        router_grad.T,
        expert_in_grad[None],
        expert_out_grad[None],
    )


def solution(mesh):
    placed = (
        P(("dp", "expert"), "tensor", None),
        P(("dp", "expert"), "tensor", None),
        P(),
        P(None, None, "tensor"),
        P("tensor", None),
        P("tensor", None),
        P(),
        P(("dp", "expert")),
        P(),
        P(),
        P(("dp", "expert"), "tensor", None, None, None),
        P("expert", None, "tensor"),
        P("expert", "tensor", None),
    )
    return jax.shard_map(
        body,
        mesh=mesh,
        in_specs=placed,
        out_specs=(
            P(("dp", "expert"), "tensor", None),
            P(("dp", "expert"), "tensor", None),
            P("tensor"),
            P(None, None, "tensor"),
            P("tensor", None),
            P("tensor", None),
            P("tensor"),
            P("tensor", None),
            P("expert", None, "tensor"),
            P("expert", "tensor", None),
        ),
        check_vma=False,
    )
```

```python
import functools

import jax
import jax.numpy as jnp
from jax import lax
from jax.experimental import pallas as pl
from jax.experimental.pallas import tpu as pltpu
from jax.sharding import PartitionSpec as P

EPSILON = 1e-06
NEG = -1e30
TOP_PRECISION = lax.Precision.HIGHEST
BF = jnp.bfloat16
F32 = jnp.float32
LANES = 128
VMEM = pl.BlockSpec()
ANY = pl.BlockSpec(memory_space=pl.ANY)
SMEM = pl.BlockSpec(memory_space=pltpu.SMEM)
SQRT_HALF = 0.7071067811865476
INV_SQRT_TWO_PI = 0.3989422804014327


def params(mib):
    return pltpu.CompilerParams(vmem_limit_bytes=mib * 1024 * 1024)


def cost(flops, moved):
    return pl.CostEstimate(flops=int(flops), bytes_accessed=int(moved), transcendentals=0)


def dot_nn(a, b):
    return lax.dot_general(a, b, (((1,), (0,)), ((), ())), preferred_element_type=F32)


def dot_nt(a, b):
    return lax.dot_general(a, b, (((1,), (1,)), ((), ())), preferred_element_type=F32)


def dot_tn(a, b):
    return lax.dot_general(a, b, (((0,), (0,)), ((), ())), preferred_element_type=F32)


def rms_scale(values):
    return lax.rsqrt(jnp.mean(values * values, axis=-1, keepdims=True) + EPSILON)


def norm_back(values, inverse, gain_vec, upstream):
    scaled = upstream * gain_vec
    return inverse * scaled - values * (inverse * inverse * inverse) * jnp.mean(
        scaled * values, axis=-1, keepdims=True
    )


def swap(values, axis, step):
    count = lax.axis_size(axis)
    return lax.ppermute(values, axis, [(i, i ^ step) for i in range(count)])


def skew_into(skew_ref, offset_ref, heads, width):
    for head in range(heads):
        row = jnp.broadcast_to(offset_ref[head : head + 1, :], (LANES, width))
        skew_ref[head] = pltpu.roll(row, width - (LANES - 1), 1, stride=1, stride_axis=0)


def attend_kernel(parts, heads, where_ref, *refs):
    x_refs = refs[:parts]
    gain_ref, weight_ref, offset_ref = refs[parts : parts + 3]
    normed_ref, proj_ref, lse_ref, ctx_ref = refs[parts + 3 : parts + 7]
    send_refs, skew_ref = refs[parts + 7 : 2 * parts + 7], refs[2 * parts + 7]
    quarter = x_refs[0].shape[0]
    length = quarter * parts
    inner = weight_ref.shape[0] // 3
    head_dim = inner // heads
    place, prefix = where_ref[0], where_ref[1]
    lane = lax.broadcasted_iota(jnp.int32, (1, 3 * inner), 1)
    column_scale = jnp.where(lane < inner, F32(head_dim ** (-0.5)), F32(1.0))
    for part in range(parts):
        x = x_refs[part][...].astype(F32)
        normed = (x * rms_scale(x) * gain_ref[0:1, :]).astype(BF)
        rows = pl.ds(pl.multiple_of((place ^ part) * quarter, quarter), quarter)
        normed_ref[rows, :] = normed
        proj_ref[rows, :] = (dot_nt(normed, weight_ref[...]) * column_scale).astype(BF)
    skew_into(skew_ref, offset_ref, heads, 2 * length)
    tiles = length // LANES
    per_block = quarter // LANES
    for block in range(parts):
        first = block * quarter
        reach = max(length // 2, first + quarter)
        key_pos = first + lax.broadcasted_iota(jnp.int32, (quarter, reach - first), 1)
        query_pos = first + lax.broadcasted_iota(jnp.int32, (quarter, reach - first), 0)
        allowed = (key_pos <= query_pos) | (key_pos < prefix)
        pieces, logs = [], []
        for head in range(heads):
            low = head * head_dim
            query = proj_ref[first : first + quarter, low : low + head_dim]
            keys = proj_ref[0:reach, inner + low : inner + low + head_dim]
            values = proj_ref[0:reach, 2 * inner + low : 2 * inner + low + head_dim]
            bias = jnp.concatenate(
                [
                    skew_ref[
                        head,
                        :,
                        LANES * (tiles - 1 - block * per_block - sub) : LANES
                        * (tiles - 1 - block * per_block - sub)
                        + reach,
                    ]
                    for sub in range(per_block)
                ],
                axis=0,
            )
            scores = dot_nt(query, keys) + bias
            tail = jnp.where(allowed, scores[:, first:], F32(NEG))
            scores = jnp.concatenate([scores[:, :first], tail], axis=1) if first else tail
            peak = jnp.max(scores, axis=1, keepdims=True)
            exponent = jnp.exp(scores - peak)
            total = jnp.sum(exponent, axis=1, keepdims=True)
            pieces.append(dot_nn(exponent.astype(BF), values) / total)
            logs.append(jnp.broadcast_to(peak + jnp.log(total), (quarter, LANES)))
        ctx_ref[block] = jnp.concatenate(pieces, axis=1).astype(BF)
        lane_row = lax.broadcasted_iota(jnp.int32, (quarter, LANES), 1)
        stacked = logs[0]
        for head in range(1, heads):
            stacked = jnp.where(lane_row == head, logs[head], stacked)
        lse_ref[block] = jnp.transpose(stacked)[0:8, :]
    for part in range(parts):
        send_refs[part][...] = ctx_ref[place ^ part]


def attend(where, blocks, gain, weight, offsets, heads):
    parts = len(blocks)
    quarter, width = blocks[0].shape
    length = parts * quarter
    inner3 = weight.shape[0]
    outs = pl.pallas_call(
        functools.partial(attend_kernel, parts, heads),
        out_shape=[
            jax.ShapeDtypeStruct((length, width), BF),
            jax.ShapeDtypeStruct((length, inner3), BF),
            jax.ShapeDtypeStruct((parts, 8, quarter), F32),
            jax.ShapeDtypeStruct((parts, quarter, inner3 // 3), BF),
        ]
        + [jax.ShapeDtypeStruct((quarter, inner3 // 3), BF)] * parts,
        in_specs=[SMEM] + [VMEM] * (parts + 3),
        out_specs=[VMEM] * (4 + parts),
        scratch_shapes=[pltpu.VMEM((heads, LANES, 2 * length), F32)],
        compiler_params=params(60),
        cost_estimate=cost(5e+10, 1e4),
    )(where, *blocks, gain, weight, offsets)
    return outs[0], outs[1], outs[2], outs[3], outs[4:]


def prepare_kernel(experts, capacity, chosen_ref, cot_ref, table_ref, bias_ref, router_in_ref, *outs):
    pack_ref, unpack_ref, packed_ref, hot_ref, offset_ref, back_ref, router_ref = outs
    slots, rows = pack_ref.shape
    chosen = chosen_ref[...]
    hot = (lax.broadcasted_iota(jnp.int32, (LANES, rows), 0) == chosen).astype(F32)
    earlier = lax.broadcasted_iota(jnp.int32, (rows, rows), 0)
    later = lax.broadcasted_iota(jnp.int32, (rows, rows), 1)
    before = dot_nn(hot.astype(BF), (earlier < later).astype(BF))
    slot = jnp.sum(before * hot, axis=0, keepdims=True)
    target = chosen * capacity + slot.astype(jnp.int32)
    pack = (lax.broadcasted_iota(jnp.int32, (slots, rows), 0) == target).astype(F32)
    pack_ref[...] = pack.astype(BF)
    unpack_ref[...] = jnp.transpose(pack).astype(BF)
    hot_ref[...] = jnp.transpose(hot)
    packed_ref[...] = dot_nn(pack.astype(BF), cot_ref[...]).astype(BF)
    heads, buckets = bias_ref.shape
    length = table_ref.shape[1]
    for row, out in ((0, offset_ref), (1, back_ref)):
        table = lax.broadcasted_iota(jnp.int32, (buckets, length), 0) == table_ref[row : row + 1, :]
        out[0:heads, :] = dot_nn(bias_ref[...], table.astype(BF))
        out[heads:, :] = jnp.zeros((8 - heads, length), F32)
    router_ref[...] = jnp.zeros_like(router_ref)
    router_ref[0:experts, :] = router_in_ref[...]


def prepare(chosen, cot, tables, bias, router, capacity):
    experts, width = router.shape
    rows = chosen.shape[1]
    slots = experts * capacity
    return pl.pallas_call(
        functools.partial(prepare_kernel, experts, capacity),
        out_shape=[
            jax.ShapeDtypeStruct((slots, rows), BF),
            jax.ShapeDtypeStruct((rows, slots), BF),
            jax.ShapeDtypeStruct((slots, width), BF),
            jax.ShapeDtypeStruct((rows, LANES), F32),
            jax.ShapeDtypeStruct((8, tables.shape[1]), F32),
            jax.ShapeDtypeStruct((8, tables.shape[1]), F32),
            jax.ShapeDtypeStruct((LANES, width), BF),
        ],
        in_specs=[VMEM] * 5,
        out_specs=[VMEM] * 7,
        compiler_params=params(60),
        cost_estimate=cost(5e+10, 1e4),
    )(chosen, cot, tables, bias, router)


def mix_kernel(parts, experts, *refs):
    hidden_ref = refs[0]
    ctx_refs, weight_refs = refs[1 : 1 + parts], refs[1 + parts : 1 + 2 * parts]
    gain_ref, router_ref, chosen_ref, pack_ref, sum_ref, gate_ref, packed_ref = refs[
        1 + 2 * parts :
    ]
    first_sum = hidden_ref[...].astype(F32)
    for part in range(parts):
        first_sum = first_sum + dot_nn(ctx_refs[part][...], weight_refs[part][...])
    sum_ref[...] = first_sum
    normed = (first_sum * rms_scale(first_sum) * gain_ref[1:2, :]).astype(BF)
    packed_ref[...] = dot_nn(pack_ref[...], normed).astype(BF)
    lane = lax.broadcasted_iota(jnp.int32, gate_ref.shape, 1)
    logits = jnp.where(lane < experts, dot_nt(normed, router_ref[...]), F32(NEG))
    logits = jnp.exp(logits - jnp.max(logits, axis=1, keepdims=True))
    gate = jnp.sum(chosen_ref[...] * logits, axis=1, keepdims=True) / jnp.sum(logits, axis=1, keepdims=True)
    gate_ref[...] = jnp.broadcast_to(gate, gate_ref.shape)


def mix(hidden, ctxs, weights, gain, router, chosen, hot, experts):
    parts = len(weights)
    rows, width = hidden.shape
    return pl.pallas_call(
        functools.partial(mix_kernel, parts, experts),
        out_shape=[
            jax.ShapeDtypeStruct((rows, width), F32),
            jax.ShapeDtypeStruct((rows, LANES), F32),
            jax.ShapeDtypeStruct((hot.shape[0], width), BF),
        ],
        in_specs=[VMEM] * (2 * parts + 5),
        out_specs=[VMEM] * 3,
        compiler_params=params(60),
        cost_estimate=cost(5e+10, 1e4),
    )(hidden, *ctxs, *weights, gain, router, chosen, hot)


def expert_kernel(in_map, out_map, experts, where_ref, *refs):
    row_ref, cot_ref, router_ref = refs[:3]
    in_refs, out_refs = refs[3 : 3 + len(in_map)], refs[3 + len(in_map) : 3 + 2 * len(in_map)]
    back_ref, out_ref, gated_ref, logit_ref, near_hbm, far_hbm = refs[
        3 + 2 * len(in_map) : 9 + 2 * len(in_map)
    ]
    in_ref, outw_ref, near_ref, far_ref, total_ref, acc_ref, load_sems, store_sems = refs[
        9 + 2 * len(in_map) :
    ]
    units = len(in_map) // 2
    name = where_ref[3]
    slots, width = row_ref.shape
    span = in_refs[0].shape[1]
    hidden = units * span
    loads = []
    for unit in range(units):
        pieces = []
        for half in range(2):
            at = slice(half * span, (half + 1) * span)
            source = in_refs[in_map.index(unit + half * units)]
            pieces.append((source, in_ref.at[unit, :, at]))
            source = out_refs[out_map.index(unit + half * units)]
            pieces.append((source, outw_ref.at[unit, at, :]))
        copies = []
        for number, (source, target) in enumerate(pieces):
            copies.append(pltpu.make_async_copy(source, target, load_sems.at[unit, number]))
            copies[-1].start()
        loads.append(copies)
    rows_step = min(512, slots)
    tiles = [slice(at, at + rows_step) for at in range(0, slots, rows_step)]
    gates, routers = [], []
    lane = lax.broadcasted_iota(jnp.int32, (rows_step, LANES), 1)
    hot = (lane == name).astype(F32)
    for tile in tiles:
        logits = jnp.where(lane < experts, dot_nt(row_ref[tile, :], router_ref[...]), F32(NEG))
        logits = jnp.exp(logits - jnp.max(logits, axis=1, keepdims=True))
        router = logits / jnp.sum(logits, axis=1, keepdims=True)
        gate = jnp.sum(router * hot, axis=1, keepdims=True)
        gated = (cot_ref[tile, :].astype(F32) * gate).astype(BF)
        gated_ref[tile, :] = gated
        far_ref[tile, 2 * hidden :] = gated
        gates.append(gate)
        routers.append(router)
    stores = [
        pltpu.make_async_copy(
            far_ref.at[:, 2 * hidden :], far_hbm.at[:, 2 * hidden :], store_sems.at[units, 0]
        )
    ]
    stores[0].start()
    for unit in range(units):
        for copy in loads[unit]:
            copy.wait()
        for tile in tiles:
            pre_act = dot_nn(row_ref[tile, :], in_ref[unit])
            below = 0.5 + 0.5 * lax.erf(pre_act * F32(SQRT_HALF))
            active = (pre_act * below).astype(BF)
            slope = below + pre_act * jnp.exp(pre_act * pre_act * F32(-0.5)) * F32(INV_SQRT_TWO_PI)
            grad = (dot_nt(gated_ref[tile, :], outw_ref[unit]) * slope).astype(BF)
            for side_ref, half in ((near_ref, 0), (far_ref, 1)):
                at = slice(half * span, (half + 1) * span)
                side_ref[tile, unit * span : (unit + 1) * span] = active[:, at]
                side_ref[tile, hidden + unit * span : hidden + (unit + 1) * span] = grad[:, at]
            total = dot_nn(active, outw_ref[unit])
            back = dot_nt(grad, in_ref[unit])
            if unit:
                total_ref[tile, :] += total
                acc_ref[tile, :] += back
            else:
                total_ref[tile, :] = total
                acc_ref[tile, :] = back
        for number, (side_ref, side_hbm, first) in enumerate(
            (
                (near_ref, near_hbm, 0),
                (near_ref, near_hbm, hidden),
                (far_ref, far_hbm, 0),
                (far_ref, far_hbm, hidden),
            )
        ):
            at = slice(first + unit * span, first + (unit + 1) * span)
            copy = pltpu.make_async_copy(
                side_ref.at[:, at], side_hbm.at[:, at], store_sems.at[unit, number]
            )
            copy.start()
            stores.append(copy)
    for tile, gate, router in zip(tiles, gates, routers):
        total = total_ref[tile, :]
        gate_grad = jnp.sum(cot_ref[tile, :].astype(F32) * total, axis=1, keepdims=True)
        logit_grad = ((gate_grad * gate) * (hot - router)).astype(BF)
        logit_ref[tile, :] = logit_grad
        out_ref[tile, :] = total.astype(BF)
        back_ref[tile, :] = (acc_ref[tile, :] + dot_nn(logit_grad, router_ref[...])).astype(BF)
    for copy in stores:
        copy.wait()


def run_expert(where, rows, cots, in_parts, out_parts, in_map, out_map, router, experts):
    slots, width = rows.shape
    span = in_parts[0].shape[1]
    units = len(in_map) // 2
    hidden = 2 * units * span
    back, out, gated, logit, near, far = pl.pallas_call(
        functools.partial(expert_kernel, in_map, out_map, experts),
        out_shape=[
            jax.ShapeDtypeStruct((slots, width), BF),
            jax.ShapeDtypeStruct((slots, width), BF),
            jax.ShapeDtypeStruct((slots, width), BF),
            jax.ShapeDtypeStruct((slots, LANES), BF),
            jax.ShapeDtypeStruct((slots, hidden), BF),
            jax.ShapeDtypeStruct((slots, hidden + width), BF),
        ],
        in_specs=[SMEM] + [VMEM] * 3 + [ANY] * (len(in_parts) + len(out_parts)),
        out_specs=[VMEM] * 4 + [ANY] * 2,
        scratch_shapes=[
            pltpu.VMEM((units, width, 2 * span), BF),
            pltpu.VMEM((units, 2 * span, width), BF),
            pltpu.VMEM((slots, hidden), BF),
            pltpu.VMEM((slots, hidden + width), BF),
            pltpu.VMEM((slots, width), F32),
            pltpu.VMEM((slots, width), F32),
            pltpu.SemaphoreType.DMA((units, 4)),
            pltpu.SemaphoreType.DMA((units + 1, 4)),
        ],
        compiler_params=params(56),
        cost_estimate=cost(25e9, 20e6),
    )(where, rows, cots, router, *in_parts, *out_parts)
    return back, out, gated, near, far, logit


def weight_kernel(parts, row_ref, peer_ref, gated_ref, near_hbm, got_hbm, *refs):
    out_hbm = refs[: 2 * parts]
    both_ref, lhs_ref, tail_ref, done_ref, load_sems, store_sems = refs[2 * parts :]
    slots, width = row_ref.shape
    span = out_hbm[0].shape[1]
    hidden = parts * span
    chunk = 2 * span
    count = 2 * hidden // chunk
    tail = pltpu.make_async_copy(got_hbm.at[:, 2 * hidden :], tail_ref, load_sems.at[count, 0])
    loads = []
    order = list(range(count // 2, count)) + list(range(count // 2))
    for index in order:
        at = slice(index * chunk, (index + 1) * chunk)
        near = pltpu.make_async_copy(
            near_hbm.at[:, at], both_ref.at[0:slots, at], load_sems.at[index, 0]
        )
        got = pltpu.make_async_copy(
            got_hbm.at[:, at], both_ref.at[slots:, at], load_sems.at[index, 1]
        )
        near.start()
        got.start()
        loads.append((near, got))
        if index == count - 1:
            tail.start()
    lhs_ref[0, :, 0:slots] = jnp.transpose(row_ref[...])
    lhs_ref[0, :, slots:] = jnp.transpose(peer_ref[...])
    stores = []
    for number, index in enumerate(order):
        inward = index >= count // 2
        if number == count // 2:
            tail.wait()
            lhs_ref[1, :, 0:slots] = jnp.transpose(gated_ref[...])
            lhs_ref[1, :, slots:] = jnp.transpose(tail_ref[...])
        for copy in loads[number]:
            copy.wait()
        at = slice(index * chunk, (index + 1) * chunk)
        done_ref[number] = dot_nn(lhs_ref[0 if inward else 1], both_ref[:, at]).astype(BF)
        for half in range(2):
            part = 2 * (index % (count // 2)) + half
            copy = pltpu.make_async_copy(
                done_ref.at[number, :, half * span : (half + 1) * span],
                out_hbm[part if inward else parts + part],
                store_sems.at[number, half],
            )
            copy.start()
            stores.append(copy)
    for copy in stores:
        copy.wait()


def weight_grads(where, rows, rows_peer, gated, near, got, parts):
    slots, width = rows.shape
    span = near.shape[1] // (2 * parts)
    one = jax.ShapeDtypeStruct((width, span), BF)
    outs = pl.pallas_call(
        functools.partial(weight_kernel, parts),
        out_shape=[one] * (2 * parts),
        in_specs=[VMEM] * 3 + [ANY] * 2,
        out_specs=[ANY] * (2 * parts),
        scratch_shapes=[
            pltpu.VMEM((2 * slots, 2 * parts * span), BF),
            pltpu.VMEM((2, width, 2 * slots), BF),
            pltpu.VMEM((slots, width), BF),
            pltpu.VMEM((parts, width, 2 * span), BF),
            pltpu.SemaphoreType.DMA((parts + 1, 2)),
            pltpu.SemaphoreType.DMA((parts, 2)),
        ],
        compiler_params=params(60),
        cost_estimate=cost(1e10, 1e6),
    )(rows, rows_peer, gated, near, got)
    return outs[:parts], outs[parts:]


def finish_kernel(where_ref, *refs):
    core = where_ref[2]
    in_ref, out_ref = refs[4:]
    span = refs[0].shape[1]
    for half in range(2):
        own_in, own_out = refs[2 * half : 2 * half + 2]
        at = pl.ds(pl.multiple_of((core ^ half) * span, LANES), span)
        in_ref[:, at] = own_in[...].astype(F32)
        out_ref[at, :] = jnp.transpose(own_out[...].astype(F32))


def finish(where, mine, peer):
    width, span = mine[0].shape
    return pl.pallas_call(
        finish_kernel,
        out_shape=[
            jax.ShapeDtypeStruct((width, 2 * span), F32),
            jax.ShapeDtypeStruct((2 * span, width), F32),
        ],
        in_specs=[SMEM] + [VMEM] * 4,
        out_specs=[VMEM, VMEM],
        compiler_params=params(40),
        cost_estimate=cost(5e+10, 1e4),
    )(where, *mine, *peer)


def residual_kernel(parts, where_ref, *refs):
    home_ref, hot_ref, sum_ref, cot_ref, gain_ref = refs[:5]
    weight_refs, old_refs = refs[5 : 5 + parts], refs[5 + parts : 5 + 2 * parts]
    grad_ref, gain_out_ref, give_ref = refs[5 + 2 * parts : 8 + 2 * parts]
    ctx_refs, keep_refs = refs[8 + 2 * parts : 8 + 3 * parts], refs[8 + 3 * parts :]
    core = where_ref[2]
    side = grad_ref.shape[1] // 2
    upstream = dot_nn(hot_ref[...], home_ref[...])
    first_sum = sum_ref[...]
    inverse = rms_scale(first_sum)
    gain_out_ref[...] = jnp.broadcast_to(
        jnp.sum(upstream * first_sum * inverse, axis=0, keepdims=True), gain_out_ref.shape
    )
    grad = cot_ref[...].astype(F32) + norm_back(first_sum, inverse, gain_ref[1:2, :], upstream)
    grad_ref[...] = grad
    low = grad.astype(BF)
    for part in range(parts):
        ctx_refs[part][...] = dot_nt(low, weight_refs[part][...]).astype(BF)
    for part in range(parts):
        product = dot_tn(old_refs[part][...], low)

        @pl.when(core == 0)
        def _(product=product, part=part):
            keep_refs[part][...] = product[:, :side]
            give_ref[part] = product[:, side:].astype(BF)

        @pl.when(core != 0)
        def _(product=product, part=part):
            keep_refs[part][...] = product[:, side:]
            give_ref[part] = product[:, :side].astype(BF)


def residual(where, home, hot, first_sum, cot, gain, weights, ctxs):
    parts = len(weights)
    rows, width = first_sum.shape
    inner = weights[0].shape[0]
    return pl.pallas_call(
        functools.partial(residual_kernel, parts),
        out_shape=[
            jax.ShapeDtypeStruct((rows, width), F32),
            jax.ShapeDtypeStruct((8, width), F32),
            jax.ShapeDtypeStruct((parts, inner, width // 2), BF),
        ]
        + [jax.ShapeDtypeStruct((rows, inner), BF)] * parts
        + [jax.ShapeDtypeStruct((inner, width // 2), F32)] * parts,
        in_specs=[SMEM] + [VMEM] * (2 * parts + 5),
        out_specs=[VMEM] * (3 + 2 * parts),
        compiler_params=params(60),
        cost_estimate=cost(2e+11, 1e4),
    )(where, home, hot, first_sum, cot, gain, *weights, *ctxs)


def attend_back_kernel(parts, heads, where_ref, *refs):
    cot_refs, refs = refs[:parts], refs[parts:]
    ctx_ref, proj_ref, normed_ref, lse_ref, weight_ref, offset_ref = refs[:6]
    scale_ref, small_ref, table_ref = refs[6:9]
    send_ref, bias_ref, keep_ref, give_ref = refs[9:13]
    skew_ref, fold_ref, cot_ref, dproj_ref, key_acc, value_acc = refs[13:]
    quarter = ctx_ref.shape[1]
    for part in range(parts):
        cot_ref[where_ref[0] ^ part] = cot_refs[part][...]
    length = quarter * parts
    inner = weight_ref.shape[0] // 3
    head_dim = inner // heads
    prefix, core = where_ref[1], where_ref[2]
    skew_into(skew_ref, offset_ref, heads, 2 * length)
    fold_ref[...] = jnp.zeros_like(fold_ref)
    key_acc[...] = jnp.zeros_like(key_acc)
    value_acc[...] = jnp.zeros_like(value_acc)
    keys_across = jnp.transpose(proj_ref[:, inner : 2 * inner])
    head_row = lax.broadcasted_iota(jnp.int32, (8, inner), 0)
    head_lane = lax.broadcasted_iota(jnp.int32, (8, inner), 1)
    picks = (head_lane // head_dim == head_row).astype(BF)
    for block in range(parts):
        first = block * quarter
        reach = max(length // 2, first + quarter)
        key_pos = first + lax.broadcasted_iota(jnp.int32, (reach - first, quarter), 0)
        query_pos = first + lax.broadcasted_iota(jnp.int32, (reach - first, quarter), 1)
        allowed = (key_pos <= query_pos) | (key_pos < prefix)
        product = cot_ref[block].astype(F32) * ctx_ref[block].astype(F32)
        high = product.astype(BF)
        rest = (product - high.astype(F32)).astype(BF)
        inner_sum = dot_nt(picks, high) + dot_nt(picks, rest)
        query_pieces = []
        for head in range(heads):
            low = head * head_dim
            query = proj_ref[first : first + quarter, low : low + head_dim]
            keys = proj_ref[0:reach, inner + low : inner + low + head_dim]
            values = proj_ref[0:reach, 2 * inner + low : 2 * inner + low + head_dim]
            grad = cot_ref[block, :, low : low + head_dim]
            bias = jnp.concatenate(
                [
                    skew_ref[
                        head,
                        :,
                        first - LANES * sub + length - LANES : first
                        - LANES * sub
                        + length
                        - LANES
                        + quarter,
                    ]
                    for sub in range(reach // LANES)
                ],
                axis=0,
            )
            scores = dot_nt(keys, query) + bias
            tail = jnp.where(allowed, scores[first:], F32(NEG))
            scores = jnp.concatenate([scores[:first], tail], axis=0) if first else tail
            probs = jnp.exp(scores - lse_ref[block, head : head + 1, :])
            prob_grad = dot_nt(values, grad)
            score_grad = (probs * (prob_grad - inner_sum[head : head + 1, :])).astype(BF)
            wide = score_grad.astype(F32)
            for sub in range(reach // LANES):
                column = first - LANES * sub + length - LANES
                fold_ref[head, :, column : column + quarter] += wide[
                    LANES * sub : LANES * (sub + 1)
                ]
            value_acc[head, 0:reach, :] += dot_nn(probs.astype(BF), grad)
            key_acc[head, 0:reach, :] += dot_nn(score_grad, query)
            query_pieces.append(dot_nn(keys_across[low : low + head_dim, 0:reach], score_grad))
        query_grad = jnp.transpose(jnp.concatenate(query_pieces, axis=0)) * F32(head_dim ** (-0.5))
        dproj_ref[first : first + quarter, 0:inner] = query_grad.astype(BF)
    dproj_ref[:, inner : 3 * inner] = jnp.concatenate(
        [key_acc[head] for head in range(heads)] + [value_acc[head] for head in range(heads)],
        axis=1,
    ).astype(BF)
    width = normed_ref.shape[1]
    side = width // 2
    split, piece, _ = keep_ref.shape
    layer = where_ref[3]
    grad_rows = dot_nn(jnp.transpose(dproj_ref[...]), normed_ref[...])
    for half in range(2):
        for part in range(split):
            chunk = grad_rows[part * piece : (part + 1) * piece, half * side : (half + 1) * side]
            slot = (layer ^ part) if split > 1 else part

            @pl.when(core == half)
            def _(chunk=chunk, slot=slot):
                keep_ref[slot] = chunk

            @pl.when(core != half)
            def _(chunk=chunk, slot=slot):
                give_ref[slot] = chunk.astype(BF)

    gain_sum = jnp.zeros((1, width), F32)
    for block in range(parts):
        rows = slice(block * quarter, (block + 1) * quarter)
        upstream = dot_nn(dproj_ref[rows, :], weight_ref[...])
        gain_sum = gain_sum + jnp.sum(
            upstream * normed_ref[rows, :].astype(F32), axis=0, keepdims=True
        )
        send_ref[block, 0:quarter, :] = upstream.astype(BF)
    extra = small_ref.shape[0]
    row = lax.broadcasted_iota(jnp.int32, small_ref.shape, 0)
    small = jnp.where(row == 0, gain_sum / scale_ref[0:1, :], small_ref[...]).astype(BF)
    share = width // parts
    for block in range(parts):
        send_ref[block, quarter:, 0:share] = small[:, block * share : (block + 1) * share]
        send_ref[block, quarter:, share:] = jnp.zeros((extra, width - share), BF)
    row_index = lax.broadcasted_iota(jnp.int32, (LANES, 2 * length), 0)
    buckets = (row_index == table_ref[1:2, :]).astype(BF)
    sums = []
    for head in range(heads):
        tile = fold_ref[head, 0:8, :]
        for group in range(8, LANES, 8):
            tile = tile + pltpu.roll(fold_ref[head, group : group + 8, :], 2 * length - group, 1)
        for bit in range(3):
            moved = pltpu.roll(tile, 2 * length - (1 << bit), 1)
            tile = jnp.where(((row_index[0:8] >> bit) & 1) == 1, moved, tile)
        tile = pltpu.roll(tile, LANES - 1, 1)
        sums.append(jnp.sum(tile, axis=0, keepdims=True))
    rest = jnp.concatenate(sums + [jnp.zeros((8 - heads, 2 * length), F32)], axis=0)
    levels = []
    for _ in range(3):
        high = rest.astype(BF).astype(F32)
        rest = rest - high
        levels.append(high)
    total = dot_nt(jnp.concatenate(levels, axis=0).astype(BF), buckets)
    total = total[0:8] + total[8:16] + total[16:24]
    bias_ref[0:8, :] = total
    bias_ref[8:, :] = jnp.zeros((bias_ref.shape[0] - 8, LANES), F32)


def attend_back(
    where, cots, ctxs, proj, normed, lse, weight, offsets, scale, small, tables, heads, split
):
    parts, quarter, inner = ctxs.shape
    width = normed.shape[1]
    length = parts * quarter
    return pl.pallas_call(
        functools.partial(attend_back_kernel, parts, heads),
        out_shape=[
            jax.ShapeDtypeStruct((parts, quarter + small.shape[0], width), BF),
            jax.ShapeDtypeStruct((small.shape[0], LANES), F32),
            jax.ShapeDtypeStruct((split, 3 * inner // split, width // 2), F32),
            jax.ShapeDtypeStruct((split, 3 * inner // split, width // 2), BF),
        ],
        in_specs=[SMEM] + [VMEM] * (9 + parts),
        out_specs=[VMEM] * 4,
        scratch_shapes=[
            pltpu.VMEM((heads, LANES, 2 * length), F32),
            pltpu.VMEM((heads, LANES, 2 * length), F32),
            pltpu.VMEM((parts, quarter, inner), BF),
            pltpu.VMEM((length, 3 * inner), BF),
            pltpu.VMEM((heads, length, inner // heads), F32),
            pltpu.VMEM((heads, length, inner // heads), F32),
        ],
        compiler_params=params(60),
        cost_estimate=cost(5e+10, 1e4),
    )(where, *cots, ctxs, proj, normed, lse, weight, offsets, scale, small, tables)


def merge_kernel(parts, where_ref, keep_ref, got_ref, *refs):
    wo_refs, (home_ref, hot_ref, sum_ref, gate_ref) = refs[:parts], refs[parts : parts + 4]
    layer_ref, send_refs, wo_ref = refs[parts + 4], refs[parts + 5 : -1], refs[-1]
    split, piece, side = keep_ref.shape
    share = wo_ref.shape[0] // split
    layer = where_ref[3]
    total = wo_refs[0][...] + wo_refs[1][0].astype(F32)
    for part in range(2, parts):
        total = total + wo_refs[part][...].astype(F32)
    wo_ref[...] = total
    expert_out = dot_nn(hot_ref[...], home_ref[...])
    layer_ref[...] = (sum_ref[...] + gate_ref[:, 0:1] * expert_out).astype(BF)
    for part in range(split):
        send_refs[part][0:piece, :] = (keep_ref[part] + got_ref[part].astype(F32)).astype(BF)
        row = (layer ^ part) * share if split > 1 else 0
        send_refs[part][piece:, :] = wo_ref[pl.ds(pl.multiple_of(row, 8), share), :].astype(BF)


def merge(where, keep, got, wos, home, hot, first_sum, gate):
    split, piece, side = keep.shape
    rows = wos[0].shape[0]
    shape = jax.ShapeDtypeStruct((piece + rows // split, side), BF)
    return pl.pallas_call(
        functools.partial(merge_kernel, len(wos)),
        out_shape=[jax.ShapeDtypeStruct(first_sum.shape, BF)] + [shape] * split,
        in_specs=[SMEM] + [VMEM] * (6 + len(wos)),
        out_specs=[VMEM] * (1 + split),
        scratch_shapes=[pltpu.VMEM((rows, side), F32)],
        compiler_params=params(60),
        cost_estimate=cost(1e+06, 1e4),
    )(where, keep, got, *wos, home, hot, first_sum, gate)


def assemble_kernel(where_ref, *refs):
    *piece_refs, qkv_ref, wo_ref, first_ref, second_ref, router_ref, bias_ref, parts_ref = refs
    split = len(piece_refs) // 2
    side = qkv_ref.shape[1] // 2
    piece, share = qkv_ref.shape[0] // split, wo_ref.shape[0] // split
    core, layer = where_ref[2], where_ref[3]
    for part in range(split):
        slot = (layer ^ part) if split > 1 else 0
        for half in range(2):
            ref = piece_refs[half * split + part]
            at = pl.ds(pl.multiple_of((core ^ half) * side, LANES), side)
            values = ref[...].astype(F32)
            qkv_ref[pl.ds(pl.multiple_of(slot * piece, 8), piece), at] = values[0:piece]
            wo_ref[pl.ds(pl.multiple_of(slot * share, 8), share), at] = values[
                piece : piece + share
            ]
            parts_ref[(core ^ half) * split + slot] = values[piece + share :]
    total = parts_ref[0]
    for part in range(1, 2 * split):
        total = total + parts_ref[part]
    share = first_ref.shape[1]
    first_ref[...] = total[0:1, 0:share]
    second_ref[...] = total[1:2, 0:share]
    router_ref[...] = total[2 : 2 + router_ref.shape[0], 0:share]
    bias_ref[...] = total[0 : bias_ref.shape[0], share : share + bias_ref.shape[1]]


def assemble(where, pieces, rows, extra, width, experts, heads, buckets):
    split = len(pieces) // 2
    both, side = pieces[0].shape
    return pl.pallas_call(
        assemble_kernel,
        out_shape=[
            jax.ShapeDtypeStruct((rows, 2 * side), F32),
            jax.ShapeDtypeStruct((split * (both - extra) - rows, 2 * side), F32),
            jax.ShapeDtypeStruct((1, width), F32),
            jax.ShapeDtypeStruct((1, width), F32),
            jax.ShapeDtypeStruct((experts, width), F32),
            jax.ShapeDtypeStruct((heads, buckets), F32),
        ],
        in_specs=[SMEM] + [VMEM] * (2 * split),
        out_specs=[VMEM] * 6,
        scratch_shapes=[pltpu.VMEM((2 * split, extra, side), F32)],
        compiler_params=params(16),
        cost_estimate=cost(1e+06, 1e4),
    )(where, *pieces)


def trade(values, axis):
    return lax.all_to_all(values, axis, split_axis=0, concat_axis=0, tiled=True)


def after(values, others):
    return lax.optimization_barrier((values, others))[0]


def body(
    hidden_in,
    cotangent,
    attn_gain,
    query_key_value_weight,
    attention_output_weight,
    rel_bias,
    bucket_table,
    prefix_len,
    moe_gain,
    w_router,
    routes,
    w_expert_in,
    w_expert_out,
):
    seq_count, quarter, model_width = hidden_in.shape
    parts = lax.axis_size("tensor")
    layers = lax.axis_size("expert")
    row_count = seq_count * quarter
    experts = w_router.shape[1]
    capacity = max(2, 2 * row_count // experts)
    slot_count = experts * capacity
    heads, buckets = rel_bias.shape
    inner = query_key_value_weight.shape[2]
    span = w_expert_in.shape[2] // 2
    place, layer, core = lax.axis_index("tensor"), lax.axis_index("expert"), lax.axis_index("dp")
    where = jnp.stack([place, prefix_len[0], core, layer]).astype(jnp.int32)
    low_core = core == 0

    own_hidden = hidden_in[0]
    own_cot = cotangent[0]

    chosen = routes.reshape(1, row_count)
    tables = jnp.stack([bucket_table, jnp.flip(bucket_table)])
    tables = jnp.pad(tables, ((0, 0), (0, 1)), constant_values=-1)
    gains = jnp.stack([attn_gain, moe_gain]).astype(F32)
    pack_hot, unpack_hot, cot_packed, chosen_hot, offset_bias, offset_back, router = prepare(
        chosen, own_cot, tables, rel_bias, w_router.T, capacity
    )

    def over_experts(packed):
        packed = packed.reshape(experts, capacity, model_width)
        return trade(packed, "expert").reshape(slot_count, model_width)

    cot_slots = over_experts(cot_packed)

    hidden_blocks = [own_hidden] + [swap(own_hidden, "tensor", k) for k in range(1, parts)]
    weight = query_key_value_weight.transpose(1, 2, 0).reshape(3 * inner, model_width)
    late_weight = after(attention_output_weight, hidden_blocks)
    out_weights = [attention_output_weight] + [
        swap(late_weight if k == parts - 1 else attention_output_weight, "tensor", k)
        for k in range(1, parts)
    ]
    early_weights = out_weights[:-1]
    first_blocks, prepared = lax.optimization_barrier(
        (hidden_blocks, (early_weights, pack_hot, unpack_hot, chosen_hot, router, offset_bias,
                         offset_back, where, gains))
    )
    early_weights, pack_hot, unpack_hot, chosen_hot, router, offset_bias, offset_back, where, gains = (
        prepared
    )
    normed_one, projected, lse, contexts, sends = attend(
        where, first_blocks, gains, weight, offset_bias, heads
    )

    in_own = lax.dynamic_slice(w_expert_in[0], (0, core * span), (model_width, span))
    out_own = lax.dynamic_slice(w_expert_out[0], (core * span, 0), (span, model_width))
    in_other = lax.dynamic_slice(w_expert_in[0], (0, (1 - core) * span), (model_width, span))
    out_other = lax.dynamic_slice(w_expert_out[0], ((1 - core) * span, 0), (span, model_width))
    in_own, out_own = after((in_own, out_own), hidden_blocks)
    in_step, out_step = swap(in_own, "tensor", 1), swap(out_own, "tensor", 2)
    out_weights = early_weights + out_weights[-1:]
    sends = after(sends, out_weights[-1])
    own_contexts = [sends[0]] + [swap(sends[k], "tensor", k) for k in range(1, parts)]


    in_next, out_next = after((in_own, out_own), own_contexts[1])
    in_next, out_next = swap(in_next, "tensor", 2), swap(out_next, "tensor", 1)
    in_far, out_far = after((in_step, out_step), (own_contexts, in_next, out_next))
    in_far, out_far = swap(in_far, "tensor", 2), swap(out_far, "tensor", 1)
    in_near, in_order = [in_own, in_step, in_next, in_far], (0, 1, 2, 3)
    out_near, out_order = [out_own, out_step, out_next, out_far], (0, 2, 1, 3)
    in_map = in_order + tuple(parts + unit for unit in in_order)
    out_map = out_order + tuple(parts + unit for unit in out_order)

    first_sum, gate, packed = mix(
        own_hidden, after(own_contexts, (cot_slots, in_step, out_step)), out_weights, gains, router,
        chosen_hot, pack_hot, experts,
    )
    row_slots = over_experts(packed)

    def cross(pieces):
        _, near, near_too, far = pieces
        near_too, far = after((near_too, far), row_slots)
        return [swap(near, "dp", 1), swap(near_too, "dp", 1), swap(far, "dp", 1)]

    in_parts = in_near + [in_other] + cross(in_near)
    out_parts = out_near + [out_other] + cross(out_near)
    rows_peer = swap(row_slots, "dp", 1)
    back_slots, out_slots, gated, near, far, logit_grad = run_expert(
        where, row_slots, cot_slots, in_parts, out_parts, in_map, out_map, router, experts
    )
    back_home = over_experts(back_slots)

    in_sums, out_sums = partial = weight_grads(
        where, row_slots, rows_peer, gated, near, swap(far, "dp", 1), parts
    )
    in_skip, out_skip = swap(in_sums[3], "tensor", 1), swap(out_sums[3], "tensor", 2)

    def plus(*terms):
        total = terms[0].astype(F32)
        for term in terms[1:]:
            total = total + term.astype(F32)
        return total.astype(BF)


    residual_grad, moe_gain_part, wo_give, *cots = residual(
        where, after(back_home, partial), unpack_hot, first_sum, own_cot, gains, out_weights,
        own_contexts,
    )
    cots, wo_keep = cots[:parts], cots[parts:]
    context_cots = [cots[0]] + [swap(cots[k], "tensor", k) for k in range(1, parts)]
    out_home = over_experts(out_slots)

    side = model_width // 2
    wo_got = swap(wo_give, "dp", 1)
    wo_low = [(wo_keep[k] + wo_got[k].astype(F32)).astype(BF) for k in range(1, parts)]
    context_cots = after(context_cots, (wo_low, in_skip, out_skip))
    in_side, out_side = after((in_sums[1], out_sums[2]), (in_skip, out_skip))
    in_side, out_side = swap(in_side, "tensor", 1), swap(out_side, "tensor", 2)
    wo_parts = [wo_keep[0], wo_got] + [
        swap(wo_low[k - 1], "tensor", k) for k in range(1, parts)
    ]

    split = layers if layers == 4 else 1
    router_part = dot_tn(logit_grad, row_slots)[:experts]
    extra = -(-(experts + 2) // 16) * 16
    small = jnp.concatenate([moe_gain_part[:1], router_part], axis=0)
    small = jnp.pad(small, ((1, extra - 2 - experts), (0, 0)))
    send_ups, bias_part, keep, give = attend_back(
        where, context_cots, contexts, projected, normed_one, lse, weight, offset_back,
        gains, small, tables, heads, split,
    )
    send_ups, give = after((send_ups, give), (wo_parts, out_home, in_side, out_side))
    ups = jnp.sum(trade(send_ups, "tensor").astype(F32), axis=0)
    own_float = own_hidden.astype(F32)
    inverse_own = rms_scale(own_float)
    input_grad = residual_grad + norm_back(own_float, inverse_own, gains[0:1], ups[:quarter])

    share = model_width // parts
    bias_part = jnp.pad(bias_part, ((0, 0), (0, side - share - LANES)))
    small = jnp.concatenate([ups[quarter:, :share], bias_part], axis=1)
    layer_out, *sends = merge(
        where, keep, swap(give, "dp", 1), wo_parts, out_home, unpack_hot, first_sum, gate
    )
    piece = sends[0].astype(F32)
    first = sends[-1]
    if split > 1:
        arrived = [swap(sends[k], "expert", k) for k in range(1, layers)]
        first = arrived[0]
        for value in arrived:
            piece = piece + value.astype(F32)
    in_skip, out_skip, in_side, out_side = after((in_skip, out_skip, in_side, out_side), first)
    in_pass, out_pass = plus(in_sums[2], in_skip), plus(out_sums[1], out_skip)
    in_last, out_last = swap(in_pass, "tensor", 2), swap(out_pass, "tensor", 1)
    if split > 1:
        piece = jnp.concatenate([piece, small], axis=0).astype(BF)
        pieces = [piece] + [swap(piece, "expert", k) for k in range(1, layers)]
    else:
        pieces = [lax.psum(jnp.concatenate([piece, small], axis=0), "expert")]
    in_last, out_last = after((in_last, out_last), pieces[:2])
    mine = (plus(in_sums[0], in_side, in_last), plus(out_sums[0], out_side, out_last))
    expert_in_grad, expert_out_grad = finish(where, mine, [swap(x, "dp", 1) for x in mine])
    pieces = pieces + [swap(x, "dp", 1) for x in pieces]
    done = (layer_out, expert_in_grad, expert_out_grad, input_grad)
    pieces, done = lax.optimization_barrier((pieces, done))
    layer_out, expert_in_grad, expert_out_grad, input_grad = done
    qkv_across, attn_out_grad, gain_one, gain_two, router_grad, bias_grad = assemble(
        where, pieces, 3 * inner, extra, share, experts, heads, buckets
    )
    qkv_grad = qkv_across.reshape(3, inner, model_width).transpose(2, 0, 1)
    return (
        layer_out.reshape(seq_count, quarter, model_width),
        input_grad.reshape(seq_count, quarter, model_width),
        gain_one[0],
        qkv_grad,
        attn_out_grad,
        bias_grad,
        gain_two[0],
        router_grad.T,
        expert_in_grad[None],
        expert_out_grad[None],
    )


def solution(mesh):
    placed = (
        P(("dp", "expert"), "tensor", None),
        P(("dp", "expert"), "tensor", None),
        P(),
        P(None, None, "tensor"),
        P("tensor", None),
        P("tensor", None),
        P(),
        P(("dp", "expert")),
        P(),
        P(),
        P(("dp", "expert"), "tensor", None, None, None),
        P("expert", None, "tensor"),
        P("expert", "tensor", None),
    )
    return jax.shard_map(
        body,
        mesh=mesh,
        in_specs=placed,
        out_specs=(
            P(("dp", "expert"), "tensor", None),
            P(("dp", "expert"), "tensor", None),
            P("tensor"),
            P(None, None, "tensor"),
            P("tensor", None),
            P("tensor", None),
            P("tensor"),
            P("tensor", None),
            P("expert", None, "tensor"),
            P("expert", "tensor", None),
        ),
        check_vma=False,
    )
```

```python
import functools

import jax
import jax.numpy as jnp
from jax import lax
from jax.experimental import pallas as pl
from jax.experimental.pallas import tpu as pltpu
from jax.sharding import PartitionSpec as P

EPSILON = 1e-06
NEG = -1e30
TOP_PRECISION = lax.Precision.HIGHEST
BF = jnp.bfloat16
F32 = jnp.float32
LANES = 128
VMEM = pl.BlockSpec()
ANY = pl.BlockSpec(memory_space=pl.ANY)
SMEM = pl.BlockSpec(memory_space=pltpu.SMEM)
SQRT_HALF = 0.7071067811865476
INV_SQRT_TWO_PI = 0.3989422804014327


def params(mib):
    return pltpu.CompilerParams(vmem_limit_bytes=mib * 1024 * 1024)


def cost(flops, moved):
    return pl.CostEstimate(flops=int(flops), bytes_accessed=int(moved), transcendentals=0)


def dot_nn(a, b):
    return lax.dot_general(a, b, (((1,), (0,)), ((), ())), preferred_element_type=F32)


def dot_nt(a, b):
    return lax.dot_general(a, b, (((1,), (1,)), ((), ())), preferred_element_type=F32)


def dot_tn(a, b):
    return lax.dot_general(a, b, (((0,), (0,)), ((), ())), preferred_element_type=F32)


def rms_scale(values):
    return lax.rsqrt(jnp.mean(values * values, axis=-1, keepdims=True) + EPSILON)


def norm_back(values, inverse, gain_vec, upstream):
    scaled = upstream * gain_vec
    return inverse * scaled - values * (inverse * inverse * inverse) * jnp.mean(
        scaled * values, axis=-1, keepdims=True
    )


def swap(values, axis, step):
    count = lax.axis_size(axis)
    return lax.ppermute(values, axis, [(i, i ^ step) for i in range(count)])


def skew_into(skew_ref, offset_ref, heads, width):
    for head in range(heads):
        row = jnp.broadcast_to(offset_ref[head : head + 1, :], (LANES, width))
        skew_ref[head] = pltpu.roll(row, width - (LANES - 1), 1, stride=1, stride_axis=0)


def attend_kernel(parts, heads, where_ref, *refs):
    x_refs = refs[:parts]
    gain_ref, weight_ref, offset_ref = refs[parts : parts + 3]
    normed_ref, proj_ref, lse_ref, ctx_ref = refs[parts + 3 : parts + 7]
    send_refs, skew_ref = refs[parts + 7 : 2 * parts + 7], refs[2 * parts + 7]
    quarter = x_refs[0].shape[0]
    length = quarter * parts
    inner = weight_ref.shape[0] // 3
    head_dim = inner // heads
    place, prefix = where_ref[0], where_ref[1]
    lane = lax.broadcasted_iota(jnp.int32, (1, 3 * inner), 1)
    column_scale = jnp.where(lane < inner, F32(head_dim ** (-0.5)), F32(1.0))
    for part in range(parts):
        x = x_refs[part][...].astype(F32)
        normed = (x * rms_scale(x) * gain_ref[0:1, :]).astype(BF)
        rows = pl.ds(pl.multiple_of((place ^ part) * quarter, quarter), quarter)
        normed_ref[rows, :] = normed
        proj_ref[rows, :] = (dot_nt(normed, weight_ref[...]) * column_scale).astype(BF)
    skew_into(skew_ref, offset_ref, heads, 2 * length)
    tiles = length // LANES
    per_block = quarter // LANES
    for block in range(parts):
        first = block * quarter
        reach = max(length // 2, first + quarter)
        key_pos = first + lax.broadcasted_iota(jnp.int32, (quarter, reach - first), 1)
        query_pos = first + lax.broadcasted_iota(jnp.int32, (quarter, reach - first), 0)
        allowed = (key_pos <= query_pos) | (key_pos < prefix)
        pieces, logs = [], []
        for head in range(heads):
            low = head * head_dim
            query = proj_ref[first : first + quarter, low : low + head_dim]
            keys = proj_ref[0:reach, inner + low : inner + low + head_dim]
            values = proj_ref[0:reach, 2 * inner + low : 2 * inner + low + head_dim]
            bias = jnp.concatenate(
                [
                    skew_ref[
                        head,
                        :,
                        LANES * (tiles - 1 - block * per_block - sub) : LANES
                        * (tiles - 1 - block * per_block - sub)
                        + reach,
                    ]
                    for sub in range(per_block)
                ],
                axis=0,
            )
            scores = dot_nt(query, keys) + bias
            tail = jnp.where(allowed, scores[:, first:], F32(NEG))
            scores = jnp.concatenate([scores[:, :first], tail], axis=1) if first else tail
            peak = jnp.max(scores, axis=1, keepdims=True)
            exponent = jnp.exp(scores - peak)
            total = jnp.sum(exponent, axis=1, keepdims=True)
            pieces.append(dot_nn(exponent.astype(BF), values) / total)
            logs.append(jnp.broadcast_to(peak + jnp.log(total), (quarter, LANES)))
        ctx_ref[block] = jnp.concatenate(pieces, axis=1).astype(BF)
        lane_row = lax.broadcasted_iota(jnp.int32, (quarter, LANES), 1)
        stacked = logs[0]
        for head in range(1, heads):
            stacked = jnp.where(lane_row == head, logs[head], stacked)
        lse_ref[block] = jnp.transpose(stacked)[0:8, :]
    for part in range(parts):
        send_refs[part][...] = ctx_ref[place ^ part]


def attend(where, blocks, gain, weight, offsets, heads):
    parts = len(blocks)
    quarter, width = blocks[0].shape
    length = parts * quarter
    inner3 = weight.shape[0]
    outs = pl.pallas_call(
        functools.partial(attend_kernel, parts, heads),
        out_shape=[
            jax.ShapeDtypeStruct((length, width), BF),
            jax.ShapeDtypeStruct((length, inner3), BF),
            jax.ShapeDtypeStruct((parts, 8, quarter), F32),
            jax.ShapeDtypeStruct((parts, quarter, inner3 // 3), BF),
        ]
        + [jax.ShapeDtypeStruct((quarter, inner3 // 3), BF)] * parts,
        in_specs=[SMEM] + [VMEM] * (parts + 3),
        out_specs=[VMEM] * (4 + parts),
        scratch_shapes=[pltpu.VMEM((heads, LANES, 2 * length), F32)],
        compiler_params=params(60),
        cost_estimate=cost(5e+10, 1e4),
    )(where, *blocks, gain, weight, offsets)
    return outs[0], outs[1], outs[2], outs[3], outs[4:]


def prepare_kernel(experts, capacity, chosen_ref, cot_ref, table_ref, bias_ref, router_in_ref, *outs):
    pack_ref, unpack_ref, packed_ref, hot_ref, offset_ref, back_ref, router_ref = outs
    slots, rows = pack_ref.shape
    chosen = chosen_ref[...]
    hot = (lax.broadcasted_iota(jnp.int32, (LANES, rows), 0) == chosen).astype(F32)
    earlier = lax.broadcasted_iota(jnp.int32, (rows, rows), 0)
    later = lax.broadcasted_iota(jnp.int32, (rows, rows), 1)
    before = dot_nn(hot.astype(BF), (earlier < later).astype(BF))
    slot = jnp.sum(before * hot, axis=0, keepdims=True)
    target = chosen * capacity + slot.astype(jnp.int32)
    pack = (lax.broadcasted_iota(jnp.int32, (slots, rows), 0) == target).astype(F32)
    pack_ref[...] = pack.astype(BF)
    unpack_ref[...] = jnp.transpose(pack).astype(BF)
    hot_ref[...] = jnp.transpose(hot)
    packed_ref[...] = dot_nn(pack.astype(BF), cot_ref[...]).astype(BF)
    heads, buckets = bias_ref.shape
    length = table_ref.shape[1]
    for row, out in ((0, offset_ref), (1, back_ref)):
        table = lax.broadcasted_iota(jnp.int32, (buckets, length), 0) == table_ref[row : row + 1, :]
        out[0:heads, :] = dot_nn(bias_ref[...], table.astype(BF))
        out[heads:, :] = jnp.zeros((8 - heads, length), F32)
    router_ref[...] = jnp.zeros_like(router_ref)
    router_ref[0:experts, :] = router_in_ref[...]


def prepare(chosen, cot, tables, bias, router, capacity):
    experts, width = router.shape
    rows = chosen.shape[1]
    slots = experts * capacity
    return pl.pallas_call(
        functools.partial(prepare_kernel, experts, capacity),
        out_shape=[
            jax.ShapeDtypeStruct((slots, rows), BF),
            jax.ShapeDtypeStruct((rows, slots), BF),
            jax.ShapeDtypeStruct((slots, width), BF),
            jax.ShapeDtypeStruct((rows, LANES), F32),
            jax.ShapeDtypeStruct((8, tables.shape[1]), F32),
            jax.ShapeDtypeStruct((8, tables.shape[1]), F32),
            jax.ShapeDtypeStruct((LANES, width), BF),
        ],
        in_specs=[VMEM] * 5,
        out_specs=[VMEM] * 7,
        compiler_params=params(60),
        cost_estimate=cost(5e+10, 1e4),
    )(chosen, cot, tables, bias, router)


def mix_kernel(parts, experts, where_ref, *refs):
    hidden_ref, near_refs, far_ref, weight_ref = refs[0], refs[1:parts], refs[parts], refs[parts + 1]
    ctx_refs = refs[parts + 2 : 2 * parts + 2]
    gain_ref, router_ref, chosen_ref, pack_ref = refs[2 * parts + 2 : 2 * parts + 6]
    sum_ref, gate_ref, packed_ref, whole_ref, all_ref = refs[2 * parts + 6 :]
    core = where_ref[2]
    inner, width = weight_ref.shape
    side = width // 2
    whole_ref[0:inner, :] = weight_ref[...]
    near_at = pl.ds(pl.multiple_of(core * side, LANES), side)
    far_at = pl.ds(pl.multiple_of((1 - core) * side, LANES), side)
    for part in range(1, parts):
        rows = slice(part * inner, (part + 1) * inner)
        whole_ref[rows, near_at] = near_refs[part - 1][...]
        whole_ref[rows, far_at] = far_ref[part - 1]
    all_ref[...] = jnp.concatenate([ref[...] for ref in ctx_refs], axis=1)
    first_sum = hidden_ref[...].astype(F32) + dot_nn(all_ref[...], whole_ref[...])
    sum_ref[...] = first_sum
    normed = (first_sum * rms_scale(first_sum) * gain_ref[1:2, :]).astype(BF)
    packed_ref[...] = dot_nn(pack_ref[...], normed).astype(BF)
    lane = lax.broadcasted_iota(jnp.int32, gate_ref.shape, 1)
    logits = jnp.where(lane < experts, dot_nt(normed, router_ref[...]), F32(NEG))
    logits = jnp.exp(logits - jnp.max(logits, axis=1, keepdims=True))
    gate = jnp.sum(chosen_ref[...] * logits, axis=1, keepdims=True) / jnp.sum(
        logits, axis=1, keepdims=True
    )
    gate_ref[...] = jnp.broadcast_to(gate, gate_ref.shape)


def mix(where, hidden, near, far, weight, ctxs, gain, router, chosen, hot, experts):
    parts = len(ctxs)
    rows, width = hidden.shape
    inner = weight.shape[0]
    return pl.pallas_call(
        functools.partial(mix_kernel, parts, experts),
        out_shape=[
            jax.ShapeDtypeStruct((rows, width), F32),
            jax.ShapeDtypeStruct((rows, LANES), F32),
            jax.ShapeDtypeStruct((hot.shape[0], width), BF),
            jax.ShapeDtypeStruct((parts * inner, width), BF),
            jax.ShapeDtypeStruct((rows, parts * inner), BF),
        ],
        in_specs=[SMEM] + [VMEM] * (2 * parts + 6),
        out_specs=[VMEM] * 5,
        compiler_params=params(60),
        cost_estimate=cost(5e10, 1e4),
    )(where, hidden, *near, far, weight, *ctxs, gain, router, chosen, hot)


def expert_kernel(in_map, out_map, experts, where_ref, *refs):
    row_ref, cot_ref, router_ref = refs[:3]
    in_refs, out_refs = refs[3 : 3 + len(in_map)], refs[3 + len(in_map) : 3 + 2 * len(in_map)]
    back_ref, out_ref, gated_ref, logit_ref, near_hbm, far_hbm = refs[
        3 + 2 * len(in_map) : 9 + 2 * len(in_map)
    ]
    in_ref, outw_ref, near_ref, far_ref, total_ref, acc_ref, load_sems, store_sems = refs[
        9 + 2 * len(in_map) :
    ]
    units = len(in_map) // 2
    name = where_ref[3]
    slots, width = row_ref.shape
    span = in_refs[0].shape[1]
    hidden = units * span
    loads = []
    for unit in range(units):
        pieces = []
        for half in range(2):
            at = slice(half * span, (half + 1) * span)
            source = in_refs[in_map.index(unit + half * units)]
            pieces.append((source, in_ref.at[unit, :, at]))
            source = out_refs[out_map.index(unit + half * units)]
            pieces.append((source, outw_ref.at[unit, at, :]))
        copies = []
        for number, (source, target) in enumerate(pieces):
            copies.append(pltpu.make_async_copy(source, target, load_sems.at[unit, number]))
            copies[-1].start()
        loads.append(copies)
    rows_step = min(512, slots)
    tiles = [slice(at, at + rows_step) for at in range(0, slots, rows_step)]
    gates, routers = [], []
    lane = lax.broadcasted_iota(jnp.int32, (rows_step, LANES), 1)
    hot = (lane == name).astype(F32)
    for tile in tiles:
        logits = jnp.where(lane < experts, dot_nt(row_ref[tile, :], router_ref[...]), F32(NEG))
        logits = jnp.exp(logits - jnp.max(logits, axis=1, keepdims=True))
        router = logits / jnp.sum(logits, axis=1, keepdims=True)
        gate = jnp.sum(router * hot, axis=1, keepdims=True)
        gated = (cot_ref[tile, :].astype(F32) * gate).astype(BF)
        gated_ref[tile, :] = gated
        far_ref[tile, 2 * hidden :] = gated
        gates.append(gate)
        routers.append(router)
    stores = [
        pltpu.make_async_copy(
            far_ref.at[:, 2 * hidden :], far_hbm.at[:, 2 * hidden :], store_sems.at[units, 0]
        )
    ]
    stores[0].start()
    for unit in range(units):
        for copy in loads[unit]:
            copy.wait()
        for tile in tiles:
            pre_act = dot_nn(row_ref[tile, :], in_ref[unit])
            below = 0.5 + 0.5 * lax.erf(pre_act * F32(SQRT_HALF))
            active = (pre_act * below).astype(BF)
            slope = below + pre_act * jnp.exp(pre_act * pre_act * F32(-0.5)) * F32(INV_SQRT_TWO_PI)
            grad = (dot_nt(gated_ref[tile, :], outw_ref[unit]) * slope).astype(BF)
            for side_ref, half in ((near_ref, 0), (far_ref, 1)):
                at = slice(half * span, (half + 1) * span)
                side_ref[tile, unit * span : (unit + 1) * span] = active[:, at]
                side_ref[tile, hidden + unit * span : hidden + (unit + 1) * span] = grad[:, at]
            total = dot_nn(active, outw_ref[unit])
            back = dot_nt(grad, in_ref[unit])
            if unit:
                total_ref[tile, :] += total
                acc_ref[tile, :] += back
            else:
                total_ref[tile, :] = total
                acc_ref[tile, :] = back
        for number, (side_ref, side_hbm, first) in enumerate(
            (
                (near_ref, near_hbm, 0),
                (near_ref, near_hbm, hidden),
                (far_ref, far_hbm, 0),
                (far_ref, far_hbm, hidden),
            )
        ):
            at = slice(first + unit * span, first + (unit + 1) * span)
            copy = pltpu.make_async_copy(
                side_ref.at[:, at], side_hbm.at[:, at], store_sems.at[unit, number]
            )
            copy.start()
            stores.append(copy)
    for tile, gate, router in zip(tiles, gates, routers):
        total = total_ref[tile, :]
        gate_grad = jnp.sum(cot_ref[tile, :].astype(F32) * total, axis=1, keepdims=True)
        logit_grad = ((gate_grad * gate) * (hot - router)).astype(BF)
        logit_ref[tile, :] = logit_grad
        out_ref[tile, :] = total.astype(BF)
        back_ref[tile, :] = (acc_ref[tile, :] + dot_nn(logit_grad, router_ref[...])).astype(BF)
    for copy in stores:
        copy.wait()


def run_expert(where, rows, cots, in_parts, out_parts, in_map, out_map, router, experts):
    slots, width = rows.shape
    span = in_parts[0].shape[1]
    units = len(in_map) // 2
    hidden = 2 * units * span
    back, out, gated, logit, near, far = pl.pallas_call(
        functools.partial(expert_kernel, in_map, out_map, experts),
        out_shape=[
            jax.ShapeDtypeStruct((slots, width), BF),
            jax.ShapeDtypeStruct((slots, width), BF),
            jax.ShapeDtypeStruct((slots, width), BF),
            jax.ShapeDtypeStruct((slots, LANES), BF),
            jax.ShapeDtypeStruct((slots, hidden), BF),
            jax.ShapeDtypeStruct((slots, hidden + width), BF),
        ],
        in_specs=[SMEM] + [VMEM] * 3 + [ANY] * (len(in_parts) + len(out_parts)),
        out_specs=[VMEM] * 4 + [ANY] * 2,
        scratch_shapes=[
            pltpu.VMEM((units, width, 2 * span), BF),
            pltpu.VMEM((units, 2 * span, width), BF),
            pltpu.VMEM((slots, hidden), BF),
            pltpu.VMEM((slots, hidden + width), BF),
            pltpu.VMEM((slots, width), F32),
            pltpu.VMEM((slots, width), F32),
            pltpu.SemaphoreType.DMA((units, 4)),
            pltpu.SemaphoreType.DMA((units + 1, 4)),
        ],
        compiler_params=params(56),
        cost_estimate=cost(25e9, 20e6),
    )(where, rows, cots, router, *in_parts, *out_parts)
    return back, out, gated, near, far, logit


def weight_kernel(parts, row_ref, peer_ref, gated_ref, near_hbm, got_hbm, *refs):
    out_hbm = refs[: 2 * parts]
    both_ref, lhs_ref, tail_ref, done_ref, load_sems, store_sems = refs[2 * parts :]
    slots, width = row_ref.shape
    span = out_hbm[0].shape[1]
    hidden = parts * span
    chunk = 2 * span
    count = 2 * hidden // chunk
    tail = pltpu.make_async_copy(got_hbm.at[:, 2 * hidden :], tail_ref, load_sems.at[count, 0])
    loads = []
    order = list(range(count // 2, count)) + list(range(count // 2))
    for index in order:
        at = slice(index * chunk, (index + 1) * chunk)
        near = pltpu.make_async_copy(
            near_hbm.at[:, at], both_ref.at[0:slots, at], load_sems.at[index, 0]
        )
        got = pltpu.make_async_copy(
            got_hbm.at[:, at], both_ref.at[slots:, at], load_sems.at[index, 1]
        )
        near.start()
        got.start()
        loads.append((near, got))
        if index == count - 1:
            tail.start()
    lhs_ref[0, :, 0:slots] = jnp.transpose(row_ref[...])
    lhs_ref[0, :, slots:] = jnp.transpose(peer_ref[...])
    stores = []
    for number, index in enumerate(order):
        inward = index >= count // 2
        if number == count // 2:
            tail.wait()
            lhs_ref[1, :, 0:slots] = jnp.transpose(gated_ref[...])
            lhs_ref[1, :, slots:] = jnp.transpose(tail_ref[...])
        for copy in loads[number]:
            copy.wait()
        at = slice(index * chunk, (index + 1) * chunk)
        done_ref[number] = dot_nn(lhs_ref[0 if inward else 1], both_ref[:, at]).astype(BF)
        for half in range(2):
            part = 2 * (index % (count // 2)) + half
            copy = pltpu.make_async_copy(
                done_ref.at[number, :, half * span : (half + 1) * span],
                out_hbm[part if inward else parts + part],
                store_sems.at[number, half],
            )
            copy.start()
            stores.append(copy)
    for copy in stores:
        copy.wait()


def weight_grads(where, rows, rows_peer, gated, near, got, parts):
    slots, width = rows.shape
    span = near.shape[1] // (2 * parts)
    one = jax.ShapeDtypeStruct((width, span), BF)
    outs = pl.pallas_call(
        functools.partial(weight_kernel, parts),
        out_shape=[one] * (2 * parts),
        in_specs=[VMEM] * 3 + [ANY] * 2,
        out_specs=[ANY] * (2 * parts),
        scratch_shapes=[
            pltpu.VMEM((2 * slots, 2 * parts * span), BF),
            pltpu.VMEM((2, width, 2 * slots), BF),
            pltpu.VMEM((slots, width), BF),
            pltpu.VMEM((parts, width, 2 * span), BF),
            pltpu.SemaphoreType.DMA((parts + 1, 2)),
            pltpu.SemaphoreType.DMA((parts, 2)),
        ],
        compiler_params=params(60),
        cost_estimate=cost(1e10, 1e6),
    )(rows, rows_peer, gated, near, got)
    return outs[:parts], outs[parts:]


def finish_kernel(where_ref, *refs):
    core = where_ref[2]
    in_ref, out_ref = refs[4:]
    span = refs[0].shape[1]
    for half in range(2):
        own_in, own_out = refs[2 * half : 2 * half + 2]
        at = pl.ds(pl.multiple_of((core ^ half) * span, LANES), span)
        in_ref[:, at] = own_in[...].astype(F32)
        out_ref[at, :] = jnp.transpose(own_out[...].astype(F32))


def finish(where, mine, peer):
    width, span = mine[0].shape
    return pl.pallas_call(
        finish_kernel,
        out_shape=[
            jax.ShapeDtypeStruct((width, 2 * span), F32),
            jax.ShapeDtypeStruct((2 * span, width), F32),
        ],
        in_specs=[SMEM] + [VMEM] * 4,
        out_specs=[VMEM, VMEM],
        compiler_params=params(40),
        cost_estimate=cost(5e+10, 1e4),
    )(where, *mine, *peer)


def residual_kernel(parts, where_ref, *refs):
    home_ref, hot_ref, sum_ref, cot_ref, gain_ref = refs[:5]
    weight_ref, all_ref, grad_ref, gain_out_ref, give_ref = refs[5:10]
    ctx_refs, keep_refs = refs[10 : 10 + parts], refs[10 + parts :]
    core = where_ref[2]
    side = grad_ref.shape[1] // 2
    upstream = dot_nn(hot_ref[...], home_ref[...])
    first_sum = sum_ref[...]
    inverse = rms_scale(first_sum)
    gain_out_ref[...] = jnp.broadcast_to(
        jnp.sum(upstream * first_sum * inverse, axis=0, keepdims=True), gain_out_ref.shape
    )
    grad = cot_ref[...].astype(F32) + norm_back(first_sum, inverse, gain_ref[1:2, :], upstream)
    grad_ref[...] = grad
    low = grad.astype(BF)
    inner = weight_ref.shape[0] // parts
    across = dot_nt(low, weight_ref[...]).astype(BF)
    for part in range(parts):
        ctx_refs[part][...] = across[:, part * inner : (part + 1) * inner]
    product = dot_tn(all_ref[...], low)
    for part in range(parts):
        rows = slice(part * inner, (part + 1) * inner)

        @pl.when(core == 0)
        def _(part=part, rows=rows):
            keep_refs[part][...] = product[rows, :side]
            give_ref[part] = product[rows, side:].astype(BF)

        @pl.when(core != 0)
        def _(part=part, rows=rows):
            keep_refs[part][...] = product[rows, side:]
            give_ref[part] = product[rows, :side].astype(BF)


def residual(where, home, hot, first_sum, cot, gain, weight, every, parts):
    rows, width = first_sum.shape
    inner = weight.shape[0] // parts
    return pl.pallas_call(
        functools.partial(residual_kernel, parts),
        out_shape=[
            jax.ShapeDtypeStruct((rows, width), F32),
            jax.ShapeDtypeStruct((8, width), F32),
            jax.ShapeDtypeStruct((parts, inner, width // 2), BF),
        ]
        + [jax.ShapeDtypeStruct((rows, inner), BF)] * parts
        + [jax.ShapeDtypeStruct((inner, width // 2), F32)] * parts,
        in_specs=[SMEM] + [VMEM] * 7,
        out_specs=[VMEM] * (3 + 2 * parts),
        compiler_params=params(60),
        cost_estimate=cost(2e+11, 1e4),
    )(where, home, hot, first_sum, cot, gain, weight, every)


def attend_back_kernel(parts, heads, where_ref, *refs):
    cot_refs, refs = refs[:parts], refs[parts:]
    ctx_ref, proj_ref, normed_ref, lse_ref, weight_ref, offset_ref = refs[:6]
    scale_ref, small_ref, moe_ref, table_ref = refs[6:10]
    send_ref, bias_ref, keep_ref, give_ref = refs[10:14]
    skew_ref, fold_ref, cot_ref, dproj_ref, key_acc, value_acc = refs[14:]
    quarter = ctx_ref.shape[1]
    for part in range(parts):
        cot_ref[where_ref[0] ^ part] = cot_refs[part][...]
    length = quarter * parts
    inner = weight_ref.shape[0] // 3
    head_dim = inner // heads
    prefix, core = where_ref[1], where_ref[2]
    skew_into(skew_ref, offset_ref, heads, 2 * length)
    fold_ref[...] = jnp.zeros_like(fold_ref)
    key_acc[...] = jnp.zeros_like(key_acc)
    value_acc[...] = jnp.zeros_like(value_acc)
    keys_across = jnp.transpose(proj_ref[:, inner : 2 * inner])
    head_row = lax.broadcasted_iota(jnp.int32, (8, inner), 0)
    head_lane = lax.broadcasted_iota(jnp.int32, (8, inner), 1)
    picks = (head_lane // head_dim == head_row).astype(BF)
    for block in range(parts):
        first = block * quarter
        reach = max(length // 2, first + quarter)
        key_pos = first + lax.broadcasted_iota(jnp.int32, (reach - first, quarter), 0)
        query_pos = first + lax.broadcasted_iota(jnp.int32, (reach - first, quarter), 1)
        allowed = (key_pos <= query_pos) | (key_pos < prefix)
        product = cot_ref[block].astype(F32) * ctx_ref[block].astype(F32)
        high = product.astype(BF)
        rest = (product - high.astype(F32)).astype(BF)
        inner_sum = dot_nt(picks, high) + dot_nt(picks, rest)
        query_pieces = []
        for head in range(heads):
            low = head * head_dim
            query = proj_ref[first : first + quarter, low : low + head_dim]
            keys = proj_ref[0:reach, inner + low : inner + low + head_dim]
            values = proj_ref[0:reach, 2 * inner + low : 2 * inner + low + head_dim]
            grad = cot_ref[block, :, low : low + head_dim]
            bias = jnp.concatenate(
                [
                    skew_ref[
                        head,
                        :,
                        first - LANES * sub + length - LANES : first
                        - LANES * sub
                        + length
                        - LANES
                        + quarter,
                    ]
                    for sub in range(reach // LANES)
                ],
                axis=0,
            )
            scores = dot_nt(keys, query) + bias
            tail = jnp.where(allowed, scores[first:], F32(NEG))
            scores = jnp.concatenate([scores[:first], tail], axis=0) if first else tail
            probs = jnp.exp(scores - lse_ref[block, head : head + 1, :])
            prob_grad = dot_nt(values, grad)
            score_grad = (probs * (prob_grad - inner_sum[head : head + 1, :])).astype(BF)
            wide = score_grad.astype(F32)
            for sub in range(reach // LANES):
                column = first - LANES * sub + length - LANES
                fold_ref[head, :, column : column + quarter] += wide[
                    LANES * sub : LANES * (sub + 1)
                ]
            value_acc[head, 0:reach, :] += dot_nn(probs.astype(BF), grad)
            key_acc[head, 0:reach, :] += dot_nn(score_grad, query)
            query_pieces.append(dot_nn(keys_across[low : low + head_dim, 0:reach], score_grad))
        query_grad = jnp.transpose(jnp.concatenate(query_pieces, axis=0)) * F32(head_dim ** (-0.5))
        dproj_ref[first : first + quarter, 0:inner] = query_grad.astype(BF)
    dproj_ref[:, inner : 3 * inner] = jnp.concatenate(
        [key_acc[head] for head in range(heads)] + [value_acc[head] for head in range(heads)],
        axis=1,
    ).astype(BF)
    width = normed_ref.shape[1]
    side = width // 2
    split, piece, _ = keep_ref.shape
    layer = where_ref[3]
    grad_rows = dot_nn(jnp.transpose(dproj_ref[...]), normed_ref[...])
    for half in range(2):
        for part in range(split):
            chunk = grad_rows[part * piece : (part + 1) * piece, half * side : (half + 1) * side]
            slot = (layer ^ part) if split > 1 else part

            @pl.when(core == half)
            def _(chunk=chunk, slot=slot):
                keep_ref[slot] = chunk

            @pl.when(core != half)
            def _(chunk=chunk, slot=slot):
                give_ref[slot] = chunk.astype(BF)

    gain_sum = jnp.zeros((1, width), F32)
    for block in range(parts):
        rows = slice(block * quarter, (block + 1) * quarter)
        upstream = dot_nn(dproj_ref[rows, :], weight_ref[...])
        gain_sum = gain_sum + jnp.sum(
            upstream * normed_ref[rows, :].astype(F32), axis=0, keepdims=True
        )
        send_ref[block, 0:quarter, :] = upstream.astype(BF)
    extra = small_ref.shape[0]
    row = lax.broadcasted_iota(jnp.int32, small_ref.shape, 0)
    small = jnp.where(row == 1, moe_ref[0:1, :], small_ref[...])
    small = jnp.where(row == 0, gain_sum / scale_ref[0:1, :], small).astype(BF)
    share = width // parts
    for block in range(parts):
        send_ref[block, quarter:, 0:share] = small[:, block * share : (block + 1) * share]
        send_ref[block, quarter:, share:] = jnp.zeros((extra, width - share), BF)
    row_index = lax.broadcasted_iota(jnp.int32, (LANES, 2 * length), 0)
    buckets = (row_index == table_ref[1:2, :]).astype(BF)
    sums = []
    for head in range(heads):
        tile = fold_ref[head, 0:8, :]
        for group in range(8, LANES, 8):
            tile = tile + pltpu.roll(fold_ref[head, group : group + 8, :], 2 * length - group, 1)
        for bit in range(3):
            moved = pltpu.roll(tile, 2 * length - (1 << bit), 1)
            tile = jnp.where(((row_index[0:8] >> bit) & 1) == 1, moved, tile)
        tile = pltpu.roll(tile, LANES - 1, 1)
        sums.append(jnp.sum(tile, axis=0, keepdims=True))
    rest = jnp.concatenate(sums + [jnp.zeros((8 - heads, 2 * length), F32)], axis=0)
    levels = []
    for _ in range(3):
        high = rest.astype(BF).astype(F32)
        rest = rest - high
        levels.append(high)
    total = dot_nt(jnp.concatenate(levels, axis=0).astype(BF), buckets)
    total = total[0:8] + total[8:16] + total[16:24]
    bias_ref[0:8, :] = total
    bias_ref[8:, :] = jnp.zeros((bias_ref.shape[0] - 8, LANES), F32)


def attend_back(
    where, cots, ctxs, proj, normed, lse, weight, offsets, scale, small, moe, tables, heads, split
):
    parts, quarter, inner = ctxs.shape
    width = normed.shape[1]
    length = parts * quarter
    return pl.pallas_call(
        functools.partial(attend_back_kernel, parts, heads),
        out_shape=[
            jax.ShapeDtypeStruct((parts, quarter + small.shape[0], width), BF),
            jax.ShapeDtypeStruct((small.shape[0], LANES), F32),
            jax.ShapeDtypeStruct((split, 3 * inner // split, width // 2), F32),
            jax.ShapeDtypeStruct((split, 3 * inner // split, width // 2), BF),
        ],
        in_specs=[SMEM] + [VMEM] * (10 + parts),
        out_specs=[VMEM] * 4,
        scratch_shapes=[
            pltpu.VMEM((heads, LANES, 2 * length), F32),
            pltpu.VMEM((heads, LANES, 2 * length), F32),
            pltpu.VMEM((parts, quarter, inner), BF),
            pltpu.VMEM((length, 3 * inner), BF),
            pltpu.VMEM((heads, length, inner // heads), F32),
            pltpu.VMEM((heads, length, inner // heads), F32),
        ],
        compiler_params=params(60),
        cost_estimate=cost(5e+10, 1e4),
    )(where, *cots, ctxs, proj, normed, lse, weight, offsets, scale, small, moe, tables)


def merge_kernel(parts, where_ref, keep_ref, got_ref, *refs):
    wo_refs, (home_ref, hot_ref, sum_ref, gate_ref) = refs[:parts], refs[parts : parts + 4]
    layer_ref, send_refs, wo_ref = refs[parts + 4], refs[parts + 5 : -1], refs[-1]
    split, piece, side = keep_ref.shape
    share = wo_ref.shape[0] // split
    layer = where_ref[3]
    total = wo_refs[0][...] + wo_refs[1][0].astype(F32)
    for part in range(2, parts):
        total = total + wo_refs[part][...].astype(F32)
    wo_ref[...] = total
    expert_out = dot_nn(hot_ref[...], home_ref[...])
    layer_ref[...] = (sum_ref[...] + gate_ref[:, 0:1] * expert_out).astype(BF)
    for part in range(split):
        send_refs[part][0:piece, :] = (keep_ref[part] + got_ref[part].astype(F32)).astype(BF)
        row = (layer ^ part) * share if split > 1 else 0
        send_refs[part][piece:, :] = wo_ref[pl.ds(pl.multiple_of(row, 8), share), :].astype(BF)


def merge(where, keep, got, wos, home, hot, first_sum, gate):
    split, piece, side = keep.shape
    rows = wos[0].shape[0]
    shape = jax.ShapeDtypeStruct((piece + rows // split, side), BF)
    return pl.pallas_call(
        functools.partial(merge_kernel, len(wos)),
        out_shape=[jax.ShapeDtypeStruct(first_sum.shape, BF)] + [shape] * split,
        in_specs=[SMEM] + [VMEM] * (6 + len(wos)),
        out_specs=[VMEM] * (1 + split),
        scratch_shapes=[pltpu.VMEM((rows, side), F32)],
        compiler_params=params(60),
        cost_estimate=cost(1e+06, 1e4),
    )(where, keep, got, *wos, home, hot, first_sum, gate)


def assemble_kernel(where_ref, *refs):
    *piece_refs, qkv_ref, wo_ref, first_ref, second_ref, router_ref, bias_ref, parts_ref = refs
    split = len(piece_refs) // 2
    side = qkv_ref.shape[1] // 2
    piece, share = qkv_ref.shape[0] // split, wo_ref.shape[0] // split
    core, layer = where_ref[2], where_ref[3]
    for part in range(split):
        slot = (layer ^ part) if split > 1 else 0
        for half in range(2):
            ref = piece_refs[half * split + part]
            at = pl.ds(pl.multiple_of((core ^ half) * side, LANES), side)
            values = ref[...].astype(F32)
            qkv_ref[pl.ds(pl.multiple_of(slot * piece, 8), piece), at] = values[0:piece]
            wo_ref[pl.ds(pl.multiple_of(slot * share, 8), share), at] = values[
                piece : piece + share
            ]
            parts_ref[(core ^ half) * split + slot] = values[piece + share :]
    total = parts_ref[0]
    for part in range(1, 2 * split):
        total = total + parts_ref[part]
    share = first_ref.shape[1]
    first_ref[...] = total[0:1, 0:share]
    second_ref[...] = total[1:2, 0:share]
    router_ref[...] = total[2 : 2 + router_ref.shape[0], 0:share]
    bias_ref[...] = total[0 : bias_ref.shape[0], share : share + bias_ref.shape[1]]


def assemble(where, pieces, rows, extra, width, experts, heads, buckets):
    split = len(pieces) // 2
    both, side = pieces[0].shape
    return pl.pallas_call(
        assemble_kernel,
        out_shape=[
            jax.ShapeDtypeStruct((rows, 2 * side), F32),
            jax.ShapeDtypeStruct((split * (both - extra) - rows, 2 * side), F32),
            jax.ShapeDtypeStruct((1, width), F32),
            jax.ShapeDtypeStruct((1, width), F32),
            jax.ShapeDtypeStruct((experts, width), F32),
            jax.ShapeDtypeStruct((heads, buckets), F32),
        ],
        in_specs=[SMEM] + [VMEM] * (2 * split),
        out_specs=[VMEM] * 6,
        scratch_shapes=[pltpu.VMEM((2 * split, extra, side), F32)],
        compiler_params=params(16),
        cost_estimate=cost(1e+06, 1e4),
    )(where, *pieces)


def trade(values, axis):
    return lax.all_to_all(values, axis, split_axis=0, concat_axis=0, tiled=True)


def after(values, others):
    return lax.optimization_barrier((values, others))[0]


def body(
    hidden_in,
    cotangent,
    attn_gain,
    query_key_value_weight,
    attention_output_weight,
    rel_bias,
    bucket_table,
    prefix_len,
    moe_gain,
    w_router,
    routes,
    w_expert_in,
    w_expert_out,
):
    seq_count, quarter, model_width = hidden_in.shape
    parts = lax.axis_size("tensor")
    layers = lax.axis_size("expert")
    row_count = seq_count * quarter
    experts = w_router.shape[1]
    capacity = max(2, 2 * row_count // experts)
    slot_count = experts * capacity
    heads, buckets = rel_bias.shape
    inner = query_key_value_weight.shape[2]
    span = w_expert_in.shape[2] // 2
    place, layer, core = lax.axis_index("tensor"), lax.axis_index("expert"), lax.axis_index("dp")
    where = jnp.stack([place, prefix_len[0], core, layer]).astype(jnp.int32)
    low_core = core == 0

    own_hidden = hidden_in[0]
    own_cot = cotangent[0]

    chosen = routes.reshape(1, row_count)
    tables = jnp.stack([bucket_table, jnp.flip(bucket_table)])
    tables = jnp.pad(tables, ((0, 0), (0, 1)), constant_values=-1)
    gains = jnp.stack([attn_gain, moe_gain]).astype(F32)
    pack_hot, unpack_hot, cot_packed, chosen_hot, offset_bias, offset_back, router = prepare(
        chosen, own_cot, tables, rel_bias, w_router.T, capacity
    )

    def over_experts(packed):
        packed = packed.reshape(experts, capacity, model_width)
        return trade(packed, "expert").reshape(slot_count, model_width)

    cot_slots = over_experts(cot_packed)

    hidden_blocks = [own_hidden] + [swap(own_hidden, "tensor", k) for k in range(1, parts)]
    weight = query_key_value_weight.transpose(1, 2, 0).reshape(3 * inner, model_width)
    side = model_width // 2
    own_weight = lax.dynamic_slice(attention_output_weight, (0, core * side), (inner, side))
    late_weight = after(own_weight, hidden_blocks)
    out_weights = [
        swap(late_weight, "tensor", k) for k in range(1, parts)
    ]
    first_blocks, prepared = lax.optimization_barrier(
        (hidden_blocks, (own_weight, pack_hot, unpack_hot, chosen_hot, router, offset_bias,
                         offset_back, where, gains))
    )
    _, pack_hot, unpack_hot, chosen_hot, router, offset_bias, offset_back, where, gains = (
        prepared
    )
    normed_one, projected, lse, contexts, sends = attend(
        where, first_blocks, gains, weight, offset_bias, heads
    )

    in_own = lax.dynamic_slice(w_expert_in[0], (0, core * span), (model_width, span))
    out_own = lax.dynamic_slice(w_expert_out[0], (core * span, 0), (span, model_width))
    in_other = lax.dynamic_slice(w_expert_in[0], (0, (1 - core) * span), (model_width, span))
    out_other = lax.dynamic_slice(w_expert_out[0], ((1 - core) * span, 0), (span, model_width))
    in_own, out_own = after((in_own, out_own), hidden_blocks)
    in_step, out_step = swap(in_own, "tensor", 1), swap(out_own, "tensor", 2)
    far_weights = swap(jnp.stack(after(out_weights, sends)), "dp", 1)
    sends = after(sends, far_weights)
    own_contexts = [sends[0]] + [swap(sends[k], "tensor", k) for k in range(1, parts)]


    in_next, out_next = after((in_own, out_own), own_contexts[1])
    in_next, out_next = swap(in_next, "tensor", 2), swap(out_next, "tensor", 1)
    in_far, out_far = after((in_step, out_step), (own_contexts, in_next, out_next))
    in_far, out_far = swap(in_far, "tensor", 2), swap(out_far, "tensor", 1)
    in_near, in_order = [in_own, in_step, in_next, in_far], (0, 1, 2, 3)
    out_near, out_order = [out_own, out_step, out_next, out_far], (0, 2, 1, 3)
    in_map = in_order + tuple(parts + unit for unit in in_order)
    out_map = out_order + tuple(parts + unit for unit in out_order)

    first_sum, gate, packed, whole_weight, every_context = mix(
        where, own_hidden, out_weights, far_weights, attention_output_weight,
        after(own_contexts, (cot_slots, in_step, out_step)), gains, router, chosen_hot, pack_hot,
        experts,
    )
    row_slots = over_experts(packed)

    def cross(pieces):
        _, near, near_too, far = pieces
        far = after(far, row_slots)
        return [swap(near, "dp", 1), swap(near_too, "dp", 1), swap(far, "dp", 1)]

    in_parts = in_near + [in_other] + cross(in_near)
    out_parts = out_near + [out_other] + cross(out_near)
    rows_peer = swap(row_slots, "dp", 1)
    back_slots, out_slots, gated, near, far, logit_grad = run_expert(
        where, row_slots, cot_slots, in_parts, out_parts, in_map, out_map, router, experts
    )
    back_home = over_experts(back_slots)

    in_sums, out_sums = partial = weight_grads(
        where, row_slots, rows_peer, gated, near, swap(far, "dp", 1), parts
    )
    in_skip, out_skip = swap(in_sums[3], "tensor", 1), swap(out_sums[3], "tensor", 2)

    def plus(*terms):
        total = terms[0].astype(F32)
        for term in terms[1:]:
            total = total + term.astype(F32)
        return total.astype(BF)


    residual_grad, moe_gain_part, wo_give, *cots = residual(
        where, after(back_home, partial), unpack_hot, first_sum, own_cot, gains, whole_weight,
        every_context, parts,
    )
    cots, wo_keep = cots[:parts], cots[parts:]
    context_cots = [cots[0]] + [swap(cots[k], "tensor", k) for k in range(1, parts)]

    wo_got = swap(wo_give, "dp", 1)
    out_home = over_experts(after(out_slots, wo_got))
    wo_low = [(wo_keep[k] + wo_got[k].astype(F32)).astype(BF) for k in range(1, parts)]
    context_cots = after(context_cots, (wo_low, in_skip, out_skip))
    in_side, out_side = after((in_sums[1], out_sums[2]), (in_skip, out_skip))
    in_side, out_side = swap(in_side, "tensor", 1), swap(out_side, "tensor", 2)
    wo_parts = [wo_keep[0], wo_got] + [
        swap(wo_low[k - 1], "tensor", k) for k in range(1, parts)
    ]

    split = layers if layers == 4 else 1
    router_part = dot_tn(logit_grad, row_slots)[:experts]
    extra = -(-(experts + 2) // 16) * 16
    small = jnp.pad(router_part, ((2, extra - 2 - experts), (0, 0)))
    send_ups, bias_part, keep, give = attend_back(
        where, context_cots, contexts, projected, normed_one, lse, weight, offset_back,
        gains, small, moe_gain_part, tables, heads, split,
    )
    send_ups, give = after((send_ups, give), (wo_parts, out_home, in_side, out_side))
    ups = jnp.sum(trade(send_ups, "tensor").astype(F32), axis=0)
    own_float = own_hidden.astype(F32)
    inverse_own = rms_scale(own_float)
    input_grad = residual_grad + norm_back(own_float, inverse_own, gains[0:1], ups[:quarter])

    share = model_width // parts
    bias_part = jnp.pad(bias_part, ((0, 0), (0, side - share - LANES)))
    small = jnp.concatenate([ups[quarter:, :share], bias_part], axis=1)
    layer_out, *sends = merge(
        where, keep, swap(give, "dp", 1), wo_parts, out_home, unpack_hot, first_sum, gate
    )
    piece = sends[0].astype(F32)
    first = sends[-1]
    if split > 1:
        arrived = [swap(sends[k], "expert", k) for k in range(1, layers)]
        first = arrived[0]
        for value in arrived:
            piece = piece + value.astype(F32)
    in_skip, out_skip, in_side, out_side = after((in_skip, out_skip, in_side, out_side), first)
    in_pass, out_pass = plus(in_sums[2], in_skip), plus(out_sums[1], out_skip)
    in_last, out_last = swap(in_pass, "tensor", 2), swap(out_pass, "tensor", 1)
    if split > 1:
        piece = jnp.concatenate([piece, small], axis=0).astype(BF)
        pieces = [piece] + [swap(piece, "expert", k) for k in range(1, layers)]
    else:
        pieces = [lax.psum(jnp.concatenate([piece, small], axis=0), "expert")]
    in_last, out_last = after((in_last, out_last), pieces[:2])
    mine = (plus(in_sums[0], in_side, in_last), plus(out_sums[0], out_side, out_last))
    expert_in_grad, expert_out_grad = finish(where, mine, [swap(x, "dp", 1) for x in mine])
    pieces = pieces + [swap(x, "dp", 1) for x in pieces]
    done = (layer_out, expert_in_grad, expert_out_grad, input_grad)
    pieces, done = lax.optimization_barrier((pieces, done))
    layer_out, expert_in_grad, expert_out_grad, input_grad = done
    qkv_across, attn_out_grad, gain_one, gain_two, router_grad, bias_grad = assemble(
        where, pieces, 3 * inner, extra, share, experts, heads, buckets
    )
    qkv_grad = qkv_across.reshape(3, inner, model_width).transpose(2, 0, 1)
    return (
        layer_out.reshape(seq_count, quarter, model_width),
        input_grad.reshape(seq_count, quarter, model_width),
        gain_one[0],
        qkv_grad,
        attn_out_grad,
        bias_grad,
        gain_two[0],
        router_grad.T,
        expert_in_grad[None],
        expert_out_grad[None],
    )


def solution(mesh):
    placed = (
        P(("dp", "expert"), "tensor", None),
        P(("dp", "expert"), "tensor", None),
        P(),
        P(None, None, "tensor"),
        P("tensor", None),
        P("tensor", None),
        P(),
        P(("dp", "expert")),
        P(),
        P(),
        P(("dp", "expert"), "tensor", None, None, None),
        P("expert", None, "tensor"),
        P("expert", "tensor", None),
    )
    return jax.shard_map(
        body,
        mesh=mesh,
        in_specs=placed,
        out_specs=(
            P(("dp", "expert"), "tensor", None),
            P(("dp", "expert"), "tensor", None),
            P("tensor"),
            P(None, None, "tensor"),
            P("tensor", None),
            P("tensor", None),
            P("tensor"),
            P("tensor", None),
            P("expert", None, "tensor"),
            P("expert", "tensor", None),
        ),
        check_vma=False,
    )
```

```python
import functools

import jax
import jax.numpy as jnp
from jax import lax
from jax.experimental import pallas as pl
from jax.experimental.pallas import tpu as pltpu
from jax.sharding import PartitionSpec as P

EPSILON = 1e-06
NEG = -1e30
TOP_PRECISION = lax.Precision.HIGHEST
BF = jnp.bfloat16
F32 = jnp.float32
LANES = 128
VMEM = pl.BlockSpec()
ANY = pl.BlockSpec(memory_space=pltpu.HBM)
SMEM = pl.BlockSpec(memory_space=pltpu.SMEM)
SQRT_HALF = 0.7071067811865476
INV_SQRT_TWO_PI = 0.3989422804014327


def params(mib):
    return pltpu.CompilerParams(vmem_limit_bytes=mib * 1024 * 1024)


def cost(flops, moved):
    return pl.CostEstimate(flops=int(flops), bytes_accessed=int(moved), transcendentals=0)


def dot_nn(a, b):
    return lax.dot_general(a, b, (((1,), (0,)), ((), ())), preferred_element_type=F32)


def dot_nt(a, b):
    return lax.dot_general(a, b, (((1,), (1,)), ((), ())), preferred_element_type=F32)


def dot_tn(a, b):
    return lax.dot_general(a, b, (((0,), (0,)), ((), ())), preferred_element_type=F32)


def rms_scale(values):
    return lax.rsqrt(jnp.mean(values * values, axis=-1, keepdims=True) + EPSILON)


def norm_back(values, inverse, gain_vec, upstream):
    scaled = upstream * gain_vec
    return inverse * scaled - values * (inverse * inverse * inverse) * jnp.mean(
        scaled * values, axis=-1, keepdims=True
    )


def swap(values, axis, step):
    count = lax.axis_size(axis)
    return lax.ppermute(values, axis, [(i, i ^ step) for i in range(count)])


def skew_into(skew_ref, offset_ref, heads, width):
    for head in range(heads):
        row = jnp.broadcast_to(offset_ref[head : head + 1, :], (LANES, width))
        skew_ref[head] = pltpu.roll(row, width - (LANES - 1), 1, stride=1, stride_axis=0)


def attend_kernel(parts, heads, where_ref, *refs):
    x_refs = refs[:parts]
    gain_ref, weight_ref, offset_ref = refs[parts : parts + 3]
    normed_ref, proj_ref, lse_ref, ctx_ref = refs[parts + 3 : parts + 7]
    send_refs, skew_ref = refs[parts + 7 : 2 * parts + 7], refs[2 * parts + 7]
    quarter = x_refs[0].shape[0]
    length = quarter * parts
    inner = weight_ref.shape[0] // 3
    head_dim = inner // heads
    place, prefix = where_ref[0], where_ref[1]
    lane = lax.broadcasted_iota(jnp.int32, (1, 3 * inner), 1)
    column_scale = jnp.where(lane < inner, F32(head_dim ** (-0.5)), F32(1.0))
    for part in range(parts):
        x = x_refs[part][...].astype(F32)
        normed = (x * rms_scale(x) * gain_ref[0:1, :]).astype(BF)
        rows = pl.ds(pl.multiple_of((place ^ part) * quarter, quarter), quarter)
        normed_ref[rows, :] = normed
        proj_ref[rows, :] = (dot_nt(normed, weight_ref[...]) * column_scale).astype(BF)
    skew_into(skew_ref, offset_ref, heads, 2 * length)
    tiles = length // LANES
    per_block = quarter // LANES
    for block in range(parts):
        first = block * quarter
        reach = max(length // 2, first + quarter)
        key_pos = first + lax.broadcasted_iota(jnp.int32, (quarter, reach - first), 1)
        query_pos = first + lax.broadcasted_iota(jnp.int32, (quarter, reach - first), 0)
        allowed = (key_pos <= query_pos) | (key_pos < prefix)
        pieces, logs = [], []
        for head in range(heads):
            low = head * head_dim
            query = proj_ref[first : first + quarter, low : low + head_dim]
            keys = proj_ref[0:reach, inner + low : inner + low + head_dim]
            values = proj_ref[0:reach, 2 * inner + low : 2 * inner + low + head_dim]
            bias = jnp.concatenate(
                [
                    skew_ref[
                        head,
                        :,
                        LANES * (tiles - 1 - block * per_block - sub) : LANES
                        * (tiles - 1 - block * per_block - sub)
                        + reach,
                    ]
                    for sub in range(per_block)
                ],
                axis=0,
            )
            scores = dot_nt(query, keys) + bias
            tail = jnp.where(allowed, scores[:, first:], F32(NEG))
            scores = jnp.concatenate([scores[:, :first], tail], axis=1) if first else tail
            peak = jnp.max(scores, axis=1, keepdims=True)
            exponent = jnp.exp(scores - peak)
            total = jnp.sum(exponent, axis=1, keepdims=True)
            pieces.append(dot_nn(exponent.astype(BF), values) / total)
            logs.append(jnp.broadcast_to(peak + jnp.log(total), (quarter, LANES)))
        ctx_ref[block] = jnp.concatenate(pieces, axis=1).astype(BF)
        lane_row = lax.broadcasted_iota(jnp.int32, (quarter, LANES), 1)
        stacked = logs[0]
        for head in range(1, heads):
            stacked = jnp.where(lane_row == head, logs[head], stacked)
        lse_ref[block] = jnp.transpose(stacked)[0:8, :]
    for part in range(parts):
        send_refs[part][...] = ctx_ref[place ^ part]


def attend(where, blocks, gain, weight, offsets, heads):
    parts = len(blocks)
    quarter, width = blocks[0].shape
    length = parts * quarter
    inner3 = weight.shape[0]
    outs = pl.pallas_call(
        functools.partial(attend_kernel, parts, heads),
        out_shape=[
            jax.ShapeDtypeStruct((length, width), BF),
            jax.ShapeDtypeStruct((length, inner3), BF),
            jax.ShapeDtypeStruct((parts, 8, quarter), F32),
            jax.ShapeDtypeStruct((parts, quarter, inner3 // 3), BF),
        ]
        + [jax.ShapeDtypeStruct((quarter, inner3 // 3), BF)] * parts,
        in_specs=[SMEM] + [VMEM] * (parts + 3),
        out_specs=[VMEM] * (4 + parts),
        scratch_shapes=[pltpu.VMEM((heads, LANES, 2 * length), F32)],
        compiler_params=params(60),
        cost_estimate=cost(5e+10, 1e4),
    )(where, *blocks, gain, weight, offsets)
    return outs[0], outs[1], outs[2], outs[3], outs[4:]


def prepare_kernel(experts, capacity, chosen_ref, cot_ref, table_ref, bias_ref, router_in_ref, *outs):
    pack_ref, unpack_ref, packed_ref, hot_ref, offset_ref, back_ref, router_ref = outs
    slots, rows = pack_ref.shape
    chosen = chosen_ref[...]
    hot = (lax.broadcasted_iota(jnp.int32, (LANES, rows), 0) == chosen).astype(F32)
    earlier = lax.broadcasted_iota(jnp.int32, (rows, rows), 0)
    later = lax.broadcasted_iota(jnp.int32, (rows, rows), 1)
    before = dot_nn(hot.astype(BF), (earlier < later).astype(BF))
    slot = jnp.sum(before * hot, axis=0, keepdims=True)
    target = chosen * capacity + slot.astype(jnp.int32)
    pack = (lax.broadcasted_iota(jnp.int32, (slots, rows), 0) == target).astype(F32)
    pack_ref[...] = pack.astype(BF)
    unpack_ref[...] = jnp.transpose(pack).astype(BF)
    hot_ref[...] = jnp.transpose(hot)
    packed_ref[...] = dot_nn(pack.astype(BF), cot_ref[...]).astype(BF)
    heads, buckets = bias_ref.shape
    length = table_ref.shape[1]
    for row, out in ((0, offset_ref), (1, back_ref)):
        table = lax.broadcasted_iota(jnp.int32, (buckets, length), 0) == table_ref[row : row + 1, :]
        out[0:heads, :] = dot_nn(bias_ref[...], table.astype(BF))
        out[heads:, :] = jnp.zeros((8 - heads, length), F32)
    router_ref[...] = jnp.zeros_like(router_ref)
    router_ref[0:experts, :] = router_in_ref[...]


def prepare(chosen, cot, tables, bias, router, capacity):
    experts, width = router.shape
    rows = chosen.shape[1]
    slots = experts * capacity
    return pl.pallas_call(
        functools.partial(prepare_kernel, experts, capacity),
        out_shape=[
            jax.ShapeDtypeStruct((slots, rows), BF),
            jax.ShapeDtypeStruct((rows, slots), BF),
            jax.ShapeDtypeStruct((slots, width), BF),
            jax.ShapeDtypeStruct((rows, LANES), F32),
            jax.ShapeDtypeStruct((8, tables.shape[1]), F32),
            jax.ShapeDtypeStruct((8, tables.shape[1]), F32),
            jax.ShapeDtypeStruct((LANES, width), BF),
        ],
        in_specs=[VMEM] * 5,
        out_specs=[VMEM] * 7,
        compiler_params=params(60),
        cost_estimate=cost(5e+10, 1e4),
    )(chosen, cot, tables, bias, router)


def mix_kernel(parts, experts, where_ref, *refs):
    hidden_ref, near_refs, far_ref, weight_ref = refs[0], refs[1:parts], refs[parts], refs[parts + 1]
    ctx_refs = refs[parts + 2 : 2 * parts + 2]
    gain_ref, router_ref, chosen_ref, pack_ref = refs[2 * parts + 2 : 2 * parts + 6]
    sum_ref, gate_ref, packed_ref, whole_ref, all_ref = refs[2 * parts + 6 :]
    core = where_ref[2]
    inner, width = weight_ref.shape
    side = width // 2
    whole_ref[0:inner, :] = weight_ref[...]
    near_at = pl.ds(pl.multiple_of(core * side, LANES), side)
    far_at = pl.ds(pl.multiple_of((1 - core) * side, LANES), side)
    for part in range(1, parts):
        rows = slice(part * inner, (part + 1) * inner)
        whole_ref[rows, near_at] = near_refs[part - 1][...]
        whole_ref[rows, far_at] = far_ref[part - 1]
    all_ref[...] = jnp.concatenate([ref[...] for ref in ctx_refs], axis=1)
    first_sum = hidden_ref[...].astype(F32) + dot_nn(all_ref[...], whole_ref[...])
    sum_ref[...] = first_sum
    normed = (first_sum * rms_scale(first_sum) * gain_ref[1:2, :]).astype(BF)
    packed_ref[...] = dot_nn(pack_ref[...], normed).astype(BF)
    lane = lax.broadcasted_iota(jnp.int32, gate_ref.shape, 1)
    logits = jnp.where(lane < experts, dot_nt(normed, router_ref[...]), F32(NEG))
    logits = jnp.exp(logits - jnp.max(logits, axis=1, keepdims=True))
    gate = jnp.sum(chosen_ref[...] * logits, axis=1, keepdims=True) / jnp.sum(
        logits, axis=1, keepdims=True
    )
    gate_ref[...] = jnp.broadcast_to(gate, gate_ref.shape)


def mix(where, hidden, near, far, weight, ctxs, gain, router, chosen, hot, experts):
    parts = len(ctxs)
    rows, width = hidden.shape
    inner = weight.shape[0]
    return pl.pallas_call(
        functools.partial(mix_kernel, parts, experts),
        out_shape=[
            jax.ShapeDtypeStruct((rows, width), F32),
            jax.ShapeDtypeStruct((rows, LANES), F32),
            jax.ShapeDtypeStruct((hot.shape[0], width), BF),
            jax.ShapeDtypeStruct((parts * inner, width), BF),
            jax.ShapeDtypeStruct((rows, parts * inner), BF),
        ],
        in_specs=[SMEM] + [VMEM] * (2 * parts + 6),
        out_specs=[VMEM] * 5,
        compiler_params=params(60),
        cost_estimate=cost(5e10, 1e4),
    )(where, hidden, *near, far, weight, *ctxs, gain, router, chosen, hot)


def expert_kernel(in_map, out_map, experts, where_ref, *refs):
    row_ref, cot_ref, router_ref = refs[:3]
    in_refs, out_refs = refs[3 : 3 + len(in_map)], refs[3 + len(in_map) : 3 + 2 * len(in_map)]
    back_ref, out_ref, gated_ref, logit_ref, near_hbm, far_hbm = refs[
        3 + 2 * len(in_map) : 9 + 2 * len(in_map)
    ]
    in_ref, outw_ref, near_ref, far_ref, total_ref, acc_ref, load_sems, store_sems = refs[
        9 + 2 * len(in_map) :
    ]
    units = len(in_map) // 2
    name = where_ref[3]
    slots, width = row_ref.shape
    span = in_refs[0].shape[1]
    hidden = units * span
    loads = []
    for unit in range(units):
        pieces = []
        for half in range(2):
            at = slice(half * span, (half + 1) * span)
            source = in_refs[in_map.index(unit + half * units)]
            pieces.append((source, in_ref.at[unit, :, at]))
            source = out_refs[out_map.index(unit + half * units)]
            pieces.append((source, outw_ref.at[unit, at, :]))
        copies = []
        for number, (source, target) in enumerate(pieces):
            copies.append(pltpu.make_async_copy(source, target, load_sems.at[unit, number]))
            copies[-1].start()
        loads.append(copies)
    rows_step = min(512, slots)
    tiles = [slice(at, at + rows_step) for at in range(0, slots, rows_step)]
    gates, routers = [], []
    lane = lax.broadcasted_iota(jnp.int32, (rows_step, LANES), 1)
    hot = (lane == name).astype(F32)
    for tile in tiles:
        logits = jnp.where(lane < experts, dot_nt(row_ref[tile, :], router_ref[...]), F32(NEG))
        logits = jnp.exp(logits - jnp.max(logits, axis=1, keepdims=True))
        router = logits / jnp.sum(logits, axis=1, keepdims=True)
        gate = jnp.sum(router * hot, axis=1, keepdims=True)
        gated = (cot_ref[tile, :].astype(F32) * gate).astype(BF)
        gated_ref[tile, :] = gated
        far_ref[tile, 2 * hidden :] = gated
        gates.append(gate)
        routers.append(router)
    stores = [
        pltpu.make_async_copy(
            far_ref.at[:, 2 * hidden :], far_hbm.at[:, 2 * hidden :], store_sems.at[units, 0]
        )
    ]
    stores[0].start()
    for unit in range(units):
        for copy in loads[unit]:
            copy.wait()
        for tile in tiles:
            pre_act = dot_nn(row_ref[tile, :], in_ref[unit])
            below = 0.5 + 0.5 * lax.erf(pre_act * F32(SQRT_HALF))
            active = (pre_act * below).astype(BF)
            slope = below + pre_act * jnp.exp(pre_act * pre_act * F32(-0.5)) * F32(INV_SQRT_TWO_PI)
            grad = (dot_nt(gated_ref[tile, :], outw_ref[unit]) * slope).astype(BF)
            for side_ref, half in ((near_ref, 0), (far_ref, 1)):
                at = slice(half * span, (half + 1) * span)
                side_ref[tile, unit * span : (unit + 1) * span] = active[:, at]
                side_ref[tile, hidden + unit * span : hidden + (unit + 1) * span] = grad[:, at]
            total = dot_nn(active, outw_ref[unit])
            back = dot_nt(grad, in_ref[unit])
            if unit:
                total_ref[tile, :] += total
                acc_ref[tile, :] += back
            else:
                total_ref[tile, :] = total
                acc_ref[tile, :] = back
        for number, (side_ref, side_hbm, first) in enumerate(
            (
                (near_ref, near_hbm, 0),
                (near_ref, near_hbm, hidden),
                (far_ref, far_hbm, 0),
                (far_ref, far_hbm, hidden),
            )
        ):
            at = slice(first + unit * span, first + (unit + 1) * span)
            copy = pltpu.make_async_copy(
                side_ref.at[:, at], side_hbm.at[:, at], store_sems.at[unit, number]
            )
            copy.start()
            stores.append(copy)
    for tile, gate, router in zip(tiles, gates, routers):
        total = total_ref[tile, :]
        gate_grad = jnp.sum(cot_ref[tile, :].astype(F32) * total, axis=1, keepdims=True)
        logit_grad = ((gate_grad * gate) * (hot - router)).astype(BF)
        logit_ref[tile, :] = logit_grad
        out_ref[tile, :] = total.astype(BF)
        back_ref[tile, :] = (acc_ref[tile, :] + dot_nn(logit_grad, router_ref[...])).astype(BF)
    for copy in stores:
        copy.wait()


def run_expert(where, rows, cots, in_parts, out_parts, in_map, out_map, router, experts):
    slots, width = rows.shape
    span = in_parts[0].shape[1]
    units = len(in_map) // 2
    hidden = 2 * units * span
    back, out, gated, logit, near, far = pl.pallas_call(
        functools.partial(expert_kernel, in_map, out_map, experts),
        out_shape=[
            jax.ShapeDtypeStruct((slots, width), BF),
            jax.ShapeDtypeStruct((slots, width), BF),
            jax.ShapeDtypeStruct((slots, width), BF),
            jax.ShapeDtypeStruct((slots, LANES), BF),
            jax.ShapeDtypeStruct((slots, hidden), BF),
            jax.ShapeDtypeStruct((slots, hidden + width), BF),
        ],
        in_specs=[SMEM] + [VMEM] * 3 + [ANY] * (len(in_parts) + len(out_parts)),
        out_specs=[VMEM] * 4 + [ANY] * 2,
        scratch_shapes=[
            pltpu.VMEM((units, width, 2 * span), BF),
            pltpu.VMEM((units, 2 * span, width), BF),
            pltpu.VMEM((slots, hidden), BF),
            pltpu.VMEM((slots, hidden + width), BF),
            pltpu.VMEM((slots, width), F32),
            pltpu.VMEM((slots, width), F32),
            pltpu.SemaphoreType.DMA((units, 4)),
            pltpu.SemaphoreType.DMA((units + 1, 4)),
        ],
        compiler_params=params(56),
        cost_estimate=cost(25e9, 20e6),
    )(where, rows, cots, router, *in_parts, *out_parts)
    return back, out, gated, near, far, logit


def weight_kernel(parts, row_ref, peer_ref, gated_ref, near_hbm, got_hbm, *refs):
    out_hbm = refs[: 2 * parts]
    both_ref, lhs_ref, tail_ref, done_ref, load_sems, store_sems = refs[2 * parts :]
    slots, width = row_ref.shape
    span = out_hbm[0].shape[1]
    hidden = parts * span
    chunk = 2 * span
    count = 2 * hidden // chunk
    tail = pltpu.make_async_copy(got_hbm.at[:, 2 * hidden :], tail_ref, load_sems.at[count, 0])
    loads = []
    order = list(range(count // 2, count)) + list(range(count // 2))
    for index in order:
        at = slice(index * chunk, (index + 1) * chunk)
        near = pltpu.make_async_copy(
            near_hbm.at[:, at], both_ref.at[0:slots, at], load_sems.at[index, 0]
        )
        got = pltpu.make_async_copy(
            got_hbm.at[:, at], both_ref.at[slots:, at], load_sems.at[index, 1]
        )
        near.start()
        got.start()
        loads.append((near, got))
        if index == count - 1:
            tail.start()
    lhs_ref[0, :, 0:slots] = jnp.transpose(row_ref[...])
    lhs_ref[0, :, slots:] = jnp.transpose(peer_ref[...])
    stores = []
    for number, index in enumerate(order):
        inward = index >= count // 2
        if number == count // 2:
            tail.wait()
            lhs_ref[1, :, 0:slots] = jnp.transpose(gated_ref[...])
            lhs_ref[1, :, slots:] = jnp.transpose(tail_ref[...])
        for copy in loads[number]:
            copy.wait()
        at = slice(index * chunk, (index + 1) * chunk)
        done_ref[number] = dot_nn(lhs_ref[0 if inward else 1], both_ref[:, at]).astype(BF)
        for half in range(2):
            part = 2 * (index % (count // 2)) + half
            copy = pltpu.make_async_copy(
                done_ref.at[number, :, half * span : (half + 1) * span],
                out_hbm[part if inward else parts + part],
                store_sems.at[number, half],
            )
            copy.start()
            stores.append(copy)
    for copy in stores:
        copy.wait()


def weight_grads(where, rows, rows_peer, gated, near, got, parts):
    slots, width = rows.shape
    span = near.shape[1] // (2 * parts)
    one = jax.ShapeDtypeStruct((width, span), BF)
    outs = pl.pallas_call(
        functools.partial(weight_kernel, parts),
        out_shape=[one] * (2 * parts),
        in_specs=[VMEM] * 3 + [ANY] * 2,
        out_specs=[ANY] * (2 * parts),
        scratch_shapes=[
            pltpu.VMEM((2 * slots, 2 * parts * span), BF),
            pltpu.VMEM((2, width, 2 * slots), BF),
            pltpu.VMEM((slots, width), BF),
            pltpu.VMEM((parts, width, 2 * span), BF),
            pltpu.SemaphoreType.DMA((parts + 1, 2)),
            pltpu.SemaphoreType.DMA((parts, 2)),
        ],
        compiler_params=params(60),
        cost_estimate=cost(1e10, 1e6),
    )(rows, rows_peer, gated, near, got)
    return outs[:parts], outs[parts:]


def residual_kernel(parts, where_ref, *refs):
    home_ref, hot_ref, sum_ref, cot_ref, gain_ref = refs[:5]
    weight_ref, all_ref, grad_ref, gain_out_ref, give_ref = refs[5:10]
    ctx_refs, keep_refs = refs[10 : 10 + parts], refs[10 + parts :]
    core = where_ref[2]
    side = grad_ref.shape[1] // 2
    upstream = dot_nn(hot_ref[...], home_ref[...])
    first_sum = sum_ref[...]
    inverse = rms_scale(first_sum)
    gain_out_ref[...] = jnp.broadcast_to(
        jnp.sum(upstream * first_sum * inverse, axis=0, keepdims=True), gain_out_ref.shape
    )
    grad = cot_ref[...].astype(F32) + norm_back(first_sum, inverse, gain_ref[1:2, :], upstream)
    grad_ref[...] = grad
    low = grad.astype(BF)
    inner = weight_ref.shape[0] // parts
    across = dot_nt(low, weight_ref[...]).astype(BF)
    for part in range(parts):
        ctx_refs[part][...] = across[:, part * inner : (part + 1) * inner]
    product = dot_tn(all_ref[...], low)
    for part in range(parts):
        rows = slice(part * inner, (part + 1) * inner)

        @pl.when(core == 0)
        def _(part=part, rows=rows):
            keep_refs[part][...] = product[rows, :side]
            give_ref[part] = product[rows, side:].astype(BF)

        @pl.when(core != 0)
        def _(part=part, rows=rows):
            keep_refs[part][...] = product[rows, side:]
            give_ref[part] = product[rows, :side].astype(BF)


def residual(where, home, hot, first_sum, cot, gain, weight, every, parts):
    rows, width = first_sum.shape
    inner = weight.shape[0] // parts
    return pl.pallas_call(
        functools.partial(residual_kernel, parts),
        out_shape=[
            jax.ShapeDtypeStruct((rows, width), F32),
            jax.ShapeDtypeStruct((8, width), F32),
            jax.ShapeDtypeStruct((parts, inner, width // 2), BF),
        ]
        + [jax.ShapeDtypeStruct((rows, inner), BF)] * parts
        + [jax.ShapeDtypeStruct((inner, width // 2), F32)] * parts,
        in_specs=[SMEM] + [VMEM] * 7,
        out_specs=[VMEM] * (3 + 2 * parts),
        compiler_params=params(60),
        cost_estimate=cost(2e+11, 1e4),
    )(where, home, hot, first_sum, cot, gain, weight, every)


def attend_back_kernel(parts, heads, where_ref, *refs):
    cot_refs, refs = refs[:parts], refs[parts:]
    ctx_ref, proj_ref, normed_ref, lse_ref, weight_ref, offset_ref = refs[:6]
    scale_ref, small_ref, moe_ref, table_ref = refs[6:10]
    send_ref, bias_ref, keep_ref, give_ref = refs[10:14]
    skew_ref, fold_ref, cot_ref, dproj_ref, key_acc, value_acc = refs[14:]
    quarter = ctx_ref.shape[1]
    for part in range(parts):
        cot_ref[where_ref[0] ^ part] = cot_refs[part][...]
    length = quarter * parts
    inner = weight_ref.shape[0] // 3
    head_dim = inner // heads
    prefix, core = where_ref[1], where_ref[2]
    skew_into(skew_ref, offset_ref, heads, 2 * length)
    fold_ref[...] = jnp.zeros_like(fold_ref)
    key_acc[...] = jnp.zeros_like(key_acc)
    value_acc[...] = jnp.zeros_like(value_acc)
    keys_across = jnp.transpose(proj_ref[:, inner : 2 * inner])
    head_row = lax.broadcasted_iota(jnp.int32, (8, inner), 0)
    head_lane = lax.broadcasted_iota(jnp.int32, (8, inner), 1)
    picks = (head_lane // head_dim == head_row).astype(BF)
    for block in range(parts):
        first = block * quarter
        reach = max(length // 2, first + quarter)
        key_pos = first + lax.broadcasted_iota(jnp.int32, (reach - first, quarter), 0)
        query_pos = first + lax.broadcasted_iota(jnp.int32, (reach - first, quarter), 1)
        allowed = (key_pos <= query_pos) | (key_pos < prefix)
        product = cot_ref[block].astype(F32) * ctx_ref[block].astype(F32)
        high = product.astype(BF)
        rest = (product - high.astype(F32)).astype(BF)
        inner_sum = dot_nt(picks, high) + dot_nt(picks, rest)
        query_pieces = []
        for head in range(heads):
            low = head * head_dim
            query = proj_ref[first : first + quarter, low : low + head_dim]
            keys = proj_ref[0:reach, inner + low : inner + low + head_dim]
            values = proj_ref[0:reach, 2 * inner + low : 2 * inner + low + head_dim]
            grad = cot_ref[block, :, low : low + head_dim]
            bias = jnp.concatenate(
                [
                    skew_ref[
                        head,
                        :,
                        first - LANES * sub + length - LANES : first
                        - LANES * sub
                        + length
                        - LANES
                        + quarter,
                    ]
                    for sub in range(reach // LANES)
                ],
                axis=0,
            )
            scores = dot_nt(keys, query) + bias
            tail = jnp.where(allowed, scores[first:], F32(NEG))
            scores = jnp.concatenate([scores[:first], tail], axis=0) if first else tail
            probs = jnp.exp(scores - lse_ref[block, head : head + 1, :])
            prob_grad = dot_nt(values, grad)
            score_grad = (probs * (prob_grad - inner_sum[head : head + 1, :])).astype(BF)
            wide = score_grad.astype(F32)
            for sub in range(reach // LANES):
                column = first - LANES * sub + length - LANES
                fold_ref[head, :, column : column + quarter] += wide[
                    LANES * sub : LANES * (sub + 1)
                ]
            value_acc[head, 0:reach, :] += dot_nn(probs.astype(BF), grad)
            key_acc[head, 0:reach, :] += dot_nn(score_grad, query)
            query_pieces.append(dot_nn(keys_across[low : low + head_dim, 0:reach], score_grad))
        query_grad = jnp.transpose(jnp.concatenate(query_pieces, axis=0)) * F32(head_dim ** (-0.5))
        dproj_ref[first : first + quarter, 0:inner] = query_grad.astype(BF)
    dproj_ref[:, inner : 3 * inner] = jnp.concatenate(
        [key_acc[head] for head in range(heads)] + [value_acc[head] for head in range(heads)],
        axis=1,
    ).astype(BF)
    width = normed_ref.shape[1]
    side = width // 2
    split, piece, _ = keep_ref.shape
    layer = where_ref[3]
    grad_rows = dot_nn(jnp.transpose(dproj_ref[...]), normed_ref[...])
    for half in range(2):
        for part in range(split):
            chunk = grad_rows[part * piece : (part + 1) * piece, half * side : (half + 1) * side]
            slot = (layer ^ part) if split > 1 else part

            @pl.when(core == half)
            def _(chunk=chunk, slot=slot):
                keep_ref[slot] = chunk

            @pl.when(core != half)
            def _(chunk=chunk, slot=slot):
                give_ref[slot] = chunk.astype(BF)

    gain_sum = jnp.zeros((1, width), F32)
    for block in range(parts):
        rows = slice(block * quarter, (block + 1) * quarter)
        upstream = dot_nn(dproj_ref[rows, :], weight_ref[...])
        gain_sum = gain_sum + jnp.sum(
            upstream * normed_ref[rows, :].astype(F32), axis=0, keepdims=True
        )
        send_ref[block, 0:quarter, :] = upstream.astype(BF)
    extra = small_ref.shape[0]
    row = lax.broadcasted_iota(jnp.int32, small_ref.shape, 0)
    small = jnp.where(row == 1, moe_ref[0:1, :], small_ref[...])
    small = jnp.where(row == 0, gain_sum / scale_ref[0:1, :], small).astype(BF)
    share = width // parts
    for block in range(parts):
        send_ref[block, quarter:, 0:share] = small[:, block * share : (block + 1) * share]
        send_ref[block, quarter:, share:] = jnp.zeros((extra, width - share), BF)
    row_index = lax.broadcasted_iota(jnp.int32, (LANES, 2 * length), 0)
    buckets = (row_index == table_ref[1:2, :]).astype(BF)
    sums = []
    for head in range(heads):
        tile = fold_ref[head, 0:8, :]
        for group in range(8, LANES, 8):
            tile = tile + pltpu.roll(fold_ref[head, group : group + 8, :], 2 * length - group, 1)
        for bit in range(3):
            moved = pltpu.roll(tile, 2 * length - (1 << bit), 1)
            tile = jnp.where(((row_index[0:8] >> bit) & 1) == 1, moved, tile)
        tile = pltpu.roll(tile, LANES - 1, 1)
        sums.append(jnp.sum(tile, axis=0, keepdims=True))
    rest = jnp.concatenate(sums + [jnp.zeros((8 - heads, 2 * length), F32)], axis=0)
    levels = []
    for _ in range(3):
        high = rest.astype(BF).astype(F32)
        rest = rest - high
        levels.append(high)
    total = dot_nt(jnp.concatenate(levels, axis=0).astype(BF), buckets)
    total = total[0:8] + total[8:16] + total[16:24]
    bias_ref[0:8, :] = total
    bias_ref[8:, :] = jnp.zeros((bias_ref.shape[0] - 8, LANES), F32)


def attend_back(
    where, cots, ctxs, proj, normed, lse, weight, offsets, scale, small, moe, tables, heads, split
):
    parts, quarter, inner = ctxs.shape
    width = normed.shape[1]
    length = parts * quarter
    return pl.pallas_call(
        functools.partial(attend_back_kernel, parts, heads),
        out_shape=[
            jax.ShapeDtypeStruct((parts, quarter + small.shape[0], width), BF),
            jax.ShapeDtypeStruct((small.shape[0], LANES), F32),
            jax.ShapeDtypeStruct((split, 3 * inner // split, width // 2), F32),
            jax.ShapeDtypeStruct((split, 3 * inner // split, width // 2), BF),
        ],
        in_specs=[SMEM] + [VMEM] * (10 + parts),
        out_specs=[VMEM] * 4,
        scratch_shapes=[
            pltpu.VMEM((heads, LANES, 2 * length), F32),
            pltpu.VMEM((heads, LANES, 2 * length), F32),
            pltpu.VMEM((parts, quarter, inner), BF),
            pltpu.VMEM((length, 3 * inner), BF),
            pltpu.VMEM((heads, length, inner // heads), F32),
            pltpu.VMEM((heads, length, inner // heads), F32),
        ],
        compiler_params=params(60),
        cost_estimate=cost(5e+10, 1e4),
    )(where, *cots, ctxs, proj, normed, lse, weight, offsets, scale, small, moe, tables)


def merge_kernel(parts, where_ref, keep_ref, got_ref, *refs):
    wo_refs, (home_ref, hot_ref, sum_ref, gate_ref) = refs[:parts], refs[parts : parts + 4]
    layer_ref, send_refs, wo_ref = refs[parts + 4], refs[parts + 5 : -1], refs[-1]
    split, piece, side = keep_ref.shape
    share = wo_ref.shape[0] // split
    layer = where_ref[3]
    total = wo_refs[0][...] + wo_refs[1][0].astype(F32)
    for part in range(2, parts):
        total = total + wo_refs[part][...].astype(F32)
    wo_ref[...] = total
    expert_out = dot_nn(hot_ref[...], home_ref[...])
    layer_ref[...] = (sum_ref[...] + gate_ref[:, 0:1] * expert_out).astype(BF)
    for part in range(split):
        send_refs[part][0:piece, :] = (keep_ref[part] + got_ref[part].astype(F32)).astype(BF)
        row = (layer ^ part) * share if split > 1 else 0
        send_refs[part][piece:, :] = wo_ref[pl.ds(pl.multiple_of(row, 8), share), :].astype(BF)


def merge(where, keep, got, wos, home, hot, first_sum, gate):
    split, piece, side = keep.shape
    rows = wos[0].shape[0]
    shape = jax.ShapeDtypeStruct((piece + rows // split, side), BF)
    return pl.pallas_call(
        functools.partial(merge_kernel, len(wos)),
        out_shape=[jax.ShapeDtypeStruct(first_sum.shape, BF)] + [shape] * split,
        in_specs=[SMEM] + [VMEM] * (6 + len(wos)),
        out_specs=[VMEM] * (1 + split),
        scratch_shapes=[pltpu.VMEM((rows, side), F32)],
        compiler_params=params(60),
        cost_estimate=cost(1e+06, 1e4),
    )(where, keep, got, *wos, home, hot, first_sum, gate)


def assemble_kernel(where_ref, *refs):
    grad_refs, refs = refs[:4], refs[4:]
    *piece_refs, in_hbm, out_hbm, qkv_ref, wo_ref, first_ref, second_ref, router_ref, bias_ref = refs[
        :-4
    ]
    parts_ref, in_ref, out_ref, sems = refs[-4:]
    split = len(piece_refs) // 2
    side = qkv_ref.shape[1] // 2
    piece, share = qkv_ref.shape[0] // split, wo_ref.shape[0] // split
    core, layer = where_ref[2], where_ref[3]
    span = grad_refs[0].shape[1]
    for half in range(2):
        at = pl.ds(pl.multiple_of((core ^ half) * span, LANES), span)
        in_ref[:, at] = grad_refs[2 * half][...].astype(F32)
    in_copy = pltpu.make_async_copy(in_ref, in_hbm, sems.at[0])
    in_copy.start()
    for half in range(2):
        at = pl.ds(pl.multiple_of((core ^ half) * span, LANES), span)
        out_ref[at, :] = jnp.transpose(grad_refs[2 * half + 1][...].astype(F32))
    out_copy = pltpu.make_async_copy(out_ref, out_hbm, sems.at[1])
    out_copy.start()
    for part in range(split):
        slot = (layer ^ part) if split > 1 else 0
        for half in range(2):
            ref = piece_refs[half * split + part]
            at = pl.ds(pl.multiple_of((core ^ half) * side, LANES), side)
            values = ref[...].astype(F32)
            qkv_ref[pl.ds(pl.multiple_of(slot * piece, 8), piece), at] = values[0:piece]
            wo_ref[pl.ds(pl.multiple_of(slot * share, 8), share), at] = values[
                piece : piece + share
            ]
            parts_ref[(core ^ half) * split + slot] = values[piece + share :]
    total = parts_ref[0]
    for part in range(1, 2 * split):
        total = total + parts_ref[part]
    share = first_ref.shape[1]
    first_ref[...] = total[0:1, 0:share]
    second_ref[...] = total[1:2, 0:share]
    router_ref[...] = total[2 : 2 + router_ref.shape[0], 0:share]
    bias_ref[...] = total[0 : bias_ref.shape[0], share : share + bias_ref.shape[1]]
    in_copy.wait()
    out_copy.wait()


def assemble(where, grads, pieces, rows, extra, width, experts, heads, buckets):
    split = len(pieces) // 2
    model_width, span = grads[0].shape
    whole = (model_width, 2 * span), (2 * span, model_width)
    both, side = pieces[0].shape
    return pl.pallas_call(
        assemble_kernel,
        out_shape=[
            jax.ShapeDtypeStruct(whole[0], F32),
            jax.ShapeDtypeStruct(whole[1], F32),
            jax.ShapeDtypeStruct((rows, 2 * side), F32),
            jax.ShapeDtypeStruct((split * (both - extra) - rows, 2 * side), F32),
            jax.ShapeDtypeStruct((1, width), F32),
            jax.ShapeDtypeStruct((1, width), F32),
            jax.ShapeDtypeStruct((experts, width), F32),
            jax.ShapeDtypeStruct((heads, buckets), F32),
        ],
        in_specs=[SMEM] + [VMEM] * (2 * split + 4),
        out_specs=[ANY] * 2 + [VMEM] * 6,
        scratch_shapes=[
            pltpu.VMEM((2 * split, extra, side), F32),
            pltpu.VMEM(whole[0], F32),
            pltpu.VMEM(whole[1], F32),
            pltpu.SemaphoreType.DMA((2,)),
        ],
        compiler_params=params(40),
        cost_estimate=cost(1e+06, 1e4),
    )(where, *grads, *pieces)


def trade(values, axis):
    return lax.all_to_all(values, axis, split_axis=0, concat_axis=0, tiled=True)


def after(values, others):
    return lax.optimization_barrier((values, others))[0]


def body(
    hidden_in,
    cotangent,
    attn_gain,
    query_key_value_weight,
    attention_output_weight,
    rel_bias,
    bucket_table,
    prefix_len,
    moe_gain,
    w_router,
    routes,
    w_expert_in,
    w_expert_out,
):
    seq_count, quarter, model_width = hidden_in.shape
    parts = lax.axis_size("tensor")
    layers = lax.axis_size("expert")
    row_count = seq_count * quarter
    experts = w_router.shape[1]
    capacity = max(2, 2 * row_count // experts)
    slot_count = experts * capacity
    heads, buckets = rel_bias.shape
    inner = query_key_value_weight.shape[2]
    span = w_expert_in.shape[2] // 2
    place, layer, core = lax.axis_index("tensor"), lax.axis_index("expert"), lax.axis_index("dp")
    where = jnp.stack([place, prefix_len[0], core, layer]).astype(jnp.int32)
    low_core = core == 0

    own_hidden = hidden_in[0]
    own_cot = cotangent[0]

    chosen = routes.reshape(1, row_count)
    tables = jnp.stack([bucket_table, jnp.flip(bucket_table)])
    tables = jnp.pad(tables, ((0, 0), (0, 1)), constant_values=-1)
    gains = jnp.stack([attn_gain, moe_gain]).astype(F32)
    pack_hot, unpack_hot, cot_packed, chosen_hot, offset_bias, offset_back, router = prepare(
        chosen, own_cot, tables, rel_bias, w_router.T, capacity
    )

    def over_experts(packed):
        packed = packed.reshape(experts, capacity, model_width)
        return trade(packed, "expert").reshape(slot_count, model_width)

    cot_slots = over_experts(cot_packed)

    hidden_blocks = [own_hidden] + [swap(own_hidden, "tensor", k) for k in range(1, parts)]
    weight = query_key_value_weight.transpose(1, 2, 0).reshape(3 * inner, model_width)
    side = model_width // 2
    own_weight = lax.dynamic_slice(attention_output_weight, (0, core * side), (inner, side))
    late_weight = after(own_weight, hidden_blocks)
    out_weights = [
        swap(late_weight, "tensor", k) for k in range(1, parts)
    ]
    first_blocks, prepared = lax.optimization_barrier(
        (hidden_blocks, (own_weight, pack_hot, unpack_hot, chosen_hot, router, offset_bias,
                         offset_back, where, gains))
    )
    _, pack_hot, unpack_hot, chosen_hot, router, offset_bias, offset_back, where, gains = (
        prepared
    )
    normed_one, projected, lse, contexts, sends = attend(
        where, first_blocks, gains, weight, offset_bias, heads
    )

    in_own = lax.dynamic_slice(w_expert_in[0], (0, core * span), (model_width, span))
    out_own = lax.dynamic_slice(w_expert_out[0], (core * span, 0), (span, model_width))
    in_other = lax.dynamic_slice(w_expert_in[0], (0, (1 - core) * span), (model_width, span))
    out_other = lax.dynamic_slice(w_expert_out[0], ((1 - core) * span, 0), (span, model_width))
    in_own, out_own = after((in_own, out_own), hidden_blocks)
    in_step, out_step = swap(in_own, "tensor", 1), swap(out_own, "tensor", 2)
    far_weights = swap(jnp.stack(after(out_weights, sends)), "dp", 1)
    sends = after(sends, far_weights)
    own_contexts = [sends[0]] + [swap(sends[k], "tensor", k) for k in range(1, parts)]


    in_next, out_next = after((in_own, out_own), own_contexts[1])
    in_next, out_next = swap(in_next, "tensor", 2), swap(out_next, "tensor", 1)
    in_far, out_far = after((in_step, out_step), (own_contexts, in_next, out_next))
    in_far, out_far = swap(in_far, "tensor", 2), swap(out_far, "tensor", 1)
    in_near, in_order = [in_own, in_step, in_next, in_far], (0, 1, 2, 3)
    out_near, out_order = [out_own, out_step, out_next, out_far], (0, 2, 1, 3)
    in_map = in_order + tuple(parts + unit for unit in in_order)
    out_map = out_order + tuple(parts + unit for unit in out_order)

    first_sum, gate, packed, whole_weight, every_context = mix(
        where, own_hidden, out_weights, far_weights, attention_output_weight,
        after(own_contexts, (cot_slots, in_step, out_step)), gains, router, chosen_hot, pack_hot,
        experts,
    )
    row_slots = over_experts(packed)

    def cross(pieces):
        _, near, near_too, far = pieces
        far = after(far, row_slots)
        return [swap(near, "dp", 1), swap(near_too, "dp", 1), swap(far, "dp", 1)]

    in_parts = in_near + [in_other] + cross(in_near)
    out_parts = out_near + [out_other] + cross(out_near)
    rows_peer = swap(row_slots, "dp", 1)
    back_slots, out_slots, gated, near, far, logit_grad = run_expert(
        where, row_slots, cot_slots, in_parts, out_parts, in_map, out_map, router, experts
    )
    back_home = over_experts(back_slots)

    in_sums, out_sums = partial = weight_grads(
        where, row_slots, rows_peer, gated, near, swap(far, "dp", 1), parts
    )
    in_skip, out_skip = swap(in_sums[3], "tensor", 1), swap(out_sums[3], "tensor", 2)

    def plus(*terms):
        total = terms[0].astype(F32)
        for term in terms[1:]:
            total = total + term.astype(F32)
        return total.astype(BF)


    router_part = dot_tn(logit_grad, row_slots)[:experts]
    extra = -(-(experts + 2) // 16) * 16
    small = jnp.pad(router_part, ((2, extra - 2 - experts), (0, 0)))
    residual_grad, moe_gain_part, wo_give, *cots = residual(
        where, after(back_home, (partial, small)), unpack_hot, first_sum, own_cot, gains, whole_weight,
        every_context, parts,
    )
    cots, wo_keep = cots[:parts], cots[parts:]
    context_cots = [cots[0]] + [swap(cots[k], "tensor", k) for k in range(1, parts)]

    wo_got = swap(wo_give, "dp", 1)
    out_home = over_experts(after(out_slots, wo_got))
    wo_low = [(wo_keep[k] + wo_got[k].astype(F32)).astype(BF) for k in range(1, parts)]
    context_cots = after(context_cots, (wo_low, in_skip, out_skip))
    in_side, out_side = after((in_sums[1], out_sums[2]), (in_skip, out_skip))
    in_side, out_side = swap(in_side, "tensor", 1), swap(out_side, "tensor", 2)
    wo_parts = [wo_keep[0], wo_got] + [
        swap(wo_low[k - 1], "tensor", k) for k in range(1, parts)
    ]

    split = layers if layers == 4 else 1
    send_ups, bias_part, keep, give = attend_back(
        where, context_cots, contexts, projected, normed_one, lse, weight, offset_back,
        gains, small, moe_gain_part, tables, heads, split,
    )
    send_ups, give = after((send_ups, give), (wo_parts, out_home, in_side, out_side))
    ups = jnp.sum(trade(send_ups, "tensor").astype(F32), axis=0)
    own_float = own_hidden.astype(F32)
    inverse_own = rms_scale(own_float)
    input_grad = residual_grad + norm_back(own_float, inverse_own, gains[0:1], ups[:quarter])

    share = model_width // parts
    bias_part = jnp.pad(bias_part, ((0, 0), (0, side - share - LANES)))
    small = jnp.concatenate([ups[quarter:, :share], bias_part], axis=1)
    layer_out, *sends = merge(
        where, keep, swap(give, "dp", 1), wo_parts, out_home, unpack_hot, first_sum, gate
    )
    piece = sends[0].astype(F32)
    first = sends[-1]
    if split > 1:
        arrived = [swap(sends[k], "expert", k) for k in range(1, layers)]
        first = arrived[0]
        for value in arrived:
            piece = piece + value.astype(F32)
    in_skip, out_skip, in_side, out_side = after((in_skip, out_skip, in_side, out_side), first)
    in_pass, out_pass = plus(in_sums[2], in_skip), plus(out_sums[1], out_skip)
    in_last, out_last = swap(in_pass, "tensor", 2), swap(out_pass, "tensor", 1)
    if split > 1:
        piece = jnp.concatenate([piece, small], axis=0).astype(BF)
        pieces = [piece] + [swap(piece, "expert", k) for k in range(1, layers)]
    else:
        pieces = [lax.psum(jnp.concatenate([piece, small], axis=0), "expert")]
    in_last, out_last = after((in_last, out_last), pieces[:2])
    mine = (plus(in_sums[0], in_side, in_last), plus(out_sums[0], out_side, out_last))
    both = (*mine, *(swap(x, "dp", 1) for x in mine))
    pieces = pieces + [swap(x, "dp", 1) for x in pieces]
    pieces, done = lax.optimization_barrier((pieces, (layer_out, input_grad)))
    layer_out, input_grad = done
    (
        expert_in_grad, expert_out_grad, qkv_across, attn_out_grad, gain_one, gain_two, router_grad,
        bias_grad,
    ) = assemble(
        where, both, pieces, 3 * inner, extra, share, experts, heads, buckets
    )
    qkv_grad = qkv_across.reshape(3, inner, model_width).transpose(2, 0, 1)
    return (
        layer_out.reshape(seq_count, quarter, model_width),
        input_grad.reshape(seq_count, quarter, model_width),
        gain_one[0],
        qkv_grad,
        attn_out_grad,
        bias_grad,
        gain_two[0],
        router_grad.T,
        expert_in_grad[None],
        expert_out_grad[None],
    )


def solution(mesh):
    placed = (
        P(("dp", "expert"), "tensor", None),
        P(("dp", "expert"), "tensor", None),
        P(),
        P(None, None, "tensor"),
        P("tensor", None),
        P("tensor", None),
        P(),
        P(("dp", "expert")),
        P(),
        P(),
        P(("dp", "expert"), "tensor", None, None, None),
        P("expert", None, "tensor"),
        P("expert", "tensor", None),
    )
    return jax.shard_map(
        body,
        mesh=mesh,
        in_specs=placed,
        out_specs=(
            P(("dp", "expert"), "tensor", None),
            P(("dp", "expert"), "tensor", None),
            P("tensor"),
            P(None, None, "tensor"),
            P("tensor", None),
            P("tensor", None),
            P("tensor"),
            P("tensor", None),
            P("expert", None, "tensor"),
            P("expert", "tensor", None),
        ),
        check_vma=False,
    )
```

```python
import functools

import jax
import jax.numpy as jnp
from jax import lax
from jax.experimental import pallas as pl
from jax.experimental.pallas import tpu as pltpu
from jax.sharding import PartitionSpec as P

EPSILON = 1e-06
NEG = -1e30
TOP_PRECISION = lax.Precision.HIGHEST
BF = jnp.bfloat16
F32 = jnp.float32
LANES = 128
VMEM = pl.BlockSpec()
ANY = pl.BlockSpec(memory_space=pl.ANY)
SMEM = pl.BlockSpec(memory_space=pltpu.SMEM)
SQRT_HALF = 0.7071067811865476
INV_SQRT_TWO_PI = 0.3989422804014327


def params(mib):
    return pltpu.CompilerParams(vmem_limit_bytes=mib * 1024 * 1024)


def cost(flops, moved):
    return pl.CostEstimate(flops=int(flops), bytes_accessed=int(moved), transcendentals=0)


def dot_nn(a, b):
    return lax.dot_general(a, b, (((1,), (0,)), ((), ())), preferred_element_type=F32)


def dot_nt(a, b):
    return lax.dot_general(a, b, (((1,), (1,)), ((), ())), preferred_element_type=F32)


def dot_tn(a, b):
    return lax.dot_general(a, b, (((0,), (0,)), ((), ())), preferred_element_type=F32)


def rms_scale(values):
    return lax.rsqrt(jnp.mean(values * values, axis=-1, keepdims=True) + EPSILON)


def norm_back(values, inverse, gain_vec, upstream):
    scaled = upstream * gain_vec
    return inverse * scaled - values * (inverse * inverse * inverse) * jnp.mean(
        scaled * values, axis=-1, keepdims=True
    )


def swap(values, axis, step):
    count = lax.axis_size(axis)
    return lax.ppermute(values, axis, [(i, i ^ step) for i in range(count)])


def skew_into(skew_ref, offset_ref, heads, width):
    for head in range(heads):
        row = jnp.broadcast_to(offset_ref[head : head + 1, :], (LANES, width))
        skew_ref[head] = pltpu.roll(row, width - (LANES - 1), 1, stride=1, stride_axis=0)


def attend_kernel(parts, heads, where_ref, *refs):
    x_refs = refs[:parts]
    gain_ref, weight_ref, offset_ref = refs[parts : parts + 3]
    normed_ref, proj_ref, lse_ref, ctx_ref = refs[parts + 3 : parts + 7]
    send_refs, skew_ref = refs[parts + 7 : 2 * parts + 7], refs[2 * parts + 7]
    quarter = x_refs[0].shape[0]
    length = quarter * parts
    inner = weight_ref.shape[0] // 3
    head_dim = inner // heads
    place, prefix = where_ref[0], where_ref[1]
    lane = lax.broadcasted_iota(jnp.int32, (1, 3 * inner), 1)
    column_scale = jnp.where(lane < inner, F32(head_dim ** (-0.5)), F32(1.0))
    for part in range(parts):
        x = x_refs[part][...].astype(F32)
        normed = (x * rms_scale(x) * gain_ref[0:1, :]).astype(BF)
        rows = pl.ds(pl.multiple_of((place ^ part) * quarter, quarter), quarter)
        normed_ref[rows, :] = normed
        proj_ref[rows, :] = (dot_nt(normed, weight_ref[...]) * column_scale).astype(BF)
    skew_into(skew_ref, offset_ref, heads, 2 * length)
    tiles = length // LANES
    per_block = quarter // LANES
    for block in range(parts):
        first = block * quarter
        reach = max(length // 2, first + quarter)
        key_pos = first + lax.broadcasted_iota(jnp.int32, (quarter, reach - first), 1)
        query_pos = first + lax.broadcasted_iota(jnp.int32, (quarter, reach - first), 0)
        allowed = (key_pos <= query_pos) | (key_pos < prefix)
        pieces, logs = [], []
        for head in range(heads):
            low = head * head_dim
            query = proj_ref[first : first + quarter, low : low + head_dim]
            keys = proj_ref[0:reach, inner + low : inner + low + head_dim]
            values = proj_ref[0:reach, 2 * inner + low : 2 * inner + low + head_dim]
            bias = jnp.concatenate(
                [
                    skew_ref[
                        head,
                        :,
                        LANES * (tiles - 1 - block * per_block - sub) : LANES
                        * (tiles - 1 - block * per_block - sub)
                        + reach,
                    ]
                    for sub in range(per_block)
                ],
                axis=0,
            )
            scores = dot_nt(query, keys) + bias
            tail = jnp.where(allowed, scores[:, first:], F32(NEG))
            scores = jnp.concatenate([scores[:, :first], tail], axis=1) if first else tail
            peak = jnp.max(scores, axis=1, keepdims=True)
            exponent = jnp.exp(scores - peak)
            total = jnp.sum(exponent, axis=1, keepdims=True)
            pieces.append(dot_nn(exponent.astype(BF), values) / total)
            logs.append(jnp.broadcast_to(peak + jnp.log(total), (quarter, LANES)))
        ctx_ref[block] = jnp.concatenate(pieces, axis=1).astype(BF)
        lane_row = lax.broadcasted_iota(jnp.int32, (quarter, LANES), 1)
        stacked = logs[0]
        for head in range(1, heads):
            stacked = jnp.where(lane_row == head, logs[head], stacked)
        lse_ref[block] = jnp.transpose(stacked)[0:8, :]
    for part in range(parts):
        send_refs[part][...] = ctx_ref[place ^ part]


def attend(where, blocks, gain, weight, offsets, heads):
    parts = len(blocks)
    quarter, width = blocks[0].shape
    length = parts * quarter
    inner3 = weight.shape[0]
    outs = pl.pallas_call(
        functools.partial(attend_kernel, parts, heads),
        out_shape=[
            jax.ShapeDtypeStruct((length, width), BF),
            jax.ShapeDtypeStruct((length, inner3), BF),
            jax.ShapeDtypeStruct((parts, 8, quarter), F32),
            jax.ShapeDtypeStruct((parts, quarter, inner3 // 3), BF),
        ]
        + [jax.ShapeDtypeStruct((quarter, inner3 // 3), BF)] * parts,
        in_specs=[SMEM] + [VMEM] * (parts + 3),
        out_specs=[VMEM] * (4 + parts),
        scratch_shapes=[pltpu.VMEM((heads, LANES, 2 * length), F32)],
        compiler_params=params(60),
        cost_estimate=cost(5e+10, 1e4),
    )(where, *blocks, gain, weight, offsets)
    return outs[0], outs[1], outs[2], outs[3], outs[4:]


def prepare_kernel(experts, capacity, chosen_ref, cot_ref, table_ref, bias_ref, router_in_ref, *outs):
    pack_ref, unpack_ref, packed_ref, hot_ref, offset_ref, back_ref, router_ref = outs
    slots, rows = pack_ref.shape
    chosen = chosen_ref[...]
    hot = (lax.broadcasted_iota(jnp.int32, (LANES, rows), 0) == chosen).astype(F32)
    earlier = lax.broadcasted_iota(jnp.int32, (rows, rows), 0)
    later = lax.broadcasted_iota(jnp.int32, (rows, rows), 1)
    before = dot_nn(hot.astype(BF), (earlier < later).astype(BF))
    slot = jnp.sum(before * hot, axis=0, keepdims=True)
    target = chosen * capacity + slot.astype(jnp.int32)
    pack = (lax.broadcasted_iota(jnp.int32, (slots, rows), 0) == target).astype(F32)
    pack_ref[...] = pack.astype(BF)
    unpack_ref[...] = jnp.transpose(pack).astype(BF)
    hot_ref[...] = jnp.transpose(hot)
    packed_ref[...] = dot_nn(pack.astype(BF), cot_ref[...]).astype(BF)
    heads, buckets = bias_ref.shape
    length = table_ref.shape[1]
    for row, out in ((0, offset_ref), (1, back_ref)):
        table = lax.broadcasted_iota(jnp.int32, (buckets, length), 0) == table_ref[row : row + 1, :]
        out[0:heads, :] = dot_nn(bias_ref[...], table.astype(BF))
        out[heads:, :] = jnp.zeros((8 - heads, length), F32)
    router_ref[...] = jnp.zeros_like(router_ref)
    router_ref[0:experts, :] = router_in_ref[...]


def prepare(chosen, cot, tables, bias, router, capacity):
    experts, width = router.shape
    rows = chosen.shape[1]
    slots = experts * capacity
    return pl.pallas_call(
        functools.partial(prepare_kernel, experts, capacity),
        out_shape=[
            jax.ShapeDtypeStruct((slots, rows), BF),
            jax.ShapeDtypeStruct((rows, slots), BF),
            jax.ShapeDtypeStruct((slots, width), BF),
            jax.ShapeDtypeStruct((rows, LANES), F32),
            jax.ShapeDtypeStruct((8, tables.shape[1]), F32),
            jax.ShapeDtypeStruct((8, tables.shape[1]), F32),
            jax.ShapeDtypeStruct((LANES, width), BF),
        ],
        in_specs=[VMEM] * 5,
        out_specs=[VMEM] * 7,
        compiler_params=params(60),
        cost_estimate=cost(5e+10, 1e4),
    )(chosen, cot, tables, bias, router)


def mix_kernel(parts, experts, where_ref, *refs):
    hidden_ref, near_refs, far_ref, weight_ref = refs[0], refs[1:parts], refs[parts], refs[parts + 1]
    ctx_refs = refs[parts + 2 : 2 * parts + 2]
    gain_ref, router_ref, chosen_ref, pack_ref = refs[2 * parts + 2 : 2 * parts + 6]
    sum_ref, gate_ref, packed_ref, whole_ref, all_ref = refs[2 * parts + 6 :]
    core = where_ref[2]
    inner, width = weight_ref.shape
    side = width // 2
    whole_ref[0:inner, :] = weight_ref[...]
    near_at = pl.ds(pl.multiple_of(core * side, LANES), side)
    far_at = pl.ds(pl.multiple_of((1 - core) * side, LANES), side)
    for part in range(1, parts):
        rows = slice(part * inner, (part + 1) * inner)
        whole_ref[rows, near_at] = near_refs[part - 1][...]
        whole_ref[rows, far_at] = far_ref[part - 1]
    all_ref[...] = jnp.concatenate([ref[...] for ref in ctx_refs], axis=1)
    first_sum = hidden_ref[...].astype(F32) + dot_nn(all_ref[...], whole_ref[...])
    sum_ref[...] = first_sum
    normed = (first_sum * rms_scale(first_sum) * gain_ref[1:2, :]).astype(BF)
    packed_ref[...] = dot_nn(pack_ref[...], normed).astype(BF)
    lane = lax.broadcasted_iota(jnp.int32, gate_ref.shape, 1)
    logits = jnp.where(lane < experts, dot_nt(normed, router_ref[...]), F32(NEG))
    logits = jnp.exp(logits - jnp.max(logits, axis=1, keepdims=True))
    gate = jnp.sum(chosen_ref[...] * logits, axis=1, keepdims=True) / jnp.sum(
        logits, axis=1, keepdims=True
    )
    gate_ref[...] = jnp.broadcast_to(gate, gate_ref.shape)


def mix(where, hidden, near, far, weight, ctxs, gain, router, chosen, hot, experts):
    parts = len(ctxs)
    rows, width = hidden.shape
    inner = weight.shape[0]
    return pl.pallas_call(
        functools.partial(mix_kernel, parts, experts),
        out_shape=[
            jax.ShapeDtypeStruct((rows, width), F32),
            jax.ShapeDtypeStruct((rows, LANES), F32),
            jax.ShapeDtypeStruct((hot.shape[0], width), BF),
            jax.ShapeDtypeStruct((parts * inner, width), BF),
            jax.ShapeDtypeStruct((rows, parts * inner), BF),
        ],
        in_specs=[SMEM] + [VMEM] * (2 * parts + 6),
        out_specs=[VMEM] * 5,
        compiler_params=params(60),
        cost_estimate=cost(5e10, 1e4),
    )(where, hidden, *near, far, weight, *ctxs, gain, router, chosen, hot)


def expert_kernel(in_map, out_map, experts, where_ref, *refs):
    row_ref, cot_ref, router_ref = refs[:3]
    in_refs, out_refs = refs[3 : 3 + len(in_map)], refs[3 + len(in_map) : 3 + 2 * len(in_map)]
    back_ref, out_ref, gated_ref, logit_ref, near_hbm, far_hbm = refs[
        3 + 2 * len(in_map) : 9 + 2 * len(in_map)
    ]
    in_ref, outw_ref, near_ref, far_ref, total_ref, acc_ref, load_sems, store_sems = refs[
        9 + 2 * len(in_map) :
    ]
    units = len(in_map) // 2
    name = where_ref[3]
    slots, width = row_ref.shape
    span = in_refs[0].shape[1]
    hidden = units * span
    loads = []
    for unit in range(units):
        pieces = []
        for half in range(2):
            at = slice(half * span, (half + 1) * span)
            source = in_refs[in_map.index(unit + half * units)]
            pieces.append((source, in_ref.at[unit, :, at]))
            source = out_refs[out_map.index(unit + half * units)]
            pieces.append((source, outw_ref.at[unit, at, :]))
        copies = []
        for number, (source, target) in enumerate(pieces):
            copies.append(pltpu.make_async_copy(source, target, load_sems.at[unit, number]))
            copies[-1].start()
        loads.append(copies)
    rows_step = min(512, slots)
    tiles = [slice(at, at + rows_step) for at in range(0, slots, rows_step)]
    gates, routers = [], []
    lane = lax.broadcasted_iota(jnp.int32, (rows_step, LANES), 1)
    hot = (lane == name).astype(F32)
    for tile in tiles:
        logits = jnp.where(lane < experts, dot_nt(row_ref[tile, :], router_ref[...]), F32(NEG))
        logits = jnp.exp(logits - jnp.max(logits, axis=1, keepdims=True))
        router = logits / jnp.sum(logits, axis=1, keepdims=True)
        gate = jnp.sum(router * hot, axis=1, keepdims=True)
        gated = (cot_ref[tile, :].astype(F32) * gate).astype(BF)
        gated_ref[tile, :] = gated
        far_ref[tile, 2 * hidden :] = gated
        gates.append(gate)
        routers.append(router)
    stores = [
        pltpu.make_async_copy(
            far_ref.at[:, 2 * hidden :], far_hbm.at[:, 2 * hidden :], store_sems.at[units, 0]
        )
    ]
    stores[0].start()
    for unit in range(units):
        for copy in loads[unit]:
            copy.wait()
        for tile in tiles:
            pre_act = dot_nn(row_ref[tile, :], in_ref[unit])
            below = 0.5 + 0.5 * lax.erf(pre_act * F32(SQRT_HALF))
            active = (pre_act * below).astype(BF)
            slope = below + pre_act * jnp.exp(pre_act * pre_act * F32(-0.5)) * F32(INV_SQRT_TWO_PI)
            grad = (dot_nt(gated_ref[tile, :], outw_ref[unit]) * slope).astype(BF)
            for side_ref, half in ((near_ref, 0), (far_ref, 1)):
                at = slice(half * span, (half + 1) * span)
                side_ref[tile, unit * span : (unit + 1) * span] = active[:, at]
                side_ref[tile, hidden + unit * span : hidden + (unit + 1) * span] = grad[:, at]
            total = dot_nn(active, outw_ref[unit])
            back = dot_nt(grad, in_ref[unit])
            if unit:
                total_ref[tile, :] += total
                acc_ref[tile, :] += back
            else:
                total_ref[tile, :] = total
                acc_ref[tile, :] = back
        for number, (side_ref, side_hbm, first) in enumerate(
            (
                (near_ref, near_hbm, 0),
                (near_ref, near_hbm, hidden),
                (far_ref, far_hbm, 0),
                (far_ref, far_hbm, hidden),
            )
        ):
            at = slice(first + unit * span, first + (unit + 1) * span)
            copy = pltpu.make_async_copy(
                side_ref.at[:, at], side_hbm.at[:, at], store_sems.at[unit, number]
            )
            copy.start()
            stores.append(copy)
    for tile, gate, router in zip(tiles, gates, routers):
        total = total_ref[tile, :]
        gate_grad = jnp.sum(cot_ref[tile, :].astype(F32) * total, axis=1, keepdims=True)
        logit_grad = ((gate_grad * gate) * (hot - router)).astype(BF)
        logit_ref[tile, :] = logit_grad
        out_ref[tile, :] = total.astype(BF)
        back_ref[tile, :] = (acc_ref[tile, :] + dot_nn(logit_grad, router_ref[...])).astype(BF)
    for copy in stores:
        copy.wait()


def run_expert(where, rows, cots, in_parts, out_parts, in_map, out_map, router, experts):
    slots, width = rows.shape
    span = in_parts[0].shape[1]
    units = len(in_map) // 2
    hidden = 2 * units * span
    back, out, gated, logit, near, far = pl.pallas_call(
        functools.partial(expert_kernel, in_map, out_map, experts),
        out_shape=[
            jax.ShapeDtypeStruct((slots, width), BF),
            jax.ShapeDtypeStruct((slots, width), BF),
            jax.ShapeDtypeStruct((slots, width), BF),
            jax.ShapeDtypeStruct((slots, LANES), BF),
            jax.ShapeDtypeStruct((slots, hidden), BF),
            jax.ShapeDtypeStruct((slots, hidden + width), BF),
        ],
        in_specs=[SMEM] + [VMEM] * 3 + [ANY] * (len(in_parts) + len(out_parts)),
        out_specs=[VMEM] * 4 + [ANY] * 2,
        scratch_shapes=[
            pltpu.VMEM((units, width, 2 * span), BF),
            pltpu.VMEM((units, 2 * span, width), BF),
            pltpu.VMEM((slots, hidden), BF),
            pltpu.VMEM((slots, hidden + width), BF),
            pltpu.VMEM((slots, width), F32),
            pltpu.VMEM((slots, width), F32),
            pltpu.SemaphoreType.DMA((units, 4)),
            pltpu.SemaphoreType.DMA((units + 1, 4)),
        ],
        compiler_params=params(56),
        cost_estimate=cost(25e9, 20e6),
    )(where, rows, cots, router, *in_parts, *out_parts)
    return back, out, gated, near, far, logit


def weight_kernel(parts, row_ref, peer_ref, gated_ref, near_hbm, got_hbm, *refs):
    out_hbm = refs[: 2 * parts]
    both_ref, lhs_ref, tail_ref, done_ref, load_sems, store_sems = refs[2 * parts :]
    slots, width = row_ref.shape
    span = out_hbm[0].shape[1]
    hidden = parts * span
    chunk = 2 * span
    count = 2 * hidden // chunk
    tail = pltpu.make_async_copy(got_hbm.at[:, 2 * hidden :], tail_ref, load_sems.at[count, 0])
    loads = []
    order = list(range(count // 2, count)) + list(range(count // 2))
    for index in order:
        at = slice(index * chunk, (index + 1) * chunk)
        near = pltpu.make_async_copy(
            near_hbm.at[:, at], both_ref.at[0:slots, at], load_sems.at[index, 0]
        )
        got = pltpu.make_async_copy(
            got_hbm.at[:, at], both_ref.at[slots:, at], load_sems.at[index, 1]
        )
        near.start()
        got.start()
        loads.append((near, got))
        if index == count - 1:
            tail.start()
    lhs_ref[0, :, 0:slots] = jnp.transpose(row_ref[...])
    lhs_ref[0, :, slots:] = jnp.transpose(peer_ref[...])
    stores = []
    for number, index in enumerate(order):
        inward = index >= count // 2
        if number == count // 2:
            tail.wait()
            lhs_ref[1, :, 0:slots] = jnp.transpose(gated_ref[...])
            lhs_ref[1, :, slots:] = jnp.transpose(tail_ref[...])
        for copy in loads[number]:
            copy.wait()
        at = slice(index * chunk, (index + 1) * chunk)
        done_ref[number] = dot_nn(lhs_ref[0 if inward else 1], both_ref[:, at]).astype(BF)
        for half in range(2):
            part = 2 * (index % (count // 2)) + half
            copy = pltpu.make_async_copy(
                done_ref.at[number, :, half * span : (half + 1) * span],
                out_hbm[part if inward else parts + part],
                store_sems.at[number, half],
            )
            copy.start()
            stores.append(copy)
    for copy in stores:
        copy.wait()


def weight_grads(where, rows, rows_peer, gated, near, got, parts):
    slots, width = rows.shape
    span = near.shape[1] // (2 * parts)
    one = jax.ShapeDtypeStruct((width, span), BF)
    outs = pl.pallas_call(
        functools.partial(weight_kernel, parts),
        out_shape=[one] * (2 * parts),
        in_specs=[VMEM] * 3 + [ANY] * 2,
        out_specs=[ANY] * (2 * parts),
        scratch_shapes=[
            pltpu.VMEM((2 * slots, 2 * parts * span), BF),
            pltpu.VMEM((2, width, 2 * slots), BF),
            pltpu.VMEM((slots, width), BF),
            pltpu.VMEM((parts, width, 2 * span), BF),
            pltpu.SemaphoreType.DMA((parts + 1, 2)),
            pltpu.SemaphoreType.DMA((parts, 2)),
        ],
        compiler_params=params(60),
        cost_estimate=cost(1e10, 1e6),
    )(rows, rows_peer, gated, near, got)
    return outs[:parts], outs[parts:]


def finish_kernel(where_ref, *refs):
    core = where_ref[2]
    in_ref, out_ref = refs[4:]
    span = refs[0].shape[1]
    for half in range(2):
        own_in, own_out = refs[2 * half : 2 * half + 2]
        at = pl.ds(pl.multiple_of((core ^ half) * span, LANES), span)
        in_ref[:, at] = own_in[...].astype(F32)
        out_ref[at, :] = jnp.transpose(own_out[...].astype(F32))


def finish(where, mine, peer):
    width, span = mine[0].shape
    return pl.pallas_call(
        finish_kernel,
        out_shape=[
            jax.ShapeDtypeStruct((width, 2 * span), F32),
            jax.ShapeDtypeStruct((2 * span, width), F32),
        ],
        in_specs=[SMEM] + [VMEM] * 4,
        out_specs=[VMEM, VMEM],
        compiler_params=params(40),
        cost_estimate=cost(5e+10, 1e4),
    )(where, *mine, *peer)


def residual_kernel(parts, where_ref, *refs):
    home_ref, hot_ref, sum_ref, cot_ref, gain_ref = refs[:5]
    weight_ref, all_ref, grad_ref, gain_out_ref, give_ref = refs[5:10]
    ctx_refs, keep_refs = refs[10 : 10 + parts], refs[10 + parts :]
    core = where_ref[2]
    side = grad_ref.shape[1] // 2
    upstream = dot_nn(hot_ref[...], home_ref[...])
    first_sum = sum_ref[...]
    inverse = rms_scale(first_sum)
    gain_out_ref[...] = jnp.broadcast_to(
        jnp.sum(upstream * first_sum * inverse, axis=0, keepdims=True), gain_out_ref.shape
    )
    grad = cot_ref[...].astype(F32) + norm_back(first_sum, inverse, gain_ref[1:2, :], upstream)
    grad_ref[...] = grad
    low = grad.astype(BF)
    inner = weight_ref.shape[0] // parts
    across = dot_nt(low, weight_ref[...]).astype(BF)
    for part in range(parts):
        ctx_refs[part][...] = across[:, part * inner : (part + 1) * inner]
    product = dot_tn(all_ref[...], low)
    for part in range(parts):
        rows = slice(part * inner, (part + 1) * inner)

        @pl.when(core == 0)
        def _(part=part, rows=rows):
            keep_refs[part][...] = product[rows, :side]
            give_ref[part] = product[rows, side:].astype(BF)

        @pl.when(core != 0)
        def _(part=part, rows=rows):
            keep_refs[part][...] = product[rows, side:]
            give_ref[part] = product[rows, :side].astype(BF)


def residual(where, home, hot, first_sum, cot, gain, weight, every, parts):
    rows, width = first_sum.shape
    inner = weight.shape[0] // parts
    return pl.pallas_call(
        functools.partial(residual_kernel, parts),
        out_shape=[
            jax.ShapeDtypeStruct((rows, width), F32),
            jax.ShapeDtypeStruct((8, width), F32),
            jax.ShapeDtypeStruct((parts, inner, width // 2), BF),
        ]
        + [jax.ShapeDtypeStruct((rows, inner), BF)] * parts
        + [jax.ShapeDtypeStruct((inner, width // 2), F32)] * parts,
        in_specs=[SMEM] + [VMEM] * 7,
        out_specs=[VMEM] * (3 + 2 * parts),
        compiler_params=params(60),
        cost_estimate=cost(2e+11, 1e4),
    )(where, home, hot, first_sum, cot, gain, weight, every)


def attend_back_kernel(parts, heads, where_ref, *refs):
    cot_refs, refs = refs[:parts], refs[parts:]
    ctx_ref, proj_ref, normed_ref, lse_ref, weight_ref, offset_ref = refs[:6]
    scale_ref, small_ref, moe_ref, table_ref = refs[6:10]
    send_ref, bias_ref, keep_ref, give_ref = refs[10:14]
    skew_ref, fold_ref, cot_ref, dproj_ref, key_acc, value_acc = refs[14:]
    quarter = ctx_ref.shape[1]
    for part in range(parts):
        cot_ref[where_ref[0] ^ part] = cot_refs[part][...]
    length = quarter * parts
    inner = weight_ref.shape[0] // 3
    head_dim = inner // heads
    prefix, core = where_ref[1], where_ref[2]
    skew_into(skew_ref, offset_ref, heads, 2 * length)
    fold_ref[...] = jnp.zeros_like(fold_ref)
    key_acc[...] = jnp.zeros_like(key_acc)
    value_acc[...] = jnp.zeros_like(value_acc)
    keys_across = jnp.transpose(proj_ref[:, inner : 2 * inner])
    head_row = lax.broadcasted_iota(jnp.int32, (8, inner), 0)
    head_lane = lax.broadcasted_iota(jnp.int32, (8, inner), 1)
    picks = (head_lane // head_dim == head_row).astype(BF)
    for block in range(parts):
        first = block * quarter
        reach = max(length // 2, first + quarter)
        key_pos = first + lax.broadcasted_iota(jnp.int32, (reach - first, quarter), 0)
        query_pos = first + lax.broadcasted_iota(jnp.int32, (reach - first, quarter), 1)
        allowed = (key_pos <= query_pos) | (key_pos < prefix)
        product = cot_ref[block].astype(F32) * ctx_ref[block].astype(F32)
        high = product.astype(BF)
        rest = (product - high.astype(F32)).astype(BF)
        inner_sum = dot_nt(picks, high) + dot_nt(picks, rest)
        query_pieces = []
        for head in range(heads):
            low = head * head_dim
            query = proj_ref[first : first + quarter, low : low + head_dim]
            keys = proj_ref[0:reach, inner + low : inner + low + head_dim]
            values = proj_ref[0:reach, 2 * inner + low : 2 * inner + low + head_dim]
            grad = cot_ref[block, :, low : low + head_dim]
            bias = jnp.concatenate(
                [
                    skew_ref[
                        head,
                        :,
                        first - LANES * sub + length - LANES : first
                        - LANES * sub
                        + length
                        - LANES
                        + quarter,
                    ]
                    for sub in range(reach // LANES)
                ],
                axis=0,
            )
            scores = dot_nt(keys, query) + bias
            tail = jnp.where(allowed, scores[first:], F32(NEG))
            scores = jnp.concatenate([scores[:first], tail], axis=0) if first else tail
            probs = jnp.exp(scores - lse_ref[block, head : head + 1, :])
            prob_grad = dot_nt(values, grad)
            score_grad = (probs * (prob_grad - inner_sum[head : head + 1, :])).astype(BF)
            wide = score_grad.astype(F32)
            for sub in range(reach // LANES):
                column = first - LANES * sub + length - LANES
                fold_ref[head, :, column : column + quarter] += wide[
                    LANES * sub : LANES * (sub + 1)
                ]
            value_acc[head, 0:reach, :] += dot_nn(probs.astype(BF), grad)
            key_acc[head, 0:reach, :] += dot_nn(score_grad, query)
            query_pieces.append(dot_nn(keys_across[low : low + head_dim, 0:reach], score_grad))
        query_grad = jnp.transpose(jnp.concatenate(query_pieces, axis=0)) * F32(head_dim ** (-0.5))
        dproj_ref[first : first + quarter, 0:inner] = query_grad.astype(BF)
    dproj_ref[:, inner : 3 * inner] = jnp.concatenate(
        [key_acc[head] for head in range(heads)] + [value_acc[head] for head in range(heads)],
        axis=1,
    ).astype(BF)
    width = normed_ref.shape[1]
    side = width // 2
    split, piece, _ = keep_ref.shape
    layer = where_ref[3]
    grad_rows = dot_nn(jnp.transpose(dproj_ref[...]), normed_ref[...])
    for half in range(2):
        for part in range(split):
            chunk = grad_rows[part * piece : (part + 1) * piece, half * side : (half + 1) * side]
            slot = (layer ^ part) if split > 1 else part

            @pl.when(core == half)
            def _(chunk=chunk, slot=slot):
                keep_ref[slot] = chunk

            @pl.when(core != half)
            def _(chunk=chunk, slot=slot):
                give_ref[slot] = chunk.astype(BF)

    gain_sum = jnp.zeros((1, width), F32)
    for block in range(parts):
        rows = slice(block * quarter, (block + 1) * quarter)
        upstream = dot_nn(dproj_ref[rows, :], weight_ref[...])
        gain_sum = gain_sum + jnp.sum(
            upstream * normed_ref[rows, :].astype(F32), axis=0, keepdims=True
        )
        send_ref[block, 0:quarter, :] = upstream.astype(BF)
    extra = small_ref.shape[0]
    row = lax.broadcasted_iota(jnp.int32, small_ref.shape, 0)
    small = jnp.where(row == 1, moe_ref[0:1, :], small_ref[...])
    small = jnp.where(row == 0, gain_sum / scale_ref[0:1, :], small).astype(BF)
    share = width // parts
    for block in range(parts):
        send_ref[block, quarter:, 0:share] = small[:, block * share : (block + 1) * share]
        send_ref[block, quarter:, share:] = jnp.zeros((extra, width - share), BF)
    row_index = lax.broadcasted_iota(jnp.int32, (LANES, 2 * length), 0)
    buckets = (row_index == table_ref[1:2, :]).astype(BF)
    sums = []
    for head in range(heads):
        tile = fold_ref[head, 0:8, :]
        for group in range(8, LANES, 8):
            tile = tile + pltpu.roll(fold_ref[head, group : group + 8, :], 2 * length - group, 1)
        for bit in range(3):
            moved = pltpu.roll(tile, 2 * length - (1 << bit), 1)
            tile = jnp.where(((row_index[0:8] >> bit) & 1) == 1, moved, tile)
        tile = pltpu.roll(tile, LANES - 1, 1)
        sums.append(jnp.sum(tile, axis=0, keepdims=True))
    rest = jnp.concatenate(sums + [jnp.zeros((8 - heads, 2 * length), F32)], axis=0)
    levels = []
    for _ in range(3):
        high = rest.astype(BF).astype(F32)
        rest = rest - high
        levels.append(high)
    total = dot_nt(jnp.concatenate(levels, axis=0).astype(BF), buckets)
    total = total[0:8] + total[8:16] + total[16:24]
    bias_ref[0:8, :] = total
    bias_ref[8:, :] = jnp.zeros((bias_ref.shape[0] - 8, LANES), F32)


def attend_back(
    where, cots, ctxs, proj, normed, lse, weight, offsets, scale, small, moe, tables, heads, split
):
    parts, quarter, inner = ctxs.shape
    width = normed.shape[1]
    length = parts * quarter
    return pl.pallas_call(
        functools.partial(attend_back_kernel, parts, heads),
        out_shape=[
            jax.ShapeDtypeStruct((parts, quarter + small.shape[0], width), BF),
            jax.ShapeDtypeStruct((small.shape[0], LANES), F32),
            jax.ShapeDtypeStruct((split, 3 * inner // split, width // 2), F32),
            jax.ShapeDtypeStruct((split, 3 * inner // split, width // 2), BF),
        ],
        in_specs=[SMEM] + [VMEM] * (10 + parts),
        out_specs=[VMEM] * 4,
        scratch_shapes=[
            pltpu.VMEM((heads, LANES, 2 * length), F32),
            pltpu.VMEM((heads, LANES, 2 * length), F32),
            pltpu.VMEM((parts, quarter, inner), BF),
            pltpu.VMEM((length, 3 * inner), BF),
            pltpu.VMEM((heads, length, inner // heads), F32),
            pltpu.VMEM((heads, length, inner // heads), F32),
        ],
        compiler_params=params(60),
        cost_estimate=cost(5e+10, 1e4),
    )(where, *cots, ctxs, proj, normed, lse, weight, offsets, scale, small, moe, tables)


def merge_kernel(parts, where_ref, keep_ref, got_ref, *refs):
    wo_refs, (home_ref, hot_ref, sum_ref, gate_ref) = refs[:parts], refs[parts : parts + 4]
    layer_ref, send_refs, wo_ref = refs[parts + 4], refs[parts + 5 : -1], refs[-1]
    split, piece, side = keep_ref.shape
    share = wo_ref.shape[0] // split
    layer = where_ref[3]
    total = wo_refs[0][...] + wo_refs[1][0].astype(F32)
    for part in range(2, parts):
        total = total + wo_refs[part][...].astype(F32)
    wo_ref[...] = total
    expert_out = dot_nn(hot_ref[...], home_ref[...])
    layer_ref[...] = (sum_ref[...] + gate_ref[:, 0:1] * expert_out).astype(BF)
    for part in range(split):
        send_refs[part][0:piece, :] = (keep_ref[part] + got_ref[part].astype(F32)).astype(BF)
        row = (layer ^ part) * share if split > 1 else 0
        send_refs[part][piece:, :] = wo_ref[pl.ds(pl.multiple_of(row, 8), share), :].astype(BF)


def merge(where, keep, got, wos, home, hot, first_sum, gate):
    split, piece, side = keep.shape
    rows = wos[0].shape[0]
    shape = jax.ShapeDtypeStruct((piece + rows // split, side), BF)
    return pl.pallas_call(
        functools.partial(merge_kernel, len(wos)),
        out_shape=[jax.ShapeDtypeStruct(first_sum.shape, BF)] + [shape] * split,
        in_specs=[SMEM] + [VMEM] * (6 + len(wos)),
        out_specs=[VMEM] * (1 + split),
        scratch_shapes=[pltpu.VMEM((rows, side), F32)],
        compiler_params=params(60),
        cost_estimate=cost(1e+06, 1e4),
    )(where, keep, got, *wos, home, hot, first_sum, gate)


def assemble_kernel(where_ref, *refs):
    *piece_refs, qkv_ref, wo_ref, first_ref, second_ref, router_ref, bias_ref, parts_ref = refs
    split = len(piece_refs) // 2
    side = qkv_ref.shape[1] // 2
    piece, share = qkv_ref.shape[0] // split, wo_ref.shape[0] // split
    core, layer = where_ref[2], where_ref[3]
    for part in range(split):
        slot = (layer ^ part) if split > 1 else 0
        for half in range(2):
            ref = piece_refs[half * split + part]
            at = pl.ds(pl.multiple_of((core ^ half) * side, LANES), side)
            values = ref[...].astype(F32)
            qkv_ref[pl.ds(pl.multiple_of(slot * piece, 8), piece), at] = values[0:piece]
            wo_ref[pl.ds(pl.multiple_of(slot * share, 8), share), at] = values[
                piece : piece + share
            ]
            parts_ref[(core ^ half) * split + slot] = values[piece + share :]
    total = parts_ref[0]
    for part in range(1, 2 * split):
        total = total + parts_ref[part]
    share = first_ref.shape[1]
    first_ref[...] = total[0:1, 0:share]
    second_ref[...] = total[1:2, 0:share]
    router_ref[...] = total[2 : 2 + router_ref.shape[0], 0:share]
    bias_ref[...] = total[0 : bias_ref.shape[0], share : share + bias_ref.shape[1]]


def assemble(where, pieces, rows, extra, width, experts, heads, buckets):
    split = len(pieces) // 2
    both, side = pieces[0].shape
    return pl.pallas_call(
        assemble_kernel,
        out_shape=[
            jax.ShapeDtypeStruct((rows, 2 * side), F32),
            jax.ShapeDtypeStruct((split * (both - extra) - rows, 2 * side), F32),
            jax.ShapeDtypeStruct((1, width), F32),
            jax.ShapeDtypeStruct((1, width), F32),
            jax.ShapeDtypeStruct((experts, width), F32),
            jax.ShapeDtypeStruct((heads, buckets), F32),
        ],
        in_specs=[SMEM] + [VMEM] * (2 * split),
        out_specs=[VMEM] * 6,
        scratch_shapes=[pltpu.VMEM((2 * split, extra, side), F32)],
        compiler_params=params(16),
        cost_estimate=cost(1e+06, 1e4),
    )(where, *pieces)


def trade(values, axis):
    return lax.all_to_all(values, axis, split_axis=0, concat_axis=0, tiled=True)


def after(values, others):
    return lax.optimization_barrier((values, others))[0]


def body(
    hidden_in,
    cotangent,
    attn_gain,
    query_key_value_weight,
    attention_output_weight,
    rel_bias,
    bucket_table,
    prefix_len,
    moe_gain,
    w_router,
    routes,
    w_expert_in,
    w_expert_out,
):
    seq_count, quarter, model_width = hidden_in.shape
    parts = lax.axis_size("tensor")
    layers = lax.axis_size("expert")
    row_count = seq_count * quarter
    experts = w_router.shape[1]
    capacity = max(2, 2 * row_count // experts)
    slot_count = experts * capacity
    heads, buckets = rel_bias.shape
    inner = query_key_value_weight.shape[2]
    span = w_expert_in.shape[2] // 2
    place, layer, core = lax.axis_index("tensor"), lax.axis_index("expert"), lax.axis_index("dp")
    where = jnp.stack([place, prefix_len[0], core, layer]).astype(jnp.int32)
    low_core = core == 0

    own_hidden = hidden_in[0]
    own_cot = cotangent[0]

    chosen = routes.reshape(1, row_count)
    tables = jnp.stack([bucket_table, jnp.flip(bucket_table)])
    tables = jnp.pad(tables, ((0, 0), (0, 1)), constant_values=-1)
    gains = jnp.stack([attn_gain, moe_gain]).astype(F32)
    pack_hot, unpack_hot, cot_packed, chosen_hot, offset_bias, offset_back, router = prepare(
        chosen, own_cot, tables, rel_bias, w_router.T, capacity
    )

    def over_experts(packed):
        packed = packed.reshape(experts, capacity, model_width)
        return trade(packed, "expert").reshape(slot_count, model_width)

    cot_slots = over_experts(cot_packed)

    hidden_blocks = [own_hidden] + [swap(own_hidden, "tensor", k) for k in range(1, parts)]
    weight = query_key_value_weight.transpose(1, 2, 0).reshape(3 * inner, model_width)
    side = model_width // 2
    own_weight = lax.dynamic_slice(attention_output_weight, (0, core * side), (inner, side))
    late_weight = after(own_weight, hidden_blocks)
    out_weights = [
        swap(late_weight, "tensor", k) for k in range(1, parts)
    ]
    first_blocks, prepared = lax.optimization_barrier(
        (hidden_blocks, (own_weight, pack_hot, unpack_hot, chosen_hot, router, offset_bias,
                         offset_back, where, gains))
    )
    _, pack_hot, unpack_hot, chosen_hot, router, offset_bias, offset_back, where, gains = (
        prepared
    )
    normed_one, projected, lse, contexts, sends = attend(
        where, first_blocks, gains, weight, offset_bias, heads
    )

    in_own = lax.dynamic_slice(w_expert_in[0], (0, core * span), (model_width, span))
    out_own = lax.dynamic_slice(w_expert_out[0], (core * span, 0), (span, model_width))
    in_other = lax.dynamic_slice(w_expert_in[0], (0, (1 - core) * span), (model_width, span))
    out_other = lax.dynamic_slice(w_expert_out[0], ((1 - core) * span, 0), (span, model_width))
    in_own, out_own = after((in_own, out_own), hidden_blocks)
    in_step, out_step = swap(in_own, "tensor", 1), swap(out_own, "tensor", 2)
    far_weights = swap(jnp.stack(after(out_weights, sends)), "dp", 1)
    sends = after(sends, far_weights)
    own_contexts = [sends[0]] + [swap(sends[k], "tensor", k) for k in range(1, parts)]


    in_next, out_next = after((in_own, out_own), own_contexts[1])
    in_next, out_next = swap(in_next, "tensor", 2), swap(out_next, "tensor", 1)
    in_far, out_far = after((in_step, out_step), (own_contexts, in_next, out_next))
    in_far, out_far = swap(in_far, "tensor", 2), swap(out_far, "tensor", 1)
    in_near, in_order = [in_own, in_step, in_next, in_far], (0, 1, 2, 3)
    out_near, out_order = [out_own, out_step, out_next, out_far], (0, 2, 1, 3)
    in_map = in_order + tuple(parts + unit for unit in in_order)
    out_map = out_order + tuple(parts + unit for unit in out_order)

    first_sum, gate, packed, whole_weight, every_context = mix(
        where, own_hidden, out_weights, far_weights, attention_output_weight,
        after(own_contexts, (cot_slots, in_step, out_step)), gains, router, chosen_hot, pack_hot,
        experts,
    )
    row_slots = over_experts(packed)

    def cross(pieces):
        _, near, near_too, far = pieces
        far = after(far, row_slots)
        return [swap(near, "dp", 1), swap(near_too, "dp", 1), swap(far, "dp", 1)]

    in_parts = in_near + [in_other] + cross(in_near)
    out_parts = out_near + [out_other] + cross(out_near)
    rows_peer = swap(row_slots, "dp", 1)
    back_slots, out_slots, gated, near, far, logit_grad = run_expert(
        where, row_slots, cot_slots, in_parts, out_parts, in_map, out_map, router, experts
    )
    back_home = over_experts(back_slots)

    in_sums, out_sums = partial = weight_grads(
        where, row_slots, rows_peer, gated, near, swap(far, "dp", 1), parts
    )
    in_skip, out_skip = swap(in_sums[3], "tensor", 1), swap(out_sums[3], "tensor", 2)

    def plus(*terms):
        total = terms[0].astype(F32)
        for term in terms[1:]:
            total = total + term.astype(F32)
        return total.astype(BF)


    router_part = dot_tn(logit_grad, row_slots)[:experts]
    extra = -(-(experts + 2) // 16) * 16
    small = jnp.pad(router_part, ((2, extra - 2 - experts), (0, 0)))
    residual_grad, moe_gain_part, wo_give, *cots = residual(
        where, after(back_home, (partial, small)), unpack_hot, first_sum, own_cot, gains, whole_weight,
        every_context, parts,
    )
    cots, wo_keep = cots[:parts], cots[parts:]
    context_cots = [cots[0]] + [swap(cots[k], "tensor", k) for k in range(1, parts)]

    wo_got = swap(wo_give, "dp", 1)
    out_home = over_experts(after(out_slots, wo_got))
    wo_low = [(wo_keep[k] + wo_got[k].astype(F32)).astype(BF) for k in range(1, parts)]
    context_cots = after(context_cots, (wo_low, in_skip, out_skip))
    in_side, out_side = after((in_sums[1], out_sums[2]), (in_skip, out_skip))
    in_side, out_side = swap(in_side, "tensor", 1), swap(out_side, "tensor", 2)
    wo_parts = [wo_keep[0], wo_got] + [
        swap(wo_low[k - 1], "tensor", k) for k in range(1, parts)
    ]

    split = layers if layers == 4 else 1
    send_ups, bias_part, keep, give = attend_back(
        where, context_cots, contexts, projected, normed_one, lse, weight, offset_back,
        gains, small, moe_gain_part, tables, heads, split,
    )
    send_ups, give = after((send_ups, give), (wo_parts, out_home, in_side, out_side))
    ups = jnp.sum(trade(send_ups, "tensor").astype(F32), axis=0)
    own_float = own_hidden.astype(F32)
    inverse_own = rms_scale(own_float)
    input_grad = residual_grad + norm_back(own_float, inverse_own, gains[0:1], ups[:quarter])

    share = model_width // parts
    bias_part = jnp.pad(bias_part, ((0, 0), (0, side - share - LANES)))
    small = jnp.concatenate([ups[quarter:, :share], bias_part], axis=1)
    layer_out, *sends = merge(
        where, keep, swap(give, "dp", 1), wo_parts, out_home, unpack_hot, first_sum, gate
    )
    piece = sends[0].astype(F32)
    first = sends[-1]
    if split > 1:
        arrived = [swap(sends[k], "expert", k) for k in range(1, layers)]
        first = arrived[0]
        for value in arrived:
            piece = piece + value.astype(F32)
    in_skip, out_skip, in_side, out_side = after((in_skip, out_skip, in_side, out_side), first)
    in_pass, out_pass = plus(in_sums[2], in_skip), plus(out_sums[1], out_skip)
    in_last, out_last = swap(in_pass, "tensor", 2), swap(out_pass, "tensor", 1)
    if split > 1:
        piece = jnp.concatenate([piece, small], axis=0).astype(BF)
        pieces = [piece] + [swap(piece, "expert", k) for k in range(1, layers)]
    else:
        pieces = [lax.psum(jnp.concatenate([piece, small], axis=0), "expert")]
    in_last, out_last = after((in_last, out_last), pieces[:2])
    mine = (plus(in_sums[0], in_side, in_last), plus(out_sums[0], out_side, out_last))
    expert_in_grad, expert_out_grad = finish(where, mine, [swap(x, "dp", 1) for x in mine])
    pieces = pieces + [swap(x, "dp", 1) for x in pieces]
    done = (layer_out, expert_in_grad, expert_out_grad, input_grad)
    pieces, done = lax.optimization_barrier((pieces, done))
    layer_out, expert_in_grad, expert_out_grad, input_grad = done
    qkv_across, attn_out_grad, gain_one, gain_two, router_grad, bias_grad = assemble(
        where, pieces, 3 * inner, extra, share, experts, heads, buckets
    )
    qkv_grad = qkv_across.reshape(3, inner, model_width).transpose(2, 0, 1)
    return (
        layer_out.reshape(seq_count, quarter, model_width),
        input_grad.reshape(seq_count, quarter, model_width),
        gain_one[0],
        qkv_grad,
        attn_out_grad,
        bias_grad,
        gain_two[0],
        router_grad.T,
        expert_in_grad[None],
        expert_out_grad[None],
    )


def solution(mesh):
    placed = (
        P(("dp", "expert"), "tensor", None),
        P(("dp", "expert"), "tensor", None),
        P(),
        P(None, None, "tensor"),
        P("tensor", None),
        P("tensor", None),
        P(),
        P(("dp", "expert")),
        P(),
        P(),
        P(("dp", "expert"), "tensor", None, None, None),
        P("expert", None, "tensor"),
        P("expert", "tensor", None),
    )
    return jax.shard_map(
        body,
        mesh=mesh,
        in_specs=placed,
        out_specs=(
            P(("dp", "expert"), "tensor", None),
            P(("dp", "expert"), "tensor", None),
            P("tensor"),
            P(None, None, "tensor"),
            P("tensor", None),
            P("tensor", None),
            P("tensor"),
            P("tensor", None),
            P("expert", None, "tensor"),
            P("expert", "tensor", None),
        ),
        check_vma=False,
    )
```
